32 devices in a mesh: groups: 2 (over x), ctx: 16 (over z, y, core).
Axes of the slice: x: 2, y: 2, z: 4, core: 2. Of those that a mesh axis runs over, the one named last changes fastest.
Arguments:
- hidden_in: bfloat16 [4096, 2048], P(('groups', 'ctx')), parts along dimension 0, may hold values from -6 to 6
- queries: bfloat16 [4096, 1024], P(('groups', 'ctx')), parts along dimension 0, as said below
- keys: bfloat16 [4096, 128], P(('groups', 'ctx')), parts along dimension 0, as said below
- values: bfloat16 [4096, 128], P(('groups', 'ctx')), parts along dimension 0, may hold values from -6 to 6
- out_weight: bfloat16 [1024, 2048], replicated, may hold values from -0.5 to 0.5
- norm_gain: float32 [2048], replicated, may hold values from 0.1 to 1.9
- gate_weight: bfloat16 [2048, 11008], P(None, 'ctx'), may hold values from -0.125 to 0.125
- up_weight: bfloat16 [2048, 11008], P(None, 'ctx'), may hold values from -0.125 to 0.125
- down_weight: bfloat16 [11008, 2048], P('ctx'), may hold values from -0.0546875 to 0.0546875
- pair_ids: int32 [4096], P('groups'), parts along dimension 0, may hold values from 0 to 3, as said below
- roles: int32 [4096], P('groups'), parts along dimension 0, may hold values from 0 to 2, as said below
- send_rows: int32 [32, 128], P(('groups', 'ctx')), parts along dimension 0, may hold values from 0 to 127, as said below
- send_counts: int32 [32, 16], P('groups'), parts along dimension 0, may hold values from 0 to 8, as said below
Outputs:
- layer_out: bfloat16 [4096, 2048], P(('groups', 'ctx')), parts along dimension 0
The draws below stay inside these ranges and needn't reach their ends.
There are 2 independent parts, one for each index of `groups`. The reference program is written for one: setup_inputs(seed, part) draws one part's arguments, and reference() takes and returns one part's arrays. A program takes and returns all parts, laid end to end along the dimension named above; an argument that names none is the same for every part. Nothing has to cross between parts.
Inputs may be any that keep to these rules, and one draw needn't show every extreme that they name: `pair_ids`: never falls along the sequence; every pair is present, and one pair's chosen response spans 256 positions or more. `roles`: each pair is a prompt, then its chosen response, then its rejected response, each of one position or more; responses fill exactly 1536 positions. `send_rows`: slots j * 8 + k with k < send_counts[i, j] list distinct local rows of device i, together exactly its positions whose role is not 0; other slots hold 0. `send_counts`: replicated on every device; every column sums to 96; some entry equals 8. `queries`: values within -8 to 8. `keys`: values within -8 to 8.
All inputs are finite; a program needn't handle non-finite values.
Results may differ from the reference program's by a relative error of at most 0.015.
Values may be sent and summed in bfloat16 or wider, within the bound.
No kernel may reach another device: no remote copies, remote signals or barrier semaphores. Data moves between devices by JAX's collectives and lax.ppermute only.
A program may use at most 128 MiB of HBM per device.

```python
import math
import jax
import jax.numpy as jnp
from jax import lax

D = 2048
FF = 11008
QH = 8
HD = 128
TOK_DEV = 128
SEQ = 2048
LIVE_DEV = 96
CAP = 8
PAIRS = 4
N_CTX = 16


def structure(key):
    base_key = jax.random.fold_in(key, 31)
    key_a, key_b, key_c, key_d = jax.random.split(base_key, 4)
    live_total = LIVE_DEV * N_CTX
    prompt_total = SEQ - live_total
    zero_one = jnp.zeros((1,), jnp.int32)
    first_prompt = jax.random.randint(key_c, (), 1, TOK_DEV + 1, dtype=jnp.int32)
    extra_len = jax.random.randint(key_d, (), 0, TOK_DEV // 2, dtype=jnp.int32)
    first_chosen = N_CTX // 2 * TOK_DEV - first_prompt + extra_len
    prompt_static = prompt_total - TOK_DEV
    prompt_cuts = jnp.sort(jax.random.permutation(key_a, prompt_static - 1)[:PAIRS - 2].astype(jnp.int32) + 1)
    prompt_edges = jnp.concatenate([zero_one, prompt_cuts, jnp.full((1,), prompt_static, jnp.int32)])
    prompt_pieces = prompt_edges[1:] - prompt_edges[:-1]
    prompt_pieces = prompt_pieces.at[-1].add(TOK_DEV - first_prompt)
    answer_static = live_total - N_CTX // 2 * TOK_DEV - TOK_DEV // 2
    answer_cuts = jnp.sort(jax.random.permutation(key_b, answer_static - 1)[:2 * PAIRS - 2].astype(jnp.int32) + 1)
    answer_edges = jnp.concatenate([zero_one, answer_cuts, jnp.full((1,), answer_static, jnp.int32)])
    answers = answer_edges[1:] - answer_edges[:-1]
    prompts = jnp.concatenate([first_prompt[None], prompt_pieces])
    chosen = jnp.concatenate([first_chosen[None], answers[1::2]])
    rejected = jnp.concatenate([(answers[0] + first_prompt - extra_len + TOK_DEV // 2)[None], answers[2::2]])
    lengths = jnp.stack([prompts, chosen, rejected], axis=1).reshape(-1)
    piece_ends = jnp.cumsum(lengths).astype(jnp.int32)
    positions = jnp.arange(SEQ, dtype=jnp.int32)
    piece_of = jnp.sum((positions[:, None] >= piece_ends[None, :]).astype(jnp.int32), axis=1)
    pair_of = piece_of // 3
    role_of = piece_of % 3
    live_flag = (role_of != 0).astype(jnp.int32)
    live_rank = (jnp.cumsum(live_flag) - live_flag).astype(jnp.int32)
    device_of = positions // TOK_DEV
    first_rank = live_rank[device_of * TOK_DEV]
    target_dev = live_rank % N_CTX
    slot_index = (live_rank - first_rank) // N_CTX
    flat_slot = jnp.where(live_flag == 1, device_of * (N_CTX * CAP) + target_dev * CAP + slot_index, N_CTX * N_CTX * CAP)
    send_table = jnp.zeros((N_CTX * N_CTX * CAP,), jnp.int32).at[flat_slot].set(positions % TOK_DEV, mode='drop')
    count_slot = jnp.where(live_flag == 1, device_of * N_CTX + target_dev, N_CTX * N_CTX)
    count_table = jnp.zeros((N_CTX * N_CTX,), jnp.int32).at[count_slot].add(1, mode='drop')
    return (pair_of, role_of, send_table.reshape(N_CTX, N_CTX * CAP), count_table.reshape(N_CTX, N_CTX))


def draw_pair_ids(key, part):
    return structure(key)[0]


def draw_roles(key, part):
    return structure(key)[1]


def draw_send_rows(key, part):
    return structure(key)[2]


def draw_send_counts(key, part):
    return structure(key)[3]


def draw_queries(key, part):
    base_draw = jnp.clip(jax.random.normal(jax.random.fold_in(key, 5), (SEQ, QH * HD), jnp.float32), -4.0, 4.0)
    return base_draw.astype(jnp.bfloat16)


def draw_keys(key, part):
    base_draw = jnp.clip(jax.random.normal(jax.random.fold_in(key, 6), (SEQ, HD), jnp.float32), -4.0, 4.0)
    return base_draw.astype(jnp.bfloat16)


def levels(own_key, shape, shards, least, top_value):
    def one(position, parts):
        steps = jax.random.uniform(jax.random.fold_in(jax.random.fold_in(own_key, 6), position), (parts,), jnp.float32, least / len(shards), top_value / len(shards))
        return jnp.repeat(jnp.exp(steps), shape[position] // parts).reshape((-1,) + (1,) * (len(shape) - position - 1))

    gain = one(*shards[0])
    for cut in shards[1:]:
        gain = gain * one(*cut)
    return gain


def noise(own_key, shape, scale, most, pieces=(), kind=jnp.bfloat16):
    values = scale * jax.random.normal(own_key, shape, jnp.float32)
    if pieces:
        values = values * levels(own_key, shape, pieces, -0.22, 0.18)
    return jnp.clip(values, -most, most).astype(kind)


def setup_inputs(seed: int = 0, part: int = 0) -> dict:
    streams_of = jax.random.split(jax.random.key(seed), 14)
    part_splits = jax.random.split(jax.random.fold_in(streams_of[13], part), 14)
    return {
        "hidden_in": noise(part_splits[0], (SEQ, D), 1.0, 6.0, ((0, 16),)),
        "queries": draw_queries(jax.random.fold_in(jax.random.fold_in(streams_of[13], part), 71), part),
        "keys": draw_keys(jax.random.fold_in(jax.random.fold_in(streams_of[13], part), 71), part),
        "values": noise(part_splits[3], (SEQ, HD), 1.0, 6.0, ((0, 16),)),
        "out_weight": noise(streams_of[4], (QH * HD, D), HD ** -0.5, 0.5),
        "norm_gain": jnp.clip(1.0 + 0.18 * jax.random.normal(streams_of[5], (D,), jnp.float32), 0.1, 1.9),
        "gate_weight": noise(streams_of[6], (D, FF), D ** -0.5, 0.125, ((1, 16),)),
        "up_weight": noise(streams_of[7], (D, FF), D ** -0.5, 0.125, ((1, 16),)),
        "down_weight": noise(streams_of[8], (FF, D), FF ** -0.5, 0.0546875, ((0, 16),)),
        "pair_ids": draw_pair_ids(jax.random.fold_in(jax.random.fold_in(streams_of[13], part), 71), part),
        "roles": draw_roles(jax.random.fold_in(jax.random.fold_in(streams_of[13], part), 71), part),
        "send_rows": draw_send_rows(jax.random.fold_in(jax.random.fold_in(streams_of[13], part), 71), part),
        "send_counts": draw_send_counts(jax.random.fold_in(jax.random.fold_in(streams_of[13], part), 71), part),
    }


NEG_FILL = -1e+30

def reference(hidden_in, queries, keys, values, out_weight, norm_gain, gate_weight, up_weight, down_weight, pair_ids, roles, send_rows, send_counts):
    seq_len = hidden_in.shape[0]
    head_count = queries.shape[1] // HD
    block_rows = math.gcd(seq_len, 512)
    query_heads = queries.reshape(seq_len, head_count, HD).astype(jnp.float32)
    key_all = keys.astype(jnp.float32)
    value_all = values.astype(jnp.float32)
    key_pos = jnp.arange(seq_len, dtype=jnp.int32)
    score_scale = 1.0 / math.sqrt(HD)

    def attend(block_index):
        begin_row = (block_index * block_rows).astype(jnp.int32)
        query_block = lax.dynamic_slice_in_dim(query_heads, begin_row, block_rows)
        query_pos = begin_row + jnp.arange(block_rows, dtype=jnp.int32)
        query_pair = lax.dynamic_slice_in_dim(pair_ids, begin_row, block_rows)
        query_role = lax.dynamic_slice_in_dim(roles, begin_row, block_rows)
        seen_mask = (query_pair[:, None] == pair_ids[None, :]) & (key_pos[None, :] <= query_pos[:, None]) & ((roles[None, :] == 0) | (roles[None, :] == query_role[:, None]))
        scores = jnp.einsum('tqd,kd->qtk', query_block, key_all) * score_scale
        masked = jnp.where(seen_mask[None], scores, NEG_FILL)
        maximum = lax.optimization_barrier(jnp.max(masked, axis=-1, keepdims=True))
        weights = jnp.where(seen_mask[None], jnp.exp(masked - maximum), 0.0)
        denominator = lax.optimization_barrier(jnp.sum(weights, axis=-1))
        rounded = lax.optimization_barrier(weights.astype(jnp.bfloat16)).astype(jnp.float32)
        numerator = jnp.einsum('qtk,kd->qtd', rounded, value_all)
        mixed_sum = numerator / denominator[..., None]
        return mixed_sum.transpose(1, 0, 2).reshape(block_rows, head_count * HD)
    attention = lax.map(attend, jnp.arange(seq_len // block_rows, dtype=jnp.int32))
    attention = attention.reshape(seq_len, head_count * HD).astype(jnp.bfloat16)
    residual = (hidden_in.astype(jnp.float32) + jnp.dot(attention, out_weight, preferred_element_type=jnp.float32)).astype(jnp.bfloat16)
    wide = residual.astype(jnp.float32)
    mean_sq = lax.optimization_barrier(jnp.mean(wide * wide, axis=-1, keepdims=True))
    normed = (wide * lax.rsqrt(mean_sq + 1e-06) * norm_gain.astype(jnp.float32)[None, :]).astype(jnp.bfloat16)
    capacity = send_rows.shape[1] // N_CTX
    slot_index = jnp.arange(N_CTX * capacity, dtype=jnp.int32)
    valid = (slot_index % capacity)[None, :] < jnp.repeat(send_counts, capacity, axis=1)
    owner = jnp.arange(N_CTX, dtype=jnp.int32)[:, None] * TOK_DEV + send_rows
    target = jnp.where(valid, owner, seq_len).reshape(-1)
    live_mask = jnp.zeros((seq_len,), jnp.float32).at[target].set(1.0, mode='drop')
    ff_dev = FF // N_CTX

    def add_term(carry, shard_index):
        begin_col = (shard_index * ff_dev).astype(jnp.int32)
        gate_slice = lax.dynamic_slice_in_dim(gate_weight, begin_col, ff_dev, 1)
        up_slice = lax.dynamic_slice_in_dim(up_weight, begin_col, ff_dev, 1)
        down_slice = lax.dynamic_slice_in_dim(down_weight, begin_col, ff_dev, 0)
        gate_out = jnp.dot(normed, gate_slice, preferred_element_type=jnp.float32)
        up_out = jnp.dot(normed, up_slice, preferred_element_type=jnp.float32)
        inner_out = (jax.nn.silu(gate_out) * up_out).astype(jnp.bfloat16)
        term_out = jnp.dot(inner_out, down_slice, preferred_element_type=jnp.float32).astype(jnp.bfloat16)
        term_out = lax.optimization_barrier(term_out)
        return (carry + term_out.astype(jnp.float32), None)
    ffn_sum, _ = lax.scan(add_term, jnp.zeros((seq_len, hidden_in.shape[1]), jnp.float32), jnp.arange(N_CTX, dtype=jnp.int32))
    ffn_round = lax.optimization_barrier(ffn_sum.astype(jnp.bfloat16)).astype(jnp.float32)
    return (residual.astype(jnp.float32) + live_mask[:, None] * ffn_round).astype(jnp.bfloat16)
```

```python
import jax
import jax.numpy as jnp
from jax import lax
from jax.sharding import PartitionSpec as P

NEG_FILL = -1e30
CORES = 2


def attend(queries, keys, values, pair_ids, roles, my_index):
    tok_rows = queries.shape[0]
    head_dim = keys.shape[1]
    head_count = queries.shape[1] // head_dim
    own_begin = my_index * tok_rows
    query_pos = own_begin + jnp.arange(tok_rows, dtype=jnp.int32)
    query_pair = lax.dynamic_slice_in_dim(pair_ids, own_begin, tok_rows)
    query_role = lax.dynamic_slice_in_dim(roles, own_begin, tok_rows)
    query_heads = queries.reshape(tok_rows, head_count, head_dim)
    score_scale = 1.0 / head_dim**0.5
    both = lax.all_gather(jnp.concatenate([keys, values], axis=1), "ctx", axis=0, tiled=True)
    key_all = both[:, :head_dim]
    value_all = both[:, head_dim:]
    key_pos = jnp.arange(key_all.shape[0], dtype=jnp.int32)
    seen_mask = (
        (query_pair[:, None] == pair_ids[None, :])
        & (key_pos[None, :] <= query_pos[:, None])
        & ((roles[None, :] == 0) | (roles[None, :] == query_role[:, None]))
    )
    scores = (
        jnp.einsum("tqd,kd->qtk", query_heads, key_all, preferred_element_type=jnp.float32)
        * score_scale
    )
    masked = jnp.where(seen_mask[None], scores, NEG_FILL)
    top = jnp.max(masked, axis=-1)
    weights = jnp.where(seen_mask[None], jnp.exp(masked - top[..., None]), 0.0)
    denominator = jnp.sum(weights, axis=-1)
    numerator = jnp.einsum(
        "qtk,kd->qtd", weights.astype(jnp.bfloat16), value_all, preferred_element_type=jnp.float32
    )
    return (
        (numerator / denominator[..., None])
        .transpose(1, 0, 2)
        .reshape(tok_rows, head_count * head_dim)
        .astype(jnp.bfloat16)
    )


def on_device(
    hidden_in,
    queries,
    keys,
    values,
    out_weight,
    norm_gain,
    gate_weight,
    up_weight,
    down_weight,
    pair_ids,
    roles,
    send_rows,
    send_counts,
):
    devices = lax.axis_size("ctx")
    my_index = lax.axis_index("ctx")
    tok_rows = hidden_in.shape[0]
    swap = [(i, i ^ 1) for i in range(devices)]
    same_core = [list(range(core, devices, CORES)) for core in range(CORES)]
    gate_mate = lax.ppermute(gate_weight, "ctx", swap)
    up_mate = lax.ppermute(up_weight, "ctx", swap)
    down_mate = lax.ppermute(down_weight, "ctx", swap)

    attention = attend(queries, keys, values, pair_ids, roles, my_index)
    residual = (
        hidden_in.astype(jnp.float32)
        + jnp.dot(attention, out_weight, preferred_element_type=jnp.float32)
    ).astype(jnp.bfloat16)
    wide = residual.astype(jnp.float32)
    mean_sq = jnp.mean(wide * wide, axis=-1, keepdims=True)
    normed = (wide * lax.rsqrt(mean_sq + 1e-06) * norm_gain[None, :]).astype(jnp.bfloat16)

    gathered = lax.all_gather(normed, "ctx", axis=0, tiled=True, axis_index_groups=same_core)

    def half(gate, up, down):
        gate_out = jnp.dot(gathered, gate, preferred_element_type=jnp.float32)
        up_out = jnp.dot(gathered, up, preferred_element_type=jnp.float32)
        inner = (jax.nn.silu(gate_out) * up_out).astype(jnp.bfloat16)
        return jnp.dot(inner, down, preferred_element_type=jnp.float32)

    term = half(gate_weight, up_weight, down_weight) + half(gate_mate, up_mate, down_mate)
    summed = lax.psum_scatter(
        term.astype(jnp.bfloat16),
        "ctx",
        scatter_dimension=0,
        tiled=True,
        axis_index_groups=same_core,
    )

    slot_total = send_rows.shape[1]
    capacity = slot_total // devices
    my_counts = lax.dynamic_slice_in_dim(send_counts, my_index, 1, 0)[0]
    valid = jnp.tile(jnp.arange(capacity, dtype=jnp.int32), devices) < jnp.repeat(
        my_counts, capacity
    )
    target = jnp.where(valid, send_rows[0], tok_rows)
    live_mask = jnp.any(
        target[None, :] == jnp.arange(tok_rows, dtype=jnp.int32)[:, None], axis=1
    ).astype(jnp.float32)
    ffn_back = summed.astype(jnp.float32) * live_mask[:, None]
    return (residual.astype(jnp.float32) + ffn_back).astype(jnp.bfloat16)


def solution(mesh):
    return jax.shard_map(
        on_device,
        mesh=mesh,
        in_specs=(
            P(("groups", "ctx"), None),
            P(("groups", "ctx"), None),
            P(("groups", "ctx"), None),
            P(("groups", "ctx"), None),
            P(),
            P(),
            P(None, "ctx"),
            P(None, "ctx"),
            P("ctx", None),
            P("groups"),
            P("groups"),
            P(("groups", "ctx"), None),
            P("groups", None),
        ),
        out_specs=P(("groups", "ctx"), None),
        check_vma=False,
    )
```

```python
import jax
import jax.numpy as jnp
from jax import lax
from jax.sharding import PartitionSpec as P

NEG_FILL = -1e30
CORES = 2
PLANE = 4


class Ring:
    def __init__(self, groups, devices):
        chips = devices // CORES
        columns = max(1, PLANE // groups)
        if chips % columns:
            columns = 1
        depth = chips // columns
        order = []
        for column in range(columns):
            line = [level * columns + column for level in range(depth)]
            order += line if column % 2 == 0 else line[::-1]
        self.chips = chips
        self.half = chips // 2
        self.fwd = []
        self.bwd = []
        for place in range(chips):
            here, there = order[place], order[(place + 1) % chips]
            for core in range(CORES):
                self.fwd.append((here * CORES + core, there * CORES + core))
                self.bwd.append((there * CORES + core, here * CORES + core))
        self.swap = [(i, i ^ 1) for i in range(devices)]
        self.order = order

    def go_fwd(self, block):
        return lax.ppermute(block, "ctx", self.fwd)

    def go_bwd(self, block):
        return lax.ppermute(block, "ctx", self.bwd)

    def go_mate(self, block):
        return lax.ppermute(block, "ctx", self.swap)


def ring_gather(ring, block):
    mid = block.shape[0] // 2
    fwd, bwd = [block], [block]
    for _ in range(1, ring.half):
        fwd.append(ring.go_fwd(fwd[-1]))
        bwd.append(ring.go_bwd(bwd[-1]))
    across = jnp.concatenate([ring.go_fwd(fwd[-1][:mid]), ring.go_bwd(bwd[-1][mid:])], axis=0)
    return fwd, bwd, across


def attend(ring, queries, keys, values, pair_ids, roles, my_index):
    tok_rows = queries.shape[0]
    head_dim = keys.shape[1]
    head_count = queries.shape[1] // head_dim
    own_begin = my_index * tok_rows
    query_pos = own_begin + jnp.arange(tok_rows, dtype=jnp.int32)
    query_pair = lax.dynamic_slice_in_dim(pair_ids, own_begin, tok_rows)
    query_role = lax.dynamic_slice_in_dim(roles, own_begin, tok_rows)
    query_heads = queries.reshape(tok_rows, head_count, head_dim)
    score_scale = 1.0 / head_dim**0.5

    both = jnp.concatenate([keys, values], axis=1)
    fwd, bwd, across = ring_gather(ring, both)
    blocks = fwd + bwd[1:] + [across]
    spots = list(range(0, -ring.half, -1)) + list(range(1, ring.half)) + [ring.half]
    chip_order = jnp.asarray(ring.order, jnp.int32)
    place_of = [0] * ring.chips
    for place, chip in enumerate(ring.order):
        place_of[chip] = place
    place = jnp.asarray(place_of, jnp.int32)[my_index // CORES]
    core = my_index % CORES
    owners = []
    for spot in spots:
        chip = chip_order[(place + spot + ring.chips) % ring.chips]
        owners.append(chip * CORES + core)
    owners = jnp.stack(owners)
    owners = jnp.concatenate([owners, owners ^ 1])
    mates = [ring.go_mate(block) for block in blocks]
    gathered = jnp.concatenate(blocks + mates, axis=0)
    key_all = gathered[:, :head_dim]
    value_all = gathered[:, head_dim:]
    key_pos = (owners[:, None] * tok_rows + jnp.arange(tok_rows, dtype=jnp.int32)[None, :]).reshape(-1)
    key_pair = pair_ids.reshape(-1, tok_rows)[owners].reshape(-1)
    key_role = roles.reshape(-1, tok_rows)[owners].reshape(-1)
    seen_mask = (
        (query_pair[:, None] == key_pair[None, :])
        & (key_pos[None, :] <= query_pos[:, None])
        & ((key_role[None, :] == 0) | (key_role[None, :] == query_role[:, None]))
    )
    scores = (
        jnp.einsum("tqd,kd->qtk", query_heads, key_all, preferred_element_type=jnp.float32)
        * score_scale
    )
    masked = jnp.where(seen_mask[None], scores, NEG_FILL)
    top = jnp.max(masked, axis=-1)
    weights = jnp.where(seen_mask[None], jnp.exp(masked - top[..., None]), 0.0)
    denominator = jnp.sum(weights, axis=-1)
    numerator = jnp.einsum(
        "qtk,kd->qtd", weights.astype(jnp.bfloat16), value_all, preferred_element_type=jnp.float32
    )
    return (
        (numerator / denominator[..., None])
        .transpose(1, 0, 2)
        .reshape(tok_rows, head_count * head_dim)
        .astype(jnp.bfloat16)
    )


def feed_forward(ring, normed, own, mate):
    rows = normed.shape[0]
    mid = rows // 2

    def ffn(block):
        total = None
        for gate, up, down in (own, mate):
            gate_out = jnp.dot(block, gate, preferred_element_type=jnp.float32)
            up_out = jnp.dot(block, up, preferred_element_type=jnp.float32)
            inner = (jax.nn.silu(gate_out) * up_out).astype(jnp.bfloat16)
            part = jnp.dot(inner, down, preferred_element_type=jnp.float32)
            total = part if total is None else total + part
        return total

    fwd, bwd, across = ring_gather(ring, normed)
    own_term = ffn(normed)
    terms = [None]
    for step in range(1, ring.half):
        terms.append(ffn(jnp.concatenate([fwd[step], bwd[step]], axis=0)).astype(jnp.bfloat16))
    far = ffn(across).astype(jnp.bfloat16)

    home_bwd = ring.go_bwd(far[:mid])
    home_fwd = ring.go_fwd(far[mid:])
    for step in range(ring.half - 1, 0, -1):
        add_bwd = terms[step][:rows].astype(jnp.float32)
        add_fwd = terms[step][rows:].astype(jnp.float32)
        if step == ring.half - 1:
            pad = jnp.zeros_like(home_bwd)
            home_bwd = jnp.concatenate([home_bwd, pad], axis=0)
            home_fwd = jnp.concatenate([pad, home_fwd], axis=0)
        home_bwd = ring.go_bwd((home_bwd.astype(jnp.float32) + add_bwd).astype(jnp.bfloat16))
        home_fwd = ring.go_fwd((home_fwd.astype(jnp.float32) + add_fwd).astype(jnp.bfloat16))
    return own_term + home_bwd.astype(jnp.float32) + home_fwd.astype(jnp.float32)


def on_device(
    ring,
    hidden_in,
    queries,
    keys,
    values,
    out_weight,
    norm_gain,
    gate_weight,
    up_weight,
    down_weight,
    pair_ids,
    roles,
    send_rows,
    send_counts,
):
    devices = lax.axis_size("ctx")
    my_index = lax.axis_index("ctx")
    tok_rows = hidden_in.shape[0]
    gate_mate = ring.go_mate(gate_weight)
    up_mate = ring.go_mate(up_weight)
    down_mate = ring.go_mate(down_weight)

    attention = attend(ring, queries, keys, values, pair_ids, roles, my_index)
    residual = (
        hidden_in.astype(jnp.float32)
        + jnp.dot(attention, out_weight, preferred_element_type=jnp.float32)
    ).astype(jnp.bfloat16)
    wide = residual.astype(jnp.float32)
    mean_sq = jnp.mean(wide * wide, axis=-1, keepdims=True)
    normed = (wide * lax.rsqrt(mean_sq + 1e-06) * norm_gain[None, :]).astype(jnp.bfloat16)
    normed, gate_mate, up_mate, down_mate = lax.optimization_barrier(
        (normed, gate_mate, up_mate, down_mate)
    )
    summed = feed_forward(
        ring, normed, (gate_weight, up_weight, down_weight), (gate_mate, up_mate, down_mate)
    )

    slot_total = send_rows.shape[1]
    capacity = slot_total // devices
    my_counts = lax.dynamic_slice_in_dim(send_counts, my_index, 1, 0)[0]
    valid = jnp.tile(jnp.arange(capacity, dtype=jnp.int32), devices) < jnp.repeat(
        my_counts, capacity
    )
    target = jnp.where(valid, send_rows[0], tok_rows)
    live_mask = jnp.any(
        target[None, :] == jnp.arange(tok_rows, dtype=jnp.int32)[:, None], axis=1
    ).astype(jnp.float32)
    ffn_back = summed.astype(jnp.bfloat16).astype(jnp.float32) * live_mask[:, None]
    return (residual.astype(jnp.float32) + ffn_back).astype(jnp.bfloat16)


def solution(mesh):
    ring = Ring(mesh.shape["groups"], mesh.shape["ctx"])

    def run(*arrays):
        return on_device(ring, *arrays)

    return jax.shard_map(
        run,
        mesh=mesh,
        in_specs=(
            P(("groups", "ctx"), None),
            P(("groups", "ctx"), None),
            P(("groups", "ctx"), None),
            P(("groups", "ctx"), None),
            P(),
            P(),
            P(None, "ctx"),
            P(None, "ctx"),
            P("ctx", None),
            P("groups"),
            P("groups"),
            P(("groups", "ctx"), None),
            P("groups", None),
        ),
        out_specs=P(("groups", "ctx"), None),
        check_vma=False,
    )
```

```python
import functools
import math

import jax
import jax.numpy as jnp
import numpy as np
from jax import lax
from jax.experimental import pallas as pl
from jax.experimental.pallas import tpu as pltpu
from jax.sharding import PartitionSpec as P

NEG_FILL = -1e30
CORES = 2
PLANE = 4
MIB = 1 << 20


class Ring:
    def __init__(self, groups, devices):
        chips = devices // CORES
        columns = max(1, PLANE // groups)
        if chips % columns:
            columns = 1
        depth = chips // columns
        order = []
        for column in range(columns):
            line = [level * columns + column for level in range(depth)]
            order += line if column % 2 == 0 else line[::-1]
        self.chips = chips
        self.half = chips // 2
        self.order = order
        self.swap = [(i, i ^ 1) for i in range(devices)]

    def go(self, block, hops):
        pairs = []
        for place in range(self.chips):
            here, there = self.order[place], self.order[(place + hops) % self.chips]
            pairs += [(here * CORES + core, there * CORES + core) for core in range(CORES)]
        return lax.ppermute(block, "ctx", pairs)

    def go_mate(self, block):
        return lax.ppermute(block, "ctx", self.swap)

    def owners(self, spots):
        place_of = {chip: place for place, chip in enumerate(self.order)}
        table = []
        for device in range(self.chips * CORES):
            chip, core = divmod(device, CORES)
            own = [
                self.order[(place_of[chip] + spot) % self.chips] * CORES + core for spot in spots
            ]
            table.append(own + [d ^ 1 for d in own])
        return np.asarray(table, np.int32)


def attention_kernel(
    count,
    heads,
    head_dim,
    owner_ref,
    edge_ref,
    query_ref,
    hidden_ref,
    gain_ref,
    pair_ref,
    role_ref,
    out_weight_hbm,
    *refs,
):
    keys, values = refs[:count], refs[count : 2 * count]
    (residual_ref, normed_ref, weight_ref, stacked, scores, top, total, summed, sem) = refs[
        2 * count :
    ]
    rows = query_ref.shape[0]
    fetch = pltpu.make_async_copy(out_weight_hbm, weight_ref, sem)
    fetch.start()
    me = owner_ref[0]
    for head in range(heads):
        stacked[pl.ds(head * rows, rows), :] = query_ref[:, head * head_dim : (head + 1) * head_dim]

    def column(ref):
        return jnp.broadcast_to(ref[pl.ds(me, 1), :], (rows, rows)).T

    query_pair, query_role = column(pair_ref), column(role_ref)
    query_pos = me * rows + lax.broadcasted_iota(jnp.int32, (rows, rows), 0)
    key_off = lax.broadcasted_iota(jnp.int32, (rows, rows), 1)

    def needed(owner):
        first_pair, last_pair = edge_ref[owner, 0], edge_ref[owner, 1]
        first_role, last_role = edge_ref[owner, 2], edge_ref[owner, 3]
        my_first, my_last = edge_ref[me, 0], edge_ref[me, 1]
        apart = (
            (first_pair == last_pair)
            & (my_first == my_last)
            & (first_role == last_role)
            & (edge_ref[me, 2] == edge_ref[me, 3])
            & (first_role != 0)
            & (first_role != edge_ref[me, 2])
        )
        return (owner <= me) & (last_pair >= my_first) & jnp.logical_not(apart)

    top[...] = jnp.full_like(top, NEG_FILL)
    total[...] = jnp.zeros_like(total)
    summed[...] = jnp.zeros_like(summed)
    for j in range(count):
        owner = owner_ref[j]

        @pl.when(needed(owner))
        def _():
            seen = (
                (query_pair == pair_ref[pl.ds(owner, 1), :])
                & (owner * rows + key_off <= query_pos)
                & (
                    (role_ref[pl.ds(owner, 1), :] == 0)
                    | (role_ref[pl.ds(owner, 1), :] == query_role)
                )
            )
            bias = jnp.where(seen, 0.0, NEG_FILL)
            raw = lax.dot_general(
                stacked[...],
                keys[j][...],
                (((1,), (1,)), ((), ())),
                preferred_element_type=jnp.float32,
            )
            masked = raw.reshape(heads, rows, rows) + bias[None]
            scores[j] = masked
            top[...] = jnp.maximum(top[...], masked)

    top[...] = jnp.broadcast_to(jnp.max(top[...], axis=-1, keepdims=True), top.shape)
    factor = math.log2(math.e) / math.sqrt(head_dim)
    for j in range(count):
        owner = owner_ref[j]

        @pl.when(needed(owner))
        def _():
            weights = jnp.exp2((scores[j] - top[...]) * factor)
            total[...] += weights
            summed[...] += jnp.dot(
                weights.astype(jnp.bfloat16).reshape(heads * rows, rows),
                values[j][...],
                preferred_element_type=jnp.float32,
            ).reshape(heads, rows, head_dim)

    mixed = (summed[...] / jnp.sum(total[...], axis=-1, keepdims=True)).astype(jnp.bfloat16)
    mixed = jnp.concatenate([mixed[head] for head in range(heads)], axis=1)
    fetch.wait()
    projected = jnp.dot(mixed, weight_ref[...], preferred_element_type=jnp.float32)
    residual = (hidden_ref[...].astype(jnp.float32) + projected).astype(jnp.bfloat16)
    residual_ref[...] = residual
    wide = residual.astype(jnp.float32)
    mean_sq = jnp.mean(wide * wide, axis=-1, keepdims=True)
    normed_ref[...] = (wide * lax.rsqrt(mean_sq + 1e-06) * gain_ref[...]).astype(jnp.bfloat16)


def attend(owners, queries, hidden, gain, pair_ids, roles, out_weight, keys, values):
    rows, width = queries.shape
    head_dim = keys[0].shape[1]
    heads = width // head_dim
    count = len(keys)
    pairs = pair_ids.reshape(-1, rows)
    parts = roles.reshape(-1, rows)
    edges = jnp.stack([pairs[:, 0], pairs[:, -1], parts[:, 0], parts[:, -1]], axis=1)
    smem = pl.BlockSpec(memory_space=pltpu.SMEM)
    vmem = pl.BlockSpec(memory_space=pltpu.VMEM)
    square = pltpu.VMEM((heads, rows, rows), jnp.float32)
    return pl.pallas_call(
        functools.partial(attention_kernel, count, heads, head_dim),
        out_shape=(
            jax.ShapeDtypeStruct(hidden.shape, jnp.bfloat16),
            jax.ShapeDtypeStruct(hidden.shape, jnp.bfloat16),
        ),
        in_specs=[smem, smem]
        + [vmem] * 5
        + [pl.BlockSpec(memory_space=pl.ANY)]
        + [vmem] * (2 * count),
        out_specs=(vmem, vmem),
        scratch_shapes=[
            pltpu.VMEM(out_weight.shape, jnp.bfloat16),
            pltpu.VMEM((heads * rows, head_dim), jnp.bfloat16),
            pltpu.VMEM((count, heads, rows, rows), jnp.float32),
            square,
            square,
            pltpu.VMEM((heads, rows, head_dim), jnp.float32),
            pltpu.SemaphoreType.DMA,
        ],
        compiler_params=pltpu.CompilerParams(vmem_limit_bytes=48 * MIB),
        name="attention",
    )(
        owners,
        edges,
        queries,
        hidden,
        gain.reshape(1, -1),
        pairs,
        parts,
        out_weight,
        *keys,
        *values,
    )


def ffn_kernel(blocks, sizes, *refs):
    inputs, refs = refs[:blocks], refs[blocks:]
    weights_hbm, refs = refs[:6], refs[6:]
    outputs, refs = refs[:blocks], refs[blocks:]
    weights, (total, sems) = refs[:6], refs[6:]
    fetches = []
    for k in range(6):
        fetches.append(pltpu.make_async_copy(weights_hbm[k], weights[k], sems.at[k]))
        fetches[k].start()
    block = jnp.concatenate([ref[...] for ref in inputs], axis=0)
    for side in range(2):
        gate, up, down = weights[3 * side : 3 * side + 3]
        fetches[3 * side].wait()
        gate_out = jnp.dot(block, gate[...], preferred_element_type=jnp.float32)
        fetches[3 * side + 1].wait()
        up_out = jnp.dot(block, up[...], preferred_element_type=jnp.float32)
        inner = (gate_out / (1.0 + jnp.exp(-gate_out)) * up_out).astype(jnp.bfloat16)
        fetches[3 * side + 2].wait()
        part = jnp.dot(inner, down[...], preferred_element_type=jnp.float32)
        if side == 0:
            total[...] = part
        else:
            part = part + total[...]
            begin = 0
            for ref, size in zip(outputs, sizes):
                ref[...] = part[begin : begin + size].astype(jnp.bfloat16)
                begin += size


def ffn(blocks, weights):
    sizes = [b.shape[0] for b in blocks]
    width = blocks[0].shape[1]
    vmem = pl.BlockSpec(memory_space=pltpu.VMEM)
    flops = 2 * sum(sizes) * sum(w.size for w in weights)
    return pl.pallas_call(
        functools.partial(ffn_kernel, len(blocks), sizes),
        out_shape=tuple(jax.ShapeDtypeStruct(b.shape, jnp.bfloat16) for b in blocks),
        in_specs=[vmem] * len(blocks) + [pl.BlockSpec(memory_space=pl.ANY)] * 6,
        out_specs=(vmem,) * len(blocks),
        scratch_shapes=[pltpu.VMEM(w.shape, w.dtype) for w in weights]
        + [pltpu.VMEM((sum(sizes), width), jnp.float32), pltpu.SemaphoreType.DMA((6,))],
        compiler_params=pltpu.CompilerParams(vmem_limit_bytes=48 * MIB),
        cost_estimate=pl.CostEstimate(
            flops=flops,
            transcendentals=0,
            bytes_accessed=2 * sum(w.size for w in weights),
        ),
        name="feed_forward",
    )(*blocks, *weights)


def feed_forward(ring, normed, weights):
    mid = normed.shape[0] // 2
    fwd, bwd = [normed], [normed]
    for _ in range(1, ring.half):
        fwd.append(ring.go(fwd[-1], 1))
        bwd.append(ring.go(bwd[-1], -1))
    far_fwd = ring.go(fwd[-1][:mid], 1)
    far_bwd = ring.go(bwd[-1][mid:], -1)
    (own_term,) = ffn((normed,), weights)
    terms = [None]
    for step in range(1, ring.half):
        terms.append(ffn((fwd[step], bwd[step]), weights))
    far_terms = ffn((far_fwd, far_bwd), weights)

    def add(a, b):
        return (a.astype(jnp.float32) + b.astype(jnp.float32)).astype(jnp.bfloat16)

    home_bwd = ring.go(far_terms[0], -1)
    home_fwd = ring.go(far_terms[1], 1)
    for step in range(ring.half - 1, 0, -1):
        term_bwd, term_fwd = terms[step]
        if step == ring.half - 1:
            home_bwd = jnp.concatenate([add(home_bwd, term_bwd[:mid]), term_bwd[mid:]], axis=0)
            home_fwd = jnp.concatenate([term_fwd[:mid], add(home_fwd, term_fwd[mid:])], axis=0)
        else:
            home_bwd, home_fwd = add(home_bwd, term_bwd), add(home_fwd, term_fwd)
        home_bwd = ring.go(home_bwd, -1)
        home_fwd = ring.go(home_fwd, 1)
    return (
        own_term.astype(jnp.float32) + home_bwd.astype(jnp.float32) + home_fwd.astype(jnp.float32)
    )


def gather_kv(ring, keys, values):
    spots = [0]
    all_keys, all_values = [keys], [values]
    for hops in range(1, ring.half):
        for way in (1, -1):
            spots.append(-way * hops)
            all_keys.append(ring.go(keys, way * hops))
            all_values.append(ring.go(values, way * hops))
    spots.append(ring.half)
    all_keys.append(ring.go(keys, ring.half))
    all_values.append(ring.go(values, -ring.half))
    all_keys += [ring.go_mate(block) for block in all_keys]
    all_values += [ring.go_mate(block) for block in all_values]
    return spots, all_keys, all_values


def on_device(
    ring,
    hidden_in,
    queries,
    keys,
    values,
    out_weight,
    norm_gain,
    gate_weight,
    up_weight,
    down_weight,
    pair_ids,
    roles,
    send_rows,
    send_counts,
):
    my_index = lax.axis_index("ctx")
    tok_rows = hidden_in.shape[0]
    own = (gate_weight, up_weight, down_weight)
    weights = own + tuple(ring.go_mate(w) for w in own)

    spots, all_keys, all_values = gather_kv(ring, keys, values)
    owners = jnp.asarray(ring.owners(spots))[my_index]
    residual, normed = attend(
        owners, queries, hidden_in, norm_gain, pair_ids, roles, out_weight, all_keys, all_values
    )
    summed = feed_forward(ring, normed, weights)
    my_roles = lax.dynamic_slice_in_dim(roles, my_index * tok_rows, tok_rows)
    live = (my_roles != 0).astype(jnp.float32)
    ffn_back = summed.astype(jnp.bfloat16).astype(jnp.float32) * live[:, None]
    return (residual.astype(jnp.float32) + ffn_back).astype(jnp.bfloat16)


def solution(mesh):
    ring = Ring(mesh.shape["groups"], mesh.shape["ctx"])

    def run(*arrays):
        return on_device(ring, *arrays)

    return jax.shard_map(
        run,
        mesh=mesh,
        in_specs=(
            P(("groups", "ctx"), None),
            P(("groups", "ctx"), None),
            P(("groups", "ctx"), None),
            P(("groups", "ctx"), None),
            P(),
            P(),
            P(None, "ctx"),
            P(None, "ctx"),
            P("ctx", None),
            P("groups"),
            P("groups"),
            P(("groups", "ctx"), None),
            P("groups", None),
        ),
        out_specs=P(("groups", "ctx"), None),
        check_vma=False,
    )
```

```python
import functools
import math

import jax
import jax.numpy as jnp
import numpy as np
from jax import lax
from jax.experimental import pallas as pl
from jax.experimental.pallas import tpu as pltpu
from jax.sharding import PartitionSpec as P

NEG_FILL = -1e30
CORES = 2
PLANE = 4
CHUNKS = 2
MIB = 1 << 20


def in_hbm(x):
    return pltpu.with_memory_space_constraint(x, pltpu.HBM)


def hold(first, then):
    return lax.optimization_barrier((first, then))


class Ring:
    def __init__(self, groups, devices):
        chips = devices // CORES
        columns = max(1, PLANE // groups)
        if chips % columns:
            columns = 1
        depth = chips // columns
        order = []
        for column in range(columns):
            line = [level * columns + column for level in range(depth)]
            order += line if column % 2 == 0 else line[::-1]
        self.chips = chips
        self.half = chips // 2
        self.order = order
        self.swap = [(i, i ^ 1) for i in range(devices)]

    def go(self, block, hops):
        pairs = []
        for place in range(self.chips):
            here, there = self.order[place], self.order[(place + hops) % self.chips]
            pairs += [(here * CORES + core, there * CORES + core) for core in range(CORES)]
        return lax.ppermute(block, "ctx", pairs)

    def go_mate(self, block):
        return lax.ppermute(block, "ctx", self.swap)

    def owners(self, spots):
        place_of = {chip: place for place, chip in enumerate(self.order)}
        table = []
        for device in range(self.chips * CORES):
            chip, core = divmod(device, CORES)
            own = [
                self.order[(place_of[chip] + spot) % self.chips] * CORES + core for spot in spots
            ]
            table.append(own + [d ^ 1 for d in own])
        return np.asarray(table, np.int32)


def attention_kernel(
    count,
    heads,
    head_dim,
    owner_ref,
    edge_ref,
    *refs,
):
    inputs, blocks_hbm, refs = refs[:6], refs[6 : 6 + count], refs[6 + count :]
    outputs, refs = refs[: CHUNKS + 1], refs[CHUNKS + 1 :]
    locals_, refs = refs[:6], refs[6:]
    (given, kept, blocks, stacked, scores, top, total, summed, sems) = refs
    fetches = [
        pltpu.make_async_copy(inputs[k], locals_[k], sems.at[count + k]) for k in range(6)
    ]
    arrivals = [
        pltpu.make_async_copy(blocks_hbm[j], blocks.at[j], sems.at[j]) for j in range(count)
    ]
    for k in range(3):
        fetches[k].start()
    for arrival in arrivals:
        arrival.start()
    for k in range(3, 6):
        fetches[k].start()
    query_ref, pair_ref, role_ref, hidden_ref, gain_ref, weight_ref = locals_
    rows = query_ref.shape[0]
    for k in range(3):
        fetches[k].wait()
    me = owner_ref[0]
    for head in range(heads):
        stacked[pl.ds(head * rows, rows), :] = query_ref[:, head * head_dim : (head + 1) * head_dim]

    def column(ref):
        return jnp.broadcast_to(ref[pl.ds(me, 1), :], (rows, rows)).T

    query_pair, query_role = column(pair_ref), column(role_ref)
    query_pos = me * rows + lax.broadcasted_iota(jnp.int32, (rows, rows), 0)
    key_off = lax.broadcasted_iota(jnp.int32, (rows, rows), 1)

    def needed(owner):
        first_pair, last_pair = edge_ref[owner, 0], edge_ref[owner, 1]
        first_role, last_role = edge_ref[owner, 2], edge_ref[owner, 3]
        my_first, my_last = edge_ref[me, 0], edge_ref[me, 1]
        apart = (
            (first_pair == last_pair)
            & (my_first == my_last)
            & (first_role == last_role)
            & (edge_ref[me, 2] == edge_ref[me, 3])
            & (first_role != 0)
            & (first_role != edge_ref[me, 2])
        )
        return (owner <= me) & (last_pair >= my_first) & jnp.logical_not(apart)

    top[...] = jnp.full_like(top, NEG_FILL)
    total[...] = jnp.zeros_like(total)
    summed[...] = jnp.zeros_like(summed)
    for j in range(count):
        owner = owner_ref[j]
        arrivals[j].wait()

        @pl.when(needed(owner))
        def _():
            seen = (
                (query_pair == pair_ref[pl.ds(owner, 1), :])
                & (owner * rows + key_off <= query_pos)
                & (
                    (role_ref[pl.ds(owner, 1), :] == 0)
                    | (role_ref[pl.ds(owner, 1), :] == query_role)
                )
            )
            bias = jnp.where(seen, 0.0, NEG_FILL)
            raw = lax.dot_general(
                stacked[...],
                blocks[j, :rows, :],
                (((1,), (1,)), ((), ())),
                preferred_element_type=jnp.float32,
            )
            masked = raw.reshape(heads, rows, rows) + bias[None]
            scores[j] = masked
            top[...] = jnp.maximum(top[...], masked)

    top[...] = jnp.broadcast_to(jnp.max(top[...], axis=-1, keepdims=True), top.shape)
    factor = math.log2(math.e) / math.sqrt(head_dim)
    for j in range(count):
        owner = owner_ref[j]

        @pl.when(needed(owner))
        def _():
            weights = jnp.exp2((scores[j] - top[...]) * factor)
            total[...] += weights
            summed[...] += jnp.dot(
                weights.astype(jnp.bfloat16).reshape(heads * rows, rows),
                blocks[j, rows:, :],
                preferred_element_type=jnp.float32,
            ).reshape(heads, rows, head_dim)

    mixed = (summed[...] / jnp.sum(total[...], axis=-1, keepdims=True)).astype(jnp.bfloat16)
    mixed = jnp.concatenate([mixed[head] for head in range(heads)], axis=1)
    for k in range(3, 6):
        fetches[k].wait()
    projected = jnp.dot(mixed, weight_ref[...], preferred_element_type=jnp.float32)
    residual = (hidden_ref[...].astype(jnp.float32) + projected).astype(jnp.bfloat16)
    wide = residual.astype(jnp.float32)
    mean_sq = jnp.mean(wide * wide, axis=-1, keepdims=True)
    given[...] = (wide * lax.rsqrt(mean_sq + 1e-06) * gain_ref[...]).astype(jnp.bfloat16)
    kept[...] = residual
    part = rows // CHUNKS
    moves = [
        pltpu.make_async_copy(given.at[pl.ds(k * part, part), :], outputs[k], sems.at[k])
        for k in range(CHUNKS)
    ]
    moves.append(pltpu.make_async_copy(kept, outputs[CHUNKS], sems.at[CHUNKS]))
    for move in moves:
        move.start()
    for move in moves:
        move.wait()


def attend(owners, queries, hidden, gain, pair_ids, roles, out_weight, blocks):
    rows, width = queries.shape
    head_dim = blocks[0].shape[1]
    heads = width // head_dim
    count = len(blocks)
    pairs = pair_ids.reshape(-1, rows)
    parts = roles.reshape(-1, rows)
    edges = jnp.stack([pairs[:, 0], pairs[:, -1], parts[:, 0], parts[:, -1]], axis=1)
    smem = pl.BlockSpec(memory_space=pltpu.SMEM)
    hbm = pl.BlockSpec(memory_space=pltpu.HBM)
    square = pltpu.VMEM((heads, rows, rows), jnp.float32)
    chunk = jax.ShapeDtypeStruct((rows // CHUNKS, hidden.shape[1]), jnp.bfloat16)
    inputs = (queries, pairs, parts, hidden, gain.reshape(1, -1), out_weight)
    *chunks, residual = pl.pallas_call(
        functools.partial(attention_kernel, count, heads, head_dim),
        out_shape=(chunk,) * CHUNKS + (jax.ShapeDtypeStruct(hidden.shape, jnp.bfloat16),),
        in_specs=[smem, smem] + [hbm] * (len(inputs) + count),
        out_specs=(hbm,) * (CHUNKS + 1),
        scratch_shapes=[pltpu.VMEM(x.shape, x.dtype) for x in inputs]
        + [
            pltpu.VMEM(hidden.shape, jnp.bfloat16),
            pltpu.VMEM(hidden.shape, jnp.bfloat16),
            pltpu.VMEM((count,) + blocks[0].shape, jnp.bfloat16),
            pltpu.VMEM((heads * rows, head_dim), jnp.bfloat16),
            pltpu.VMEM((count, heads, rows, rows), jnp.float32),
            square,
            square,
            pltpu.VMEM((heads, rows, head_dim), jnp.float32),
            pltpu.SemaphoreType.DMA((count + len(inputs),)),
        ],
        compiler_params=pltpu.CompilerParams(vmem_limit_bytes=32 * MIB),
        name="attention",
    )(owners, edges, *(in_hbm(x) for x in inputs), *blocks)
    return residual, chunks


def join_kernel(keys_ref, values_ref, both_ref, sems):
    rows = keys_ref.shape[0]
    moves = [
        pltpu.make_async_copy(keys_ref, both_ref.at[pl.ds(0, rows), :], sems.at[0]),
        pltpu.make_async_copy(values_ref, both_ref.at[pl.ds(rows, rows), :], sems.at[1]),
    ]
    for move in moves:
        move.start()
    for move in moves:
        move.wait()


def join(keys, values):
    hbm = pl.BlockSpec(memory_space=pltpu.HBM)
    return pl.pallas_call(
        join_kernel,
        out_shape=jax.ShapeDtypeStruct((2 * keys.shape[0], keys.shape[1]), keys.dtype),
        in_specs=[hbm, hbm],
        out_specs=hbm,
        scratch_shapes=[pltpu.SemaphoreType.DMA((2,))],
        name="join",
    )(in_hbm(keys), in_hbm(values))


def ffn_kernel(blocks, *refs):
    inputs, refs = refs[:blocks], refs[blocks:]
    weights, refs = refs[:6], refs[6:]
    outputs, refs = refs[:blocks], refs[blocks:]
    held, given, sems = refs
    part = held.shape[0] // blocks
    moves = [
        pltpu.make_async_copy(inputs[k], held.at[pl.ds(k * part, part), :], sems.at[k])
        for k in range(blocks)
    ]
    for move in moves:
        move.start()
    for move in moves:
        move.wait()
    block = held[...]
    across = (((1,), (1,)), ((), ()))
    term = None
    for side in range(2):
        gate, up, down = weights[3 * side : 3 * side + 3]
        gate_out = lax.dot_general(block, gate[...], across, preferred_element_type=jnp.float32)
        up_out = lax.dot_general(block, up[...], across, preferred_element_type=jnp.float32)
        inner = (gate_out / (1.0 + jnp.exp(-gate_out)) * up_out).astype(jnp.bfloat16)
        one = jnp.dot(inner, down[...], preferred_element_type=jnp.float32)
        term = one if term is None else term + one
    given[...] = term.astype(jnp.bfloat16)
    moves = [
        pltpu.make_async_copy(given.at[pl.ds(k * part, part), :], outputs[k], sems.at[k])
        for k in range(blocks)
    ]
    for move in moves:
        move.start()
    for move in moves:
        move.wait()


def ffn(blocks, weights):
    count = len(blocks)
    rows, width = blocks[0].shape
    vmem = pl.BlockSpec(memory_space=pltpu.VMEM)
    hbm = pl.BlockSpec(memory_space=pltpu.HBM)
    flops = 2 * count * rows * sum(w.size for w in weights)
    return pl.pallas_call(
        functools.partial(ffn_kernel, count),
        out_shape=tuple(jax.ShapeDtypeStruct(b.shape, jnp.bfloat16) for b in blocks),
        in_specs=[hbm] * count + [vmem] * 6,
        out_specs=(hbm,) * count,
        scratch_shapes=[
            pltpu.VMEM((count * rows, width), jnp.bfloat16),
            pltpu.VMEM((count * rows, width), jnp.bfloat16),
            pltpu.SemaphoreType.DMA((count,)),
        ],
        compiler_params=pltpu.CompilerParams(vmem_limit_bytes=16 * MIB),
        cost_estimate=pl.CostEstimate(
            flops=flops,
            transcendentals=0,
            bytes_accessed=2 * sum(w.size for w in weights),
        ),
        name="feed_forward",
    )(*blocks, *weights)


def feed_forward(ring, chunks, weights):
    half = ring.half
    held = [[(chunks[0], chunks[1])], [(chunks[1], chunks[0])]]
    terms = [[None], [None]]

    def send(pair, way):
        return ring.go(pair[0], way), ring.go(pair[1], -way)

    sends = [(group, step) for step in range(1, half) for group in range(2)] + [(0, half)]
    ready = None
    for group, step in sends:
        pair = held[group][step - 1]
        if ready is not None:
            done, pair = hold(ffn(held[ready][-2], weights), pair)
            terms[ready].append(done)
        held[group].append(send(pair, 1))
        ready = group if step > 1 else None
    done, pair = hold(ffn(held[0][half - 1], weights), held[1][half - 1])
    terms[0].append(done)
    terms[1].append(ffn(pair, weights))
    terms[0].append(ffn(held[0][half], weights))

    def add(a, b):
        return (a.astype(jnp.float32) + b.astype(jnp.float32)).astype(jnp.bfloat16)

    home = [None, None]
    order = []
    for step in range(half - 1, 0, -1):
        order += [(1, step), (0, step + 1)]
    order.append((0, 1))
    own = None
    for group, step in order:
        pair = terms[group][step]
        if home[group] is not None:
            pair = (add(home[group][0], pair[0]), add(home[group][1], pair[1]))
            if own is None:
                _, first = hold(home[group], held[0][0])
                own = ffn(first, weights)
        home[group] = send(hold(*pair), -1)
    wide = [[x.astype(jnp.float32) for x in pair] for pair in (own, home[0], home[1])]
    return [wide[0][0] + wide[1][0] + wide[2][1], wide[0][1] + wide[1][1] + wide[2][0]]


def gather_kv(ring, block, weights):
    half = ring.half
    gate, up, down = weights
    gate_mate = ring.go_mate(gate)
    fwd, bwd, far = {0: block}, {0: block}, None
    mates, waiting = {}, [("fwd", 0)]
    reach = 0
    up_mate = None
    while far is None:
        fresh = []
        base = max(0, reach - 1)
        for hops in (reach + 1, reach + 2):
            jump = hops - (reach if hops == reach + 2 else base) if reach else hops
            start = hops - jump
            if hops < half:
                fwd[hops] = ring.go(fwd[start], jump)
                bwd[hops] = ring.go(bwd[start], -jump)
                fresh += [("fwd", hops), ("bwd", hops)]
            elif hops == half:
                far = ring.go(fwd[start], jump)
                fresh.append(("far", hops))
        if reach:
            for side, hops in waiting:
                mates[side, hops] = ring.go_mate({"fwd": fwd, "bwd": bwd}[side][hops])
            waiting = []
        reach += 2
        fwd, bwd, far, mates, again = lax.optimization_barrier((fwd, bwd, far, mates, gate_mate))
        if up_mate is None:
            gate_mate, up_mate = again, ring.go_mate(hold((again, fwd[1]), up)[1])
        waiting += fresh
    down_mate = ring.go_mate(hold((up_mate, fwd[half - 1]), down)[1])
    for side, hops in waiting:
        mates[side, hops] = ring.go_mate(far if side == "far" else {"fwd": fwd, "bwd": bwd}[side][hops])
    spots, blocks, swapped = [0], [fwd[0]], [mates["fwd", 0]]
    for hops in range(1, half):
        spots += [-hops, hops]
        blocks += [fwd[hops], bwd[hops]]
        swapped += [mates["fwd", hops], mates["bwd", hops]]
    return spots + [half], blocks + [far] + swapped + [mates["far", half]], (gate_mate, up_mate, down_mate)


def on_device(
    ring,
    hidden_in,
    queries,
    keys,
    values,
    out_weight,
    norm_gain,
    gate_weight,
    up_weight,
    down_weight,
    pair_ids,
    roles,
    send_rows,
    send_counts,
):
    my_index = lax.axis_index("ctx")
    tok_rows = hidden_in.shape[0]
    own = (gate_weight.T, up_weight.T, down_weight)
    spots, blocks, mates = gather_kv(ring, join(keys, values), own)
    owners = jnp.asarray(ring.owners(spots))[my_index]
    residual, chunks = attend(
        owners, queries, hidden_in, norm_gain, pair_ids, roles, out_weight, blocks
    )
    summed = feed_forward(ring, chunks, own + mates)
    my_roles = lax.dynamic_slice_in_dim(roles, my_index * tok_rows, tok_rows)
    live = (my_roles != 0).astype(jnp.float32)
    ffn_back = jnp.concatenate(summed, axis=0).astype(jnp.bfloat16).astype(jnp.float32)
    return (residual.astype(jnp.float32) + ffn_back * live[:, None]).astype(jnp.bfloat16)


def solution(mesh):
    ring = Ring(mesh.shape["groups"], mesh.shape["ctx"])

    def run(*arrays):
        return on_device(ring, *arrays)

    return jax.shard_map(
        run,
        mesh=mesh,
        in_specs=(
            P(("groups", "ctx"), None),
            P(("groups", "ctx"), None),
            P(("groups", "ctx"), None),
            P(("groups", "ctx"), None),
            P(),
            P(),
            P(None, "ctx"),
            P(None, "ctx"),
            P("ctx", None),
            P("groups"),
            P("groups"),
            P(("groups", "ctx"), None),
            P("groups", None),
        ),
        out_specs=P(("groups", "ctx"), None),
        check_vma=False,
    )
```

```python
import functools
import math

import jax
import jax.numpy as jnp
import numpy as np
from jax import lax
from jax.experimental import pallas as pl
from jax.experimental.pallas import tpu as pltpu
from jax.sharding import PartitionSpec as P

NEG_FILL = -1e30
CORES = 2
PLANE = 4
CHUNKS = 2
TILE = 16
MIB = 1 << 20


def in_hbm(x):
    return pltpu.with_memory_space_constraint(x, pltpu.HBM)


def hold(first, then):
    return lax.optimization_barrier((first, then))


class Ring:
    def __init__(self, groups, devices):
        chips = devices // CORES
        columns = max(1, PLANE // groups)
        if chips % columns:
            columns = 1
        depth = chips // columns
        order = []
        for column in range(columns):
            line = [level * columns + column for level in range(depth)]
            order += line if column % 2 == 0 else line[::-1]
        self.chips = chips
        self.half = chips // 2
        self.order = order
        self.swap = [(i, i ^ 1) for i in range(devices)]

    def go(self, block, hops):
        pairs = []
        for place in range(self.chips):
            here, there = self.order[place], self.order[(place + hops) % self.chips]
            pairs += [(here * CORES + core, there * CORES + core) for core in range(CORES)]
        return lax.ppermute(block, "ctx", pairs)

    def go_mate(self, block):
        return lax.ppermute(block, "ctx", self.swap)

    def go_split(self, block, hops):
        pairs = []
        for place in range(self.chips):
            for core, way in ((0, hops), (1, -hops)):
                here, there = self.order[place], self.order[(place + way) % self.chips]
                pairs.append((here * CORES + core, there * CORES + core))
        return lax.ppermute(block, "ctx", pairs)

    def owners(self, spots, swapped=False):
        place_of = {chip: place for place, chip in enumerate(self.order)}
        table = []
        for device in range(self.chips * CORES):
            chip, core = divmod(device, CORES)
            row = []
            for spot in spots:
                first = self.order[(place_of[chip] + spot[core]) % self.chips] * CORES + core
                row += [first ^ 1, first] if swapped else [first, first ^ 1]
            table.append(row)
        return np.asarray(table, np.int32)


def attention_kernel(
    count,
    pieces,
    heads,
    head_dim,
    query_rows,
    owner_ref,
    edge_ref,
    *refs,
):
    inputs, blocks_hbm, refs = refs[:6], refs[6 : 6 + pieces], refs[6 + pieces :]
    outputs, refs = refs[: CHUNKS + 1], refs[CHUNKS + 1 :]
    locals_, refs = refs[:6], refs[6:]
    (given, kept, blocks, stacked, scores, top, total, summed, sems) = refs
    fetches = [
        pltpu.make_async_copy(inputs[k], locals_[k], sems.at[pieces + k]) for k in range(6)
    ]
    arrivals, due, begin = [], {}, 0
    for j in range(pieces):
        size = blocks_hbm[j].shape[0]
        due[begin // (2 * query_rows)] = j
        arrivals.append(
            pltpu.make_async_copy(blocks_hbm[j], blocks.at[pl.ds(begin, size), :], sems.at[j])
        )
        begin += size
    for k in range(3):
        fetches[k].start()
    for arrival in arrivals:
        arrival.start()
    for k in range(3, 6):
        fetches[k].start()
    query_ref, pair_ref, role_ref, hidden_ref, gain_ref, weight_ref = locals_
    rows = query_ref.shape[0]
    for k in range(3):
        fetches[k].wait()
    me = owner_ref[0]
    for head in range(heads):
        stacked[pl.ds(head * rows, rows), :] = query_ref[:, head * head_dim : (head + 1) * head_dim]

    def column(ref):
        return jnp.broadcast_to(ref[pl.ds(me, 1), :], (rows, rows)).T

    query_pair, query_role = column(pair_ref), column(role_ref)
    query_pos = me * rows + lax.broadcasted_iota(jnp.int32, (rows, rows), 0)
    key_off = lax.broadcasted_iota(jnp.int32, (rows, rows), 1)

    def needed(owner):
        first_pair, last_pair = edge_ref[owner, 0], edge_ref[owner, 1]
        first_role, last_role = edge_ref[owner, 2], edge_ref[owner, 3]
        my_first, my_last = edge_ref[me, 0], edge_ref[me, 1]
        apart = (
            (first_pair == last_pair)
            & (my_first == my_last)
            & (first_role == last_role)
            & (edge_ref[me, 2] == edge_ref[me, 3])
            & (first_role != 0)
            & (first_role != edge_ref[me, 2])
        )
        return (owner <= me) & (last_pair >= my_first) & jnp.logical_not(apart)

    top[...] = jnp.full_like(top, NEG_FILL)
    total[...] = jnp.zeros_like(total)
    summed[...] = jnp.zeros_like(summed)
    for j in range(count):
        owner = owner_ref[j]
        if j in due:
            arrivals[due[j]].wait()

        @pl.when(needed(owner))
        def _():
            seen = (
                (query_pair == pair_ref[pl.ds(owner, 1), :])
                & (owner * rows + key_off <= query_pos)
                & (
                    (role_ref[pl.ds(owner, 1), :] == 0)
                    | (role_ref[pl.ds(owner, 1), :] == query_role)
                )
            )
            bias = jnp.where(seen, 0.0, NEG_FILL)
            raw = lax.dot_general(
                stacked[...],
                blocks[pl.ds(2 * j * rows, rows), :],
                (((1,), (1,)), ((), ())),
                preferred_element_type=jnp.float32,
            )
            masked = raw.reshape(heads, rows, rows) + bias[None]
            scores[j] = masked
            top[...] = jnp.maximum(top[...], masked)

    top[...] = jnp.broadcast_to(jnp.max(top[...], axis=-1, keepdims=True), top.shape)
    factor = math.log2(math.e) / math.sqrt(head_dim)
    for j in range(count):
        owner = owner_ref[j]

        @pl.when(needed(owner))
        def _():
            weights = jnp.exp2((scores[j] - top[...]) * factor)
            total[...] += weights
            summed[...] += jnp.dot(
                weights.astype(jnp.bfloat16).reshape(heads * rows, rows),
                blocks[pl.ds((2 * j + 1) * rows, rows), :],
                preferred_element_type=jnp.float32,
            ).reshape(heads, rows, head_dim)

    mixed = (summed[...] / jnp.sum(total[...], axis=-1, keepdims=True)).astype(jnp.bfloat16)
    mixed = jnp.concatenate([mixed[head] for head in range(heads)], axis=1)
    for k in range(3, 6):
        fetches[k].wait()
    projected = jnp.dot(mixed, weight_ref[...], preferred_element_type=jnp.float32)
    residual = (hidden_ref[...].astype(jnp.float32) + projected).astype(jnp.bfloat16)
    wide = residual.astype(jnp.float32)
    mean_sq = jnp.mean(wide * wide, axis=-1, keepdims=True)
    given[...] = (wide * lax.rsqrt(mean_sq + 1e-06) * gain_ref[...]).astype(jnp.bfloat16)
    kept[...] = residual
    part = rows // CHUNKS
    moves = [
        pltpu.make_async_copy(given.at[pl.ds(k * part, part), :], outputs[k], sems.at[k])
        for k in range(CHUNKS)
    ]
    moves.append(pltpu.make_async_copy(kept, outputs[CHUNKS], sems.at[CHUNKS]))
    for move in moves:
        move.start()
    for move in moves:
        move.wait()


def attend(owners, queries, hidden, gain, pair_ids, roles, out_weight, blocks):
    rows, width = queries.shape
    head_dim = blocks[0].shape[1]
    heads = width // head_dim
    count = owners.shape[0]
    total_rows = sum(b.shape[0] for b in blocks)
    pairs = pair_ids.reshape(-1, rows)
    parts = roles.reshape(-1, rows)
    edges = jnp.stack([pairs[:, 0], pairs[:, -1], parts[:, 0], parts[:, -1]], axis=1)
    smem = pl.BlockSpec(memory_space=pltpu.SMEM)
    hbm = pl.BlockSpec(memory_space=pltpu.HBM)
    square = pltpu.VMEM((heads, rows, rows), jnp.float32)
    chunk = jax.ShapeDtypeStruct((rows // CHUNKS, hidden.shape[1]), jnp.bfloat16)
    inputs = (queries, pairs, parts, hidden, gain.reshape(1, -1), out_weight)
    *chunks, residual = pl.pallas_call(
        functools.partial(attention_kernel, count, len(blocks), heads, head_dim, rows),
        out_shape=(chunk,) * CHUNKS + (jax.ShapeDtypeStruct(hidden.shape, jnp.bfloat16),),
        in_specs=[smem, smem] + [hbm] * (len(inputs) + len(blocks)),
        out_specs=(hbm,) * (CHUNKS + 1),
        scratch_shapes=[pltpu.VMEM(x.shape, x.dtype) for x in inputs]
        + [
            pltpu.VMEM(hidden.shape, jnp.bfloat16),
            pltpu.VMEM(hidden.shape, jnp.bfloat16),
            pltpu.VMEM((total_rows, head_dim), jnp.bfloat16),
            pltpu.VMEM((heads * rows, head_dim), jnp.bfloat16),
            pltpu.VMEM((count, heads, rows, rows), jnp.float32),
            square,
            square,
            pltpu.VMEM((heads, rows, head_dim), jnp.float32),
            pltpu.SemaphoreType.DMA((len(blocks) + len(inputs),)),
        ],
        compiler_params=pltpu.CompilerParams(vmem_limit_bytes=32 * MIB),
        name="attention",
    )(owners, edges, *(in_hbm(x) for x in inputs), *blocks)
    return residual, chunks


def join_kernel(count, *refs):
    inputs, own_ref, both_ref, sems = refs[:count], refs[count], refs[count + 1], refs[count + 2]
    rows = inputs[0].shape[0]
    moves = []
    for k in range(count):
        moves.append((inputs[k], both_ref, k))
        if k < count // CORES:
            moves.append((inputs[k], own_ref, k))
    moves = [
        pltpu.make_async_copy(src, dst.at[pl.ds(k * rows, rows), :], sems.at[n])
        for n, (src, dst, k) in enumerate(moves)
    ]
    for move in moves:
        move.start()
    for move in moves:
        move.wait()


def join(*parts):
    count = len(parts)
    rows, width = parts[0].shape
    vmem = pl.BlockSpec(memory_space=pltpu.VMEM)
    return pl.pallas_call(
        functools.partial(join_kernel, count),
        out_shape=(
            jax.ShapeDtypeStruct((count // CORES * rows, width), parts[0].dtype),
            jax.ShapeDtypeStruct((count * rows, width), parts[0].dtype),
        ),
        in_specs=[pl.BlockSpec(memory_space=pltpu.HBM)] * count,
        out_specs=(vmem, vmem),
        scratch_shapes=[pltpu.SemaphoreType.DMA((count + count // CORES,))],
        name="join",
    )(*parts)


def ffn_kernel(blocks, cuts, *refs):
    inputs, refs = refs[:blocks], refs[blocks:]
    weights_hbm, refs = refs[:6], refs[6:]
    outputs, refs = refs[:blocks], refs[blocks:]
    weights, (held, inner, total, given, in_sems, sems) = refs[:6], refs[6:]
    part = held.shape[0] // blocks
    pieces = len(cuts)

    def fetch(k, piece):
        begin, size = cuts[piece]
        span = pl.ds(begin, size)
        return pltpu.make_async_copy(
            weights_hbm[k].at[span, :], weights[k].at[span, :], sems.at[k * pieces + piece]
        )

    moves = [
        pltpu.make_async_copy(inputs[k], held.at[pl.ds(k * part, part), :], in_sems.at[k])
        for k in range(blocks)
    ]
    for move in moves:
        move.start()
    for side in range(2):
        for piece in range(pieces):
            fetch(3 * side, piece).start()
            fetch(3 * side + 1, piece).start()
        for piece in range(pieces):
            fetch(3 * side + 2, piece).start()
    for move in moves:
        move.wait()
    block = held[...]
    across = (((1,), (1,)), ((), ()))
    for side in range(2):
        gate, up, down = weights[3 * side : 3 * side + 3]
        for piece, (begin, size) in enumerate(cuts):
            span = pl.ds(begin, size)
            fetch(3 * side, piece).wait()
            gate_out = lax.dot_general(
                gate[span, :], block, across, preferred_element_type=jnp.float32
            )
            fetch(3 * side + 1, piece).wait()
            up_out = lax.dot_general(
                up[span, :], block, across, preferred_element_type=jnp.float32
            )
            inner[span, :] = (gate_out / (1.0 + jnp.exp(-gate_out)) * up_out).astype(jnp.bfloat16)
        for piece in range(pieces):
            fetch(3 * side + 2, piece).wait()
        term = jnp.dot(inner[...].T, down[...], preferred_element_type=jnp.float32)
        if side == 0:
            total[...] = term
        else:
            given[...] = (term + total[...]).astype(jnp.bfloat16)
    moves = [
        pltpu.make_async_copy(given.at[pl.ds(k * part, part), :], outputs[k], in_sems.at[k])
        for k in range(blocks)
    ]
    for move in moves:
        move.start()
    for move in moves:
        move.wait()


def ffn(blocks, weights):
    count = len(blocks)
    rows, width = blocks[0].shape
    hidden = weights[0].shape[0]
    cuts = [(0, hidden)]
    if hidden % TILE == 0:
        first = hidden // (2 * TILE) * TILE
        cuts = [(0, first), (first, hidden - first)]
    hbm = pl.BlockSpec(memory_space=pltpu.HBM)
    flops = 2 * count * rows * sum(w.size for w in weights)
    return pl.pallas_call(
        functools.partial(ffn_kernel, count, cuts),
        out_shape=tuple(jax.ShapeDtypeStruct(b.shape, jnp.bfloat16) for b in blocks),
        in_specs=[hbm] * (count + 6),
        out_specs=(hbm,) * count,
        scratch_shapes=[pltpu.VMEM(w.shape, w.dtype) for w in weights]
        + [
            pltpu.VMEM((count * rows, width), jnp.bfloat16),
            pltpu.VMEM((hidden, count * rows), jnp.bfloat16),
            pltpu.VMEM((count * rows, width), jnp.float32),
            pltpu.VMEM((count * rows, width), jnp.bfloat16),
            pltpu.SemaphoreType.DMA((count,)),
            pltpu.SemaphoreType.DMA((6 * len(cuts),)),
        ],
        compiler_params=pltpu.CompilerParams(vmem_limit_bytes=36 * MIB),
        cost_estimate=pl.CostEstimate(
            flops=flops,
            transcendentals=0,
            bytes_accessed=2 * sum(w.size for w in weights),
        ),
        name="feed_forward",
    )(*blocks, *(in_hbm(w) for w in weights))


def feed_forward(ring, chunks, weights):
    half = ring.half

    def send(pair, way):
        first, second = hold(*pair)
        return ring.go(first, way), ring.go(second, -way)

    held = [[(chunks[0], chunks[1])], [(chunks[1], chunks[0])]]
    terms = [{}, {}]
    for group in range(2):
        held[group].append(send(held[group][0], 1))
    own = ffn(held[0][0], weights)
    last = own
    for step in range(1, half):
        last, pair = hold(last, held[0][step])
        held[0].append(send(pair, 1))
        if step + 1 < half:
            held[1].append(send(hold(last, held[1][step])[1], 1))
        last = ffn(held[0][step] + held[1][step], weights)
        terms[0][step], terms[1][step] = last[:2], last[2:]
    _, pair = hold(last, held[0][half])
    terms[0][half] = ffn(pair, weights)

    def add(a, b):
        return (a.astype(jnp.float32) + b.astype(jnp.float32)).astype(jnp.bfloat16)

    home = [None, None]
    order = []
    for step in range(half - 1, 0, -1):
        order += [(1, step), (0, step + 1)]
    order.append((0, 1))
    for group, step in order:
        pair = terms[group][step]
        if home[group] is not None:
            pair = (add(home[group][0], pair[0]), add(home[group][1], pair[1]))
        home[group] = send(pair, -1)
    wide = [[x.astype(jnp.float32) for x in pair] for pair in (own, home[0], home[1])]
    return [wide[0][0] + wide[2][1] + wide[1][0], wide[0][1] + wide[2][0] + wide[1][1]]


def gather_kv(ring, keys, values):
    own, both = join(
        in_hbm(keys), in_hbm(values), ring.go_mate(keys), ring.go_mate(values)
    )
    blocks = [both]
    owners = [ring.owners([(0, 0)])]
    sent = [ring.go_split(both, hops) for hops in range(1, ring.half)]
    far = ring.go(own, ring.half)
    owners += [ring.owners([(-hops, hops)]) for hops in range(1, ring.half)]
    owners += [ring.owners([(hops, -hops)], True) for hops in range(1, ring.half)]
    across = ring.owners([(ring.half, ring.half)])
    blocks += sent + [ring.go_mate(b) for b in sent] + [far, ring.go_mate(far)]
    return blocks, np.concatenate(owners + [across], axis=1), (sent, far)


def on_device(
    ring,
    hidden_in,
    queries,
    keys,
    values,
    out_weight,
    norm_gain,
    gate_weight,
    up_weight,
    down_weight,
    pair_ids,
    roles,
    send_rows,
    send_counts,
):
    my_index = lax.axis_index("ctx")
    tok_rows = hidden_in.shape[0]
    own = (gate_weight.T, up_weight.T, down_weight)
    blocks, table, arrived = gather_kv(ring, keys, values)
    gate_mate = ring.go_mate(own[0])
    up_mate = ring.go_mate(hold(arrived, own[1])[1])
    down_mate = ring.go_mate(hold(up_mate, own[2])[1])
    mates = (gate_mate, up_mate, down_mate)
    owners = jnp.asarray(table)[my_index]
    residual, chunks = attend(
        owners, queries, hidden_in, norm_gain, pair_ids, roles, out_weight, blocks
    )
    summed = feed_forward(ring, chunks, own + mates)
    my_roles = lax.dynamic_slice_in_dim(roles, my_index * tok_rows, tok_rows)
    live = (my_roles != 0).astype(jnp.float32)
    ffn_back = jnp.concatenate(summed, axis=0).astype(jnp.bfloat16).astype(jnp.float32)
    return (residual.astype(jnp.float32) + ffn_back * live[:, None]).astype(jnp.bfloat16)


def solution(mesh):
    ring = Ring(mesh.shape["groups"], mesh.shape["ctx"])

    def run(*arrays):
        return on_device(ring, *arrays)

    return jax.shard_map(
        run,
        mesh=mesh,
        in_specs=(
            P(("groups", "ctx"), None),
            P(("groups", "ctx"), None),
            P(("groups", "ctx"), None),
            P(("groups", "ctx"), None),
            P(),
            P(),
            P(None, "ctx"),
            P(None, "ctx"),
            P("ctx", None),
            P("groups"),
            P("groups"),
            P(("groups", "ctx"), None),
            P("groups", None),
        ),
        out_specs=P(("groups", "ctx"), None),
        check_vma=False,
    )
```

```python
import functools
import math

import jax
import jax.numpy as jnp
import numpy as np
from jax import lax
from jax.experimental import pallas as pl
from jax.experimental.pallas import tpu as pltpu
from jax.sharding import PartitionSpec as P

NEG_FILL = -1e30
CORES = 2
PLANE = 4
CHUNKS = 2
TILE = 16
MIB = 1 << 20


def in_hbm(x):
    return pltpu.with_memory_space_constraint(x, pltpu.HBM)


def hold(first, then):
    return lax.optimization_barrier((first, then))


class Ring:
    def __init__(self, groups, devices):
        chips = devices // CORES
        columns = max(1, PLANE // groups)
        if chips % columns:
            columns = 1
        depth = chips // columns
        order = []
        for column in range(columns):
            line = [level * columns + column for level in range(depth)]
            order += line if column % 2 == 0 else line[::-1]
        self.chips = chips
        self.half = chips // 2
        self.order = order
        self.swap = [(i, i ^ 1) for i in range(devices)]

    def go(self, block, hops):
        pairs = []
        for place in range(self.chips):
            here, there = self.order[place], self.order[(place + hops) % self.chips]
            pairs += [(here * CORES + core, there * CORES + core) for core in range(CORES)]
        return lax.ppermute(block, "ctx", pairs)

    def go_mate(self, block):
        return lax.ppermute(block, "ctx", self.swap)

    def go_split(self, block, hops):
        pairs = []
        for place in range(self.chips):
            for core, way in ((0, hops), (1, -hops)):
                here, there = self.order[place], self.order[(place + way) % self.chips]
                pairs.append((here * CORES + core, there * CORES + core))
        return lax.ppermute(block, "ctx", pairs)

    def owners(self, spots, swapped=False):
        place_of = {chip: place for place, chip in enumerate(self.order)}
        table = []
        for device in range(self.chips * CORES):
            chip, core = divmod(device, CORES)
            row = []
            for spot in spots:
                first = self.order[(place_of[chip] + spot[core]) % self.chips] * CORES + core
                row += [first ^ 1, first] if swapped else [first, first ^ 1]
            table.append(row)
        return np.asarray(table, np.int32)


def attention_kernel(
    count,
    pieces,
    heads,
    head_dim,
    query_rows,
    owner_ref,
    edge_ref,
    *refs,
):
    inputs, blocks_hbm, refs = refs[:6], refs[6 : 6 + pieces], refs[6 + pieces :]
    outputs, refs = refs[: CHUNKS + 1], refs[CHUNKS + 1 :]
    locals_, refs = refs[:6], refs[6:]
    (given, kept, blocks, stacked, scores, top, total, summed, sems) = refs
    fetches = [
        pltpu.make_async_copy(inputs[k], locals_[k], sems.at[pieces + k]) for k in range(6)
    ]
    arrivals, due, begin = [], {}, 0
    for j in range(pieces):
        size = blocks_hbm[j].shape[0]
        due[begin // (2 * query_rows)] = j
        arrivals.append(
            pltpu.make_async_copy(blocks_hbm[j], blocks.at[pl.ds(begin, size), :], sems.at[j])
        )
        begin += size
    for k in range(3):
        fetches[k].start()
    for arrival in arrivals:
        arrival.start()
    for k in range(3, 6):
        fetches[k].start()
    query_ref, pair_ref, role_ref, hidden_ref, gain_ref, weight_ref = locals_
    rows = query_ref.shape[0]
    for k in range(3):
        fetches[k].wait()
    me = owner_ref[0]
    for head in range(heads):
        stacked[pl.ds(head * rows, rows), :] = query_ref[:, head * head_dim : (head + 1) * head_dim]

    def column(ref):
        return jnp.broadcast_to(ref[pl.ds(me, 1), :], (rows, rows)).T

    query_pair, query_role = column(pair_ref), column(role_ref)
    query_pos = me * rows + lax.broadcasted_iota(jnp.int32, (rows, rows), 0)
    key_off = lax.broadcasted_iota(jnp.int32, (rows, rows), 1)

    def needed(owner):
        first_pair, last_pair = edge_ref[owner, 0], edge_ref[owner, 1]
        first_role, last_role = edge_ref[owner, 2], edge_ref[owner, 3]
        my_first, my_last = edge_ref[me, 0], edge_ref[me, 1]
        apart = (
            (first_pair == last_pair)
            & (my_first == my_last)
            & (first_role == last_role)
            & (edge_ref[me, 2] == edge_ref[me, 3])
            & (first_role != 0)
            & (first_role != edge_ref[me, 2])
        )
        return (owner <= me) & (last_pair >= my_first) & jnp.logical_not(apart)

    top[...] = jnp.full_like(top, NEG_FILL)
    total[...] = jnp.zeros_like(total)
    summed[...] = jnp.zeros_like(summed)
    for j in range(count):
        owner = owner_ref[j]
        if j in due:
            arrivals[due[j]].wait()

        @pl.when(needed(owner))
        def _():
            seen = (
                (query_pair == pair_ref[pl.ds(owner, 1), :])
                & (owner * rows + key_off <= query_pos)
                & (
                    (role_ref[pl.ds(owner, 1), :] == 0)
                    | (role_ref[pl.ds(owner, 1), :] == query_role)
                )
            )
            bias = jnp.where(seen, 0.0, NEG_FILL)
            raw = lax.dot_general(
                stacked[...],
                blocks[pl.ds(2 * j * rows, rows), :],
                (((1,), (1,)), ((), ())),
                preferred_element_type=jnp.float32,
            )
            masked = raw.reshape(heads, rows, rows) + bias[None]
            scores[j] = masked
            top[...] = jnp.maximum(top[...], masked)

    top[...] = jnp.broadcast_to(jnp.max(top[...], axis=-1, keepdims=True), top.shape)
    factor = math.log2(math.e) / math.sqrt(head_dim)
    for j in range(count):
        owner = owner_ref[j]

        @pl.when(needed(owner))
        def _():
            weights = jnp.exp2((scores[j] - top[...]) * factor)
            total[...] += weights
            summed[...] += jnp.dot(
                weights.astype(jnp.bfloat16).reshape(heads * rows, rows),
                blocks[pl.ds((2 * j + 1) * rows, rows), :],
                preferred_element_type=jnp.float32,
            ).reshape(heads, rows, head_dim)

    mixed = (summed[...] / jnp.sum(total[...], axis=-1, keepdims=True)).astype(jnp.bfloat16)
    mixed = jnp.concatenate([mixed[head] for head in range(heads)], axis=1)
    for k in range(3, 6):
        fetches[k].wait()
    projected = jnp.dot(mixed, weight_ref[...], preferred_element_type=jnp.float32)
    residual = (hidden_ref[...].astype(jnp.float32) + projected).astype(jnp.bfloat16)
    wide = residual.astype(jnp.float32)
    mean_sq = jnp.mean(wide * wide, axis=-1, keepdims=True)
    given[...] = (wide * lax.rsqrt(mean_sq + 1e-06) * gain_ref[...]).astype(jnp.bfloat16)
    kept[...] = residual
    part = rows // CHUNKS
    moves = [
        pltpu.make_async_copy(given.at[pl.ds(k * part, part), :], outputs[k], sems.at[k])
        for k in range(CHUNKS)
    ]
    moves.append(pltpu.make_async_copy(kept, outputs[CHUNKS], sems.at[CHUNKS]))
    for move in moves:
        move.start()
    for move in moves:
        move.wait()


def attend(owners, queries, hidden, gain, pair_ids, roles, out_weight, blocks):
    rows, width = queries.shape
    head_dim = blocks[0].shape[1]
    heads = width // head_dim
    count = owners.shape[0]
    total_rows = sum(b.shape[0] for b in blocks)
    pairs = pair_ids.reshape(-1, rows)
    parts = roles.reshape(-1, rows)
    edges = jnp.stack([pairs[:, 0], pairs[:, -1], parts[:, 0], parts[:, -1]], axis=1)
    smem = pl.BlockSpec(memory_space=pltpu.SMEM)
    hbm = pl.BlockSpec(memory_space=pltpu.HBM)
    square = pltpu.VMEM((heads, rows, rows), jnp.float32)
    chunk = jax.ShapeDtypeStruct((rows // CHUNKS, hidden.shape[1]), jnp.bfloat16)
    inputs = (queries, pairs, parts, hidden, gain.reshape(1, -1), out_weight)
    *chunks, residual = pl.pallas_call(
        functools.partial(attention_kernel, count, len(blocks), heads, head_dim, rows),
        out_shape=(chunk,) * CHUNKS + (jax.ShapeDtypeStruct(hidden.shape, jnp.bfloat16),),
        in_specs=[smem, smem] + [hbm] * (len(inputs) + len(blocks)),
        out_specs=(hbm,) * (CHUNKS + 1),
        scratch_shapes=[pltpu.VMEM(x.shape, x.dtype) for x in inputs]
        + [
            pltpu.VMEM(hidden.shape, jnp.bfloat16),
            pltpu.VMEM(hidden.shape, jnp.bfloat16),
            pltpu.VMEM((total_rows, head_dim), jnp.bfloat16),
            pltpu.VMEM((heads * rows, head_dim), jnp.bfloat16),
            pltpu.VMEM((count, heads, rows, rows), jnp.float32),
            square,
            square,
            pltpu.VMEM((heads, rows, head_dim), jnp.float32),
            pltpu.SemaphoreType.DMA((len(blocks) + len(inputs),)),
        ],
        compiler_params=pltpu.CompilerParams(vmem_limit_bytes=32 * MIB),
        name="attention",
    )(owners, edges, *(in_hbm(x) for x in inputs), *blocks)
    return residual, chunks


def join_kernel(count, *refs):
    inputs, both_ref, sems = refs[:count], refs[count], refs[count + 1]
    rows = inputs[0].shape[0]
    moves = [
        pltpu.make_async_copy(inputs[k], both_ref.at[pl.ds(k * rows, rows), :], sems.at[k])
        for k in range(count)
    ]
    for move in moves:
        move.start()
    for move in moves:
        move.wait()


def join(*parts):
    count = len(parts)
    rows, width = parts[0].shape
    return pl.pallas_call(
        functools.partial(join_kernel, count),
        out_shape=jax.ShapeDtypeStruct((count * rows, width), parts[0].dtype),
        in_specs=[pl.BlockSpec(memory_space=pltpu.HBM)] * count,
        out_specs=pl.BlockSpec(memory_space=pltpu.VMEM),
        scratch_shapes=[pltpu.SemaphoreType.DMA((count,))],
        name="join",
    )(*parts)


def ffn_kernel(blocks, cuts, *refs):
    inputs, refs = refs[:blocks], refs[blocks:]
    weights_hbm, refs = refs[:6], refs[6:]
    outputs, refs = refs[:blocks], refs[blocks:]
    weights, (held, turned, inner, total, given, in_sems, sems) = refs[:6], refs[6:]
    part = held.shape[0] // blocks
    pieces = len(cuts)

    def fetch(k, piece):
        begin, size = cuts[piece]
        span = pl.ds(begin, size)
        return pltpu.make_async_copy(
            weights_hbm[k].at[span, :], weights[k].at[span, :], sems.at[k * pieces + piece]
        )

    moves = [
        pltpu.make_async_copy(inputs[k], held.at[pl.ds(k * part, part), :], in_sems.at[k])
        for k in range(blocks)
    ]
    for move in moves:
        move.start()
    for side in range(2):
        for piece in range(pieces):
            fetch(3 * side, piece).start()
            fetch(3 * side + 1, piece).start()
        for piece in range(pieces):
            fetch(3 * side + 2, piece).start()
    for move in moves:
        move.wait()
    turned[...] = held[...].T
    for side in range(2):
        gate, up, down = weights[3 * side : 3 * side + 3]
        for piece, (begin, size) in enumerate(cuts):
            span = pl.ds(begin, size)
            fetch(3 * side, piece).wait()
            gate_out = jnp.dot(gate[span, :], turned[...], preferred_element_type=jnp.float32)
            fetch(3 * side + 1, piece).wait()
            up_out = jnp.dot(up[span, :], turned[...], preferred_element_type=jnp.float32)
            inner[span, :] = (gate_out / (1.0 + jnp.exp(-gate_out)) * up_out).astype(jnp.bfloat16)
        for piece in range(pieces):
            fetch(3 * side + 2, piece).wait()
        term = jnp.dot(inner[...].T, down[...], preferred_element_type=jnp.float32)
        if side == 0:
            total[...] = term
        else:
            given[...] = (term + total[...]).astype(jnp.bfloat16)
    moves = [
        pltpu.make_async_copy(given.at[pl.ds(k * part, part), :], outputs[k], in_sems.at[k])
        for k in range(blocks)
    ]
    for move in moves:
        move.start()
    for move in moves:
        move.wait()


def ffn(blocks, weights):
    count = len(blocks)
    rows, width = blocks[0].shape
    hidden = weights[0].shape[0]
    cuts = [(0, hidden)]
    if hidden % TILE == 0:
        first = hidden // (2 * TILE) * TILE
        cuts = [(0, first), (first, hidden - first)]
    hbm = pl.BlockSpec(memory_space=pltpu.HBM)
    flops = 2 * count * rows * sum(w.size for w in weights)
    return pl.pallas_call(
        functools.partial(ffn_kernel, count, cuts),
        out_shape=tuple(jax.ShapeDtypeStruct(b.shape, jnp.bfloat16) for b in blocks),
        in_specs=[hbm] * (count + 6),
        out_specs=(hbm,) * count,
        scratch_shapes=[pltpu.VMEM(w.shape, w.dtype) for w in weights]
        + [
            pltpu.VMEM((count * rows, width), jnp.bfloat16),
            pltpu.VMEM((width, count * rows), jnp.bfloat16),
            pltpu.VMEM((hidden, count * rows), jnp.bfloat16),
            pltpu.VMEM((count * rows, width), jnp.float32),
            pltpu.VMEM((count * rows, width), jnp.bfloat16),
            pltpu.SemaphoreType.DMA((count,)),
            pltpu.SemaphoreType.DMA((6 * len(cuts),)),
        ],
        compiler_params=pltpu.CompilerParams(vmem_limit_bytes=36 * MIB),
        cost_estimate=pl.CostEstimate(
            flops=flops,
            transcendentals=0,
            bytes_accessed=2 * sum(w.size for w in weights),
        ),
        name="feed_forward",
    )(*blocks, *(in_hbm(w) for w in weights))


def feed_forward(ring, chunks, weights):
    half = ring.half

    def send(pair, way):
        first, second = hold(*pair)
        return ring.go(first, way), ring.go(second, -way)

    held = [[(chunks[0], chunks[1])], [(chunks[1], chunks[0])]]
    terms = [{}, {}]
    for group in range(2):
        held[group].append(send(held[group][0], 1))
    own = ffn(held[0][0], weights)
    last = own
    for step in range(1, half):
        last, pair = hold(last, held[0][step])
        held[0].append(send(pair, 1))
        if step + 1 < half:
            pair = held[1][step]
            if step == 1:
                last, pair = hold(last, pair)
            held[1].append(send(pair, 1))
        if step == 1:
            own = last
        else:
            terms[0][step - 1], terms[1][step - 1] = last[:2], last[2:]
        last = ffn(held[0][step] + held[1][step], weights)
    last, pair = hold(last, held[0][half])
    terms[0][half - 1], terms[1][half - 1] = last[:2], last[2:]
    terms[0][half] = ffn(pair, weights)

    def add(a, b):
        return (a.astype(jnp.float32) + b.astype(jnp.float32)).astype(jnp.bfloat16)

    home = [None, None]
    order = []
    for step in range(half - 1, 0, -1):
        order += [(1, step), (0, step + 1)]
    order.append((0, 1))
    for group, step in order:
        pair = terms[group][step]
        if home[group] is not None:
            pair = (add(home[group][0], pair[0]), add(home[group][1], pair[1]))
        if step == half:
            home[1], pair = hold(home[1], pair)
        home[group] = send(pair, -1)
    wide = [[x.astype(jnp.float32) for x in pair] for pair in (own, home[0], home[1])]
    return [wide[0][0] + wide[2][1] + wide[1][0], wide[0][1] + wide[2][0] + wide[1][1]]


def gather_kv(ring, keys, values, weights):
    half = ring.half
    gate, up, down = weights
    gate_mate = ring.go_mate(gate)
    both = join(in_hbm(keys), in_hbm(values), ring.go_mate(keys), ring.go_mate(values))
    gate_mate, up, both = lax.optimization_barrier((gate_mate, up, both))
    up_mate = ring.go_mate(up)
    held, mates = {0: both}, {}
    reach = 0
    while reach < half:
        fresh = range(reach + 1, min(reach + 2, half) + 1)
        for hops in fresh:
            jump = min(2, hops)
            held[hops] = ring.go_split(held[hops - jump], jump)
        for hops in range(max(1, reach - 1), reach + 1):
            mates[hops] = ring.go_mate(held[hops])
        held, mates = lax.optimization_barrier((held, mates))
        reach = fresh[-1]
    up_mate, down, held = lax.optimization_barrier((up_mate, down, held))
    down_mate = ring.go_mate(down)
    for hops in range(1, half):
        if hops not in mates:
            mates[hops] = ring.go_mate(held[hops])
    blocks = [held[hops] for hops in range(half + 1)] + [mates[hops] for hops in range(1, half)]
    owners = [ring.owners([(-hops, hops)]) for hops in range(half + 1)]
    owners += [ring.owners([(hops, -hops)], True) for hops in range(1, half)]
    return blocks, np.concatenate(owners, axis=1), (gate_mate, up_mate, down_mate)


def on_device(
    ring,
    hidden_in,
    queries,
    keys,
    values,
    out_weight,
    norm_gain,
    gate_weight,
    up_weight,
    down_weight,
    pair_ids,
    roles,
    send_rows,
    send_counts,
):
    my_index = lax.axis_index("ctx")
    tok_rows = hidden_in.shape[0]
    own = (gate_weight.T, up_weight.T, down_weight)
    blocks, table, mates = gather_kv(ring, keys, values, own)
    owners = jnp.asarray(table)[my_index]
    residual, chunks = attend(
        owners, queries, hidden_in, norm_gain, pair_ids, roles, out_weight, blocks
    )
    summed = feed_forward(ring, chunks, own + mates)
    my_roles = lax.dynamic_slice_in_dim(roles, my_index * tok_rows, tok_rows)
    live = (my_roles != 0).astype(jnp.float32)
    ffn_back = jnp.concatenate(summed, axis=0).astype(jnp.bfloat16).astype(jnp.float32)
    return (residual.astype(jnp.float32) + ffn_back * live[:, None]).astype(jnp.bfloat16)


def solution(mesh):
    ring = Ring(mesh.shape["groups"], mesh.shape["ctx"])

    def run(*arrays):
        return on_device(ring, *arrays)

    return jax.shard_map(
        run,
        mesh=mesh,
        in_specs=(
            P(("groups", "ctx"), None),
            P(("groups", "ctx"), None),
            P(("groups", "ctx"), None),
            P(("groups", "ctx"), None),
            P(),
            P(),
            P(None, "ctx"),
            P(None, "ctx"),
            P("ctx", None),
            P("groups"),
            P("groups"),
            P(("groups", "ctx"), None),
            P("groups", None),
        ),
        out_specs=P(("groups", "ctx"), None),
        check_vma=False,
    )
```

```python
import functools
import math

import jax
import jax.numpy as jnp
import numpy as np
from jax import lax
from jax.experimental import pallas as pl
from jax.experimental.pallas import tpu as pltpu
from jax.sharding import PartitionSpec as P

NEG_FILL = -1e30
CORES = 2
PLANE = 4
CHUNKS = 2
TILE = 16
WINDOW = 3
MIB = 1 << 20


def in_hbm(x):
    return pltpu.with_memory_space_constraint(x, pltpu.HBM)


def hold(first, then):
    return lax.optimization_barrier((first, then))


class Ring:
    def __init__(self, groups, devices):
        chips = devices // CORES
        columns = max(1, PLANE // groups)
        if chips % columns:
            columns = 1
        depth = chips // columns
        order = []
        for column in range(columns):
            line = [level * columns + column for level in range(depth)]
            order += line if column % 2 == 0 else line[::-1]
        self.chips = chips
        self.half = chips // 2
        self.order = order
        self.swap = [(i, i ^ 1) for i in range(devices)]

    def go(self, block, hops):
        pairs = []
        for place in range(self.chips):
            here, there = self.order[place], self.order[(place + hops) % self.chips]
            pairs += [(here * CORES + core, there * CORES + core) for core in range(CORES)]
        return lax.ppermute(block, "ctx", pairs)

    def go_mate(self, block):
        return lax.ppermute(block, "ctx", self.swap)

    def go_split(self, block, hops):
        pairs = []
        for place in range(self.chips):
            for core, way in ((0, hops), (1, -hops)):
                here, there = self.order[place], self.order[(place + way) % self.chips]
                pairs.append((here * CORES + core, there * CORES + core))
        return lax.ppermute(block, "ctx", pairs)

    def owners(self, spots, swapped=False):
        place_of = {chip: place for place, chip in enumerate(self.order)}
        table = []
        for device in range(self.chips * CORES):
            chip, core = divmod(device, CORES)
            row = []
            for spot in spots:
                first = self.order[(place_of[chip] + spot[core]) % self.chips] * CORES + core
                row += [first ^ 1, first] if swapped else [first, first ^ 1]
            table.append(row)
        return np.asarray(table, np.int32)


def attention_kernel(
    count,
    pieces,
    heads,
    head_dim,
    owner_ref,
    pair_smem,
    role_smem,
    *refs,
):
    inputs, blocks_hbm, refs = refs[:6], refs[6 : 6 + pieces], refs[6 + pieces :]
    outputs, refs = refs[: CHUNKS + 1], refs[CHUNKS + 1 :]
    locals_, refs = refs[:6], refs[6:]
    (given, kept, blocks, stacked, scores, top, total, summed, sems) = refs
    fetches = [
        pltpu.make_async_copy(inputs[k], locals_[k], sems.at[pieces + k]) for k in range(6)
    ]
    arrivals, begin = [], 0
    for j in range(pieces):
        size = blocks_hbm[j].shape[0]
        arrivals.append(
            pltpu.make_async_copy(blocks_hbm[j], blocks.at[pl.ds(begin, size), :], sems.at[j])
        )
        begin += size
    for k in range(3):
        fetches[k].start()
    for arrival in arrivals:
        arrival.start()
    query_ref, pair_ref, role_ref, hidden_ref, gain_ref, weight_ref = locals_
    rows = query_ref.shape[0]
    for k in range(3):
        fetches[k].wait()
    for arrival in arrivals:
        arrival.wait()
    for k in range(3, 6):
        fetches[k].start()
    me = owner_ref[0]
    for head in range(heads):
        stacked[pl.ds(head * rows, rows), :] = query_ref[:, head * head_dim : (head + 1) * head_dim]

    def column(ref):
        return jnp.broadcast_to(ref[pl.ds(me, 1), :], (rows, rows)).T

    query_pair, query_role = column(pair_ref), column(role_ref)
    query_pos = me * rows + lax.broadcasted_iota(jnp.int32, (rows, rows), 0)
    key_off = lax.broadcasted_iota(jnp.int32, (rows, rows), 1)

    def needed(owner):
        first_pair, last_pair = pair_smem[owner, 0], pair_smem[owner, rows - 1]
        first_role, last_role = role_smem[owner, 0], role_smem[owner, rows - 1]
        my_first, my_last = pair_smem[me, 0], pair_smem[me, rows - 1]
        my_role = role_smem[me, 0]
        apart = (
            (first_pair == last_pair)
            & (my_first == my_last)
            & (first_role == last_role)
            & (my_role == role_smem[me, rows - 1])
            & (first_role != 0)
            & (first_role != my_role)
        )
        return (owner <= me) & (last_pair >= my_first) & jnp.logical_not(apart)

    top[...] = jnp.full_like(top, NEG_FILL)
    total[...] = jnp.zeros_like(total)
    summed[...] = jnp.zeros_like(summed)
    for j in range(count):
        owner = owner_ref[j]

        @pl.when(needed(owner))
        def _():
            seen = (
                (query_pair == pair_ref[pl.ds(owner, 1), :])
                & (owner * rows + key_off <= query_pos)
                & (
                    (role_ref[pl.ds(owner, 1), :] == 0)
                    | (role_ref[pl.ds(owner, 1), :] == query_role)
                )
            )
            bias = jnp.where(seen, 0.0, NEG_FILL)
            raw = lax.dot_general(
                stacked[...],
                blocks[pl.ds(2 * j * rows, rows), :],
                (((1,), (1,)), ((), ())),
                preferred_element_type=jnp.float32,
            )
            masked = raw.reshape(heads, rows, rows) + bias[None]
            scores[j] = masked
            top[...] = jnp.maximum(top[...], masked)

    top[...] = jnp.broadcast_to(jnp.max(top[...], axis=-1, keepdims=True), top.shape)
    factor = math.log2(math.e) / math.sqrt(head_dim)
    for j in range(count):
        owner = owner_ref[j]

        @pl.when(needed(owner))
        def _():
            weights = jnp.exp2((scores[j] - top[...]) * factor)
            total[...] += weights
            summed[...] += jnp.dot(
                weights.astype(jnp.bfloat16).reshape(heads * rows, rows),
                blocks[pl.ds((2 * j + 1) * rows, rows), :],
                preferred_element_type=jnp.float32,
            ).reshape(heads, rows, head_dim)

    mixed = (summed[...] / jnp.sum(total[...], axis=-1, keepdims=True)).astype(jnp.bfloat16)
    mixed = jnp.concatenate([mixed[head] for head in range(heads)], axis=1)
    for k in range(3, 6):
        fetches[k].wait()
    projected = jnp.dot(mixed, weight_ref[...], preferred_element_type=jnp.float32)
    residual = (hidden_ref[...].astype(jnp.float32) + projected).astype(jnp.bfloat16)
    wide = residual.astype(jnp.float32)
    mean_sq = jnp.mean(wide * wide, axis=-1, keepdims=True)
    given[...] = (wide * lax.rsqrt(mean_sq + 1e-06) * gain_ref[...]).astype(jnp.bfloat16)
    kept[...] = residual
    part = rows // CHUNKS
    moves = [
        pltpu.make_async_copy(given.at[pl.ds(k * part, part), :], outputs[k], sems.at[k])
        for k in range(CHUNKS)
    ]
    moves.append(pltpu.make_async_copy(kept, outputs[CHUNKS], sems.at[CHUNKS]))
    for move in moves:
        move.start()
    for move in moves:
        move.wait()


def attend(owners, queries, pairs, parts, hidden, gain, out_weight, blocks):
    rows, width = queries.shape
    head_dim = blocks[0].shape[1]
    heads = width // head_dim
    count = owners.shape[0]
    total_rows = sum(b.shape[0] for b in blocks)
    smem = pl.BlockSpec(memory_space=pltpu.SMEM)
    hbm = pl.BlockSpec(memory_space=pltpu.HBM)
    square = pltpu.VMEM((heads, rows, rows), jnp.float32)
    chunk = jax.ShapeDtypeStruct((rows // CHUNKS, hidden.shape[1]), jnp.bfloat16)
    inputs = (queries, pairs, parts, hidden, gain.reshape(1, -1), out_weight)
    *chunks, residual = pl.pallas_call(
        functools.partial(attention_kernel, count, len(blocks), heads, head_dim),
        out_shape=(chunk,) * CHUNKS + (jax.ShapeDtypeStruct(hidden.shape, jnp.bfloat16),),
        in_specs=[smem] * 3 + [hbm] * (len(inputs) + len(blocks)),
        out_specs=(hbm,) * (CHUNKS + 1),
        scratch_shapes=[pltpu.VMEM(x.shape, x.dtype) for x in inputs]
        + [
            pltpu.VMEM(hidden.shape, jnp.bfloat16),
            pltpu.VMEM(hidden.shape, jnp.bfloat16),
            pltpu.VMEM((total_rows, head_dim), jnp.bfloat16),
            pltpu.VMEM((heads * rows, head_dim), jnp.bfloat16),
            pltpu.VMEM((count, heads, rows, rows), jnp.float32),
            square,
            square,
            pltpu.VMEM((heads, rows, head_dim), jnp.float32),
            pltpu.SemaphoreType.DMA((len(blocks) + len(inputs),)),
        ],
        compiler_params=pltpu.CompilerParams(vmem_limit_bytes=32 * MIB),
        name="attention",
    )(owners, pairs, parts, *(in_hbm(x) for x in inputs), *blocks)
    return residual, chunks


def join_kernel(count, *refs):
    inputs, both_ref, sems = refs[:count], refs[count], refs[count + 1]
    rows = inputs[0].shape[0]
    moves = [
        pltpu.make_async_copy(inputs[k], both_ref.at[pl.ds(k * rows, rows), :], sems.at[k])
        for k in range(count)
    ]
    for move in moves:
        move.start()
    for move in moves:
        move.wait()


def join(*parts):
    count = len(parts)
    rows, width = parts[0].shape
    return pl.pallas_call(
        functools.partial(join_kernel, count),
        out_shape=jax.ShapeDtypeStruct((count * rows, width), parts[0].dtype),
        in_specs=[pl.BlockSpec(memory_space=pl.ANY)] * count,
        out_specs=pl.BlockSpec(memory_space=pltpu.VMEM),
        scratch_shapes=[pltpu.SemaphoreType.DMA((count,))],
        name="join",
    )(*parts)


def ffn_kernel(blocks, cuts, *refs):
    inputs, refs = refs[:blocks], refs[blocks:]
    weights_hbm, refs = refs[:6], refs[6:]
    outputs, refs = refs[:blocks], refs[blocks:]
    weights, (held, turned, inner, total, given, in_sems, sems) = refs[:6], refs[6:]
    part = held.shape[0] // blocks
    pieces = len(cuts)

    def fetch(k, piece):
        begin, size = cuts[piece]
        span = pl.ds(begin, size)
        return pltpu.make_async_copy(
            weights_hbm[k].at[span, :], weights[k].at[span, :], sems.at[k * pieces + piece]
        )

    moves = [
        pltpu.make_async_copy(inputs[k], held.at[pl.ds(k * part, part), :], in_sems.at[k])
        for k in range(blocks)
    ]
    for move in moves:
        move.start()
    queue = []
    for side in range(2):
        for piece in range(pieces):
            queue += [(3 * side, piece), (3 * side + 1, piece)]
        queue += [(3 * side + 2, piece) for piece in range(pieces)]
    for item in queue[:WINDOW]:
        fetch(*item).start()
    asked = iter(queue[WINDOW:])

    def take(k, piece):
        fetch(k, piece).wait()
        item = next(asked, None)
        if item is not None:
            fetch(*item).start()

    for move in moves:
        move.wait()
    turned[...] = held[...].T
    for side in range(2):
        gate, up, down = weights[3 * side : 3 * side + 3]
        for piece, (begin, size) in enumerate(cuts):
            span = pl.ds(begin, size)
            take(3 * side, piece)
            gate_out = jnp.dot(gate[span, :], turned[...], preferred_element_type=jnp.float32)
            take(3 * side + 1, piece)
            up_out = jnp.dot(up[span, :], turned[...], preferred_element_type=jnp.float32)
            inner[span, :] = (gate_out / (1.0 + jnp.exp(-gate_out)) * up_out).astype(jnp.bfloat16)
        for piece in range(pieces):
            take(3 * side + 2, piece)
        term = jnp.dot(inner[...].T, down[...], preferred_element_type=jnp.float32)
        if side == 0:
            total[...] = term
        else:
            given[...] = (term + total[...]).astype(jnp.bfloat16)
    moves = [
        pltpu.make_async_copy(given.at[pl.ds(k * part, part), :], outputs[k], in_sems.at[k])
        for k in range(blocks)
    ]
    for move in moves:
        move.start()
    for move in moves:
        move.wait()


def ffn(blocks, weights):
    count = len(blocks)
    rows, width = blocks[0].shape
    hidden = weights[0].shape[0]
    cuts = [(0, hidden)]
    if hidden % TILE == 0:
        first = hidden // (2 * TILE) * TILE
        cuts = [(0, first), (first, hidden - first)]
    hbm = pl.BlockSpec(memory_space=pltpu.HBM)
    flops = 2 * count * rows * sum(w.size for w in weights)
    return pl.pallas_call(
        functools.partial(ffn_kernel, count, cuts),
        out_shape=tuple(jax.ShapeDtypeStruct(b.shape, jnp.bfloat16) for b in blocks),
        in_specs=[hbm] * (count + 6),
        out_specs=(hbm,) * count,
        scratch_shapes=[pltpu.VMEM(w.shape, w.dtype) for w in weights]
        + [
            pltpu.VMEM((count * rows, width), jnp.bfloat16),
            pltpu.VMEM((width, count * rows), jnp.bfloat16),
            pltpu.VMEM((hidden, count * rows), jnp.bfloat16),
            pltpu.VMEM((count * rows, width), jnp.float32),
            pltpu.VMEM((count * rows, width), jnp.bfloat16),
            pltpu.SemaphoreType.DMA((count,)),
            pltpu.SemaphoreType.DMA((6 * len(cuts),)),
        ],
        compiler_params=pltpu.CompilerParams(vmem_limit_bytes=36 * MIB),
        cost_estimate=pl.CostEstimate(
            flops=flops,
            transcendentals=0,
            bytes_accessed=2 * sum(w.size for w in weights),
        ),
        name="feed_forward",
    )(*blocks, *(in_hbm(w) for w in weights))


def feed_forward(ring, chunks, weights):
    half = ring.half

    def send(pair, way):
        first, second = hold(*pair)
        return ring.go(first, way), ring.go(second, -way)

    held = [[(chunks[0], chunks[1])], [(chunks[1], chunks[0])]]
    terms = [{}, {}]
    for group in range(2):
        held[group].append(send(held[group][0], 1))
    own = ffn(held[0][0], weights)
    last = own
    for step in range(1, half):
        last, pair = hold(last, held[0][step])
        held[0].append(send(pair, 1))
        if step + 1 < half:
            pair = held[1][step]
            if step == 1:
                last, pair = hold(last, pair)
            held[1].append(send(pair, 1))
        if step == 1:
            own = last
        else:
            terms[0][step - 1], terms[1][step - 1] = last[:2], last[2:]
        last = ffn(held[0][step] + held[1][step], weights)
    last, pair = hold(last, held[0][half])
    terms[0][half - 1], terms[1][half - 1] = last[:2], last[2:]
    terms[0][half] = ffn(pair, weights)

    def add(a, b):
        return (a.astype(jnp.float32) + b.astype(jnp.float32)).astype(jnp.bfloat16)

    home = [None, None]
    order = []
    for step in range(half - 1, 0, -1):
        order += [(1, step), (0, step + 1)]
    order.append((0, 1))
    for group, step in order:
        pair = terms[group][step]
        if home[group] is not None:
            pair = (add(home[group][0], pair[0]), add(home[group][1], pair[1]))
        if group == 0 and step in (half, 1):
            home[1], pair = hold(home[1], pair)
        home[group] = send(pair, -1)
    wide = [[x.astype(jnp.float32) for x in pair] for pair in (own, home[0], home[1])]
    return [wide[0][0] + wide[2][1] + wide[1][0], wide[0][1] + wide[2][0] + wide[1][1]]


def gather_kv(ring, keys, values, weights, extras):
    half = ring.half
    gate, up, down = weights
    both = join(in_hbm(keys), in_hbm(values), ring.go_mate(keys), ring.go_mate(values))
    gate, up, both = lax.optimization_barrier((gate, up, both))
    gate_mate, up_mate = ring.go_mate(gate), ring.go_mate(up)
    held, mates = {0: both}, {}
    reach = 0
    while reach < half:
        fresh = range(reach + 1, min(reach + 2, half) + 1)
        for hops in fresh:
            jump = min(2, hops)
            held[hops] = ring.go_split(held[hops - jump], jump)
        for hops in range(max(1, reach - 1), reach + 1):
            mates[hops] = ring.go_mate(held[hops])
        held, mates, extras = lax.optimization_barrier((held, mates, extras))
        reach = fresh[-1]
    for hops in range(1, half):
        if hops not in mates:
            mates[hops] = ring.go_mate(held[hops])
    gate_mate, up_mate, down, held, mates = lax.optimization_barrier(
        (gate_mate, up_mate, down, held, mates)
    )
    down_mate = ring.go_mate(down)
    blocks = [held[hops] for hops in range(half + 1)] + [mates[hops] for hops in range(1, half)]
    return blocks, (gate_mate, up_mate, down_mate), extras


def block_owners(ring):
    half = ring.half
    owners = [ring.owners([(-hops, hops)]) for hops in range(half + 1)]
    owners += [ring.owners([(hops, -hops)], True) for hops in range(1, half)]
    return np.concatenate(owners, axis=1)


def on_device(
    ring,
    hidden_in,
    queries,
    keys,
    values,
    out_weight,
    norm_gain,
    gate_weight,
    up_weight,
    down_weight,
    pair_ids,
    roles,
    send_rows,
    send_counts,
):
    my_index = lax.axis_index("ctx")
    tok_rows = hidden_in.shape[0]
    own = (gate_weight.T, up_weight.T, down_weight)
    owners = jnp.asarray(block_owners(ring))[my_index]
    pairs = pair_ids.reshape(-1, tok_rows)
    parts = roles.reshape(-1, tok_rows)
    my_roles = lax.dynamic_slice_in_dim(roles, my_index * tok_rows, tok_rows)
    live = (my_roles != 0).astype(jnp.float32)
    blocks, mates, extras = gather_kv(ring, keys, values, own, (owners, live))
    owners, live = extras
    residual, chunks = attend(
        owners, queries, pairs, parts, hidden_in, norm_gain, out_weight, blocks
    )
    summed = feed_forward(ring, chunks, own + mates)
    ffn_back = jnp.concatenate(summed, axis=0).astype(jnp.bfloat16).astype(jnp.float32)
    return (residual.astype(jnp.float32) + ffn_back * live[:, None]).astype(jnp.bfloat16)


def solution(mesh):
    ring = Ring(mesh.shape["groups"], mesh.shape["ctx"])

    def run(*arrays):
        return on_device(ring, *arrays)

    return jax.shard_map(
        run,
        mesh=mesh,
        in_specs=(
            P(("groups", "ctx"), None),
            P(("groups", "ctx"), None),
            P(("groups", "ctx"), None),
            P(("groups", "ctx"), None),
            P(),
            P(),
            P(None, "ctx"),
            P(None, "ctx"),
            P("ctx", None),
            P("groups"),
            P("groups"),
            P(("groups", "ctx"), None),
            P("groups", None),
        ),
        out_specs=P(("groups", "ctx"), None),
        check_vma=False,
    )
```

```python
import functools
import math

import jax
import jax.numpy as jnp
import numpy as np
from jax import lax
from jax.experimental import pallas as pl
from jax.experimental.pallas import tpu as pltpu
from jax.sharding import PartitionSpec as P

NEG_FILL = -1e30
CORES = 2
PLANE = 4
CHUNKS = 2
MIB = 1 << 20


def in_hbm(x):
    return pltpu.with_memory_space_constraint(x, pltpu.HBM)


def hold(first, then):
    return lax.optimization_barrier((first, then))


class Ring:
    def __init__(self, groups, devices):
        chips = devices // CORES
        columns = max(1, PLANE // groups)
        if chips % columns:
            columns = 1
        depth = chips // columns
        order = []
        for column in range(columns):
            line = [level * columns + column for level in range(depth)]
            order += line if column % 2 == 0 else line[::-1]
        self.chips = chips
        self.half = chips // 2
        self.order = order
        self.swap = [(i, i ^ 1) for i in range(devices)]

    def go(self, block, hops):
        pairs = []
        for place in range(self.chips):
            here, there = self.order[place], self.order[(place + hops) % self.chips]
            pairs += [(here * CORES + core, there * CORES + core) for core in range(CORES)]
        return lax.ppermute(block, "ctx", pairs)

    def go_mate(self, block):
        return lax.ppermute(block, "ctx", self.swap)

    def go_split(self, block, hops):
        pairs = []
        for place in range(self.chips):
            for core, way in ((0, hops), (1, -hops)):
                here, there = self.order[place], self.order[(place + way) % self.chips]
                pairs.append((here * CORES + core, there * CORES + core))
        return lax.ppermute(block, "ctx", pairs)

    def owners(self, spots, swapped=False):
        place_of = {chip: place for place, chip in enumerate(self.order)}
        table = []
        for device in range(self.chips * CORES):
            chip, core = divmod(device, CORES)
            row = []
            for spot in spots:
                first = self.order[(place_of[chip] + spot[core]) % self.chips] * CORES + core
                row += [first ^ 1, first] if swapped else [first, first ^ 1]
            table.append(row)
        return np.asarray(table, np.int32)


def attention_kernel(
    count,
    pieces,
    heads,
    head_dim,
    owner_ref,
    pair_smem,
    role_smem,
    *refs,
):
    inputs, blocks_hbm, refs = refs[:6], refs[6 : 6 + pieces], refs[6 + pieces :]
    outputs, refs = refs[: CHUNKS + 1], refs[CHUNKS + 1 :]
    locals_, refs = refs[:6], refs[6:]
    (given, kept, blocks, stacked, scores, top, total, summed, sems) = refs
    fetches = [
        pltpu.make_async_copy(inputs[k], locals_[k], sems.at[pieces + k]) for k in range(6)
    ]
    arrivals, begin = [], 0
    for j in range(pieces):
        size = blocks_hbm[j].shape[0]
        arrivals.append(
            pltpu.make_async_copy(blocks_hbm[j], blocks.at[pl.ds(begin, size), :], sems.at[j])
        )
        begin += size
    for k in range(3):
        fetches[k].start()
    for arrival in arrivals:
        arrival.start()
    query_ref, pair_ref, role_ref, hidden_ref, gain_ref, weight_ref = locals_
    rows = query_ref.shape[0]
    for k in range(3):
        fetches[k].wait()
    for arrival in arrivals:
        arrival.wait()
    for k in range(3, 6):
        fetches[k].start()
    me = owner_ref[0]
    for head in range(heads):
        stacked[pl.ds(head * rows, rows), :] = query_ref[:, head * head_dim : (head + 1) * head_dim]

    def column(ref):
        return jnp.broadcast_to(ref[pl.ds(me, 1), :], (rows, rows)).T

    query_pair, query_role = column(pair_ref), column(role_ref)
    query_pos = me * rows + lax.broadcasted_iota(jnp.int32, (rows, rows), 0)
    key_off = lax.broadcasted_iota(jnp.int32, (rows, rows), 1)

    def needed(owner):
        first_pair, last_pair = pair_smem[owner, 0], pair_smem[owner, rows - 1]
        first_role, last_role = role_smem[owner, 0], role_smem[owner, rows - 1]
        my_first, my_last = pair_smem[me, 0], pair_smem[me, rows - 1]
        my_role = role_smem[me, 0]
        apart = (
            (first_pair == last_pair)
            & (my_first == my_last)
            & (first_role == last_role)
            & (my_role == role_smem[me, rows - 1])
            & (first_role != 0)
            & (first_role != my_role)
        )
        return (owner <= me) & (last_pair >= my_first) & jnp.logical_not(apart)

    top[...] = jnp.full_like(top, NEG_FILL)
    total[...] = jnp.zeros_like(total)
    summed[...] = jnp.zeros_like(summed)
    for j in range(count):
        owner = owner_ref[j]

        @pl.when(needed(owner))
        def _():
            seen = (
                (query_pair == pair_ref[pl.ds(owner, 1), :])
                & (owner * rows + key_off <= query_pos)
                & (
                    (role_ref[pl.ds(owner, 1), :] == 0)
                    | (role_ref[pl.ds(owner, 1), :] == query_role)
                )
            )
            bias = jnp.where(seen, 0.0, NEG_FILL)
            raw = lax.dot_general(
                stacked[...],
                blocks[pl.ds(2 * j * rows, rows), :],
                (((1,), (1,)), ((), ())),
                preferred_element_type=jnp.float32,
            )
            masked = raw.reshape(heads, rows, rows) + bias[None]
            scores[j] = masked
            top[...] = jnp.maximum(top[...], masked)

    top[...] = jnp.broadcast_to(jnp.max(top[...], axis=-1, keepdims=True), top.shape)
    factor = math.log2(math.e) / math.sqrt(head_dim)
    for j in range(count):
        owner = owner_ref[j]

        @pl.when(needed(owner))
        def _():
            weights = jnp.exp2((scores[j] - top[...]) * factor)
            total[...] += weights
            summed[...] += jnp.dot(
                weights.astype(jnp.bfloat16).reshape(heads * rows, rows),
                blocks[pl.ds((2 * j + 1) * rows, rows), :],
                preferred_element_type=jnp.float32,
            ).reshape(heads, rows, head_dim)

    mixed = (summed[...] / jnp.sum(total[...], axis=-1, keepdims=True)).astype(jnp.bfloat16)
    mixed = jnp.concatenate([mixed[head] for head in range(heads)], axis=1)
    for k in range(3, 6):
        fetches[k].wait()
    projected = jnp.dot(mixed, weight_ref[...], preferred_element_type=jnp.float32)
    residual = (hidden_ref[...].astype(jnp.float32) + projected).astype(jnp.bfloat16)
    wide = residual.astype(jnp.float32)
    mean_sq = jnp.mean(wide * wide, axis=-1, keepdims=True)
    given[...] = (wide * lax.rsqrt(mean_sq + 1e-06) * gain_ref[...]).astype(jnp.bfloat16)
    kept[...] = residual
    part = rows // CHUNKS
    moves = [
        pltpu.make_async_copy(given.at[pl.ds(k * part, part), :], outputs[k], sems.at[k])
        for k in range(CHUNKS)
    ]
    moves.append(pltpu.make_async_copy(kept, outputs[CHUNKS], sems.at[CHUNKS]))
    for move in moves:
        move.start()
    for move in moves:
        move.wait()


def attend(owners, queries, pairs, parts, hidden, gain, out_weight, blocks):
    rows, width = queries.shape
    head_dim = blocks[0].shape[1]
    heads = width // head_dim
    count = owners.shape[0]
    total_rows = sum(b.shape[0] for b in blocks)
    smem = pl.BlockSpec(memory_space=pltpu.SMEM)
    hbm = pl.BlockSpec(memory_space=pltpu.HBM)
    square = pltpu.VMEM((heads, rows, rows), jnp.float32)
    chunk = jax.ShapeDtypeStruct((rows // CHUNKS, hidden.shape[1]), jnp.bfloat16)
    inputs = (queries, pairs, parts, hidden, gain.reshape(1, -1), out_weight)
    tall = heads * rows * rows * jnp.dtype(jnp.float32).itemsize
    need = (count + 3) * tall + sum(x.size * x.dtype.itemsize for x in inputs + blocks + (hidden,) * 2)
    *chunks, residual = pl.pallas_call(
        functools.partial(attention_kernel, count, len(blocks), heads, head_dim),
        out_shape=(chunk,) * CHUNKS + (jax.ShapeDtypeStruct(hidden.shape, jnp.bfloat16),),
        in_specs=[smem] * 3 + [hbm] * (len(inputs) + len(blocks)),
        out_specs=(hbm,) * (CHUNKS + 1),
        scratch_shapes=[pltpu.VMEM(x.shape, x.dtype) for x in inputs]
        + [
            pltpu.VMEM(hidden.shape, jnp.bfloat16),
            pltpu.VMEM(hidden.shape, jnp.bfloat16),
            pltpu.VMEM((total_rows, head_dim), jnp.bfloat16),
            pltpu.VMEM((heads * rows, head_dim), jnp.bfloat16),
            pltpu.VMEM((count, heads, rows, rows), jnp.float32),
            square,
            square,
            pltpu.VMEM((heads, rows, head_dim), jnp.float32),
            pltpu.SemaphoreType.DMA((len(blocks) + len(inputs),)),
        ],
        compiler_params=pltpu.CompilerParams(vmem_limit_bytes=need + 6 * MIB),
        name="attention",
    )(owners, pairs, parts, *(in_hbm(x) for x in inputs), *blocks)
    return residual, chunks


def load_kernel(count, *refs):
    inputs, outputs, sems = refs[:count], refs[count : 2 * count], refs[2 * count]
    moves = [pltpu.make_async_copy(inputs[k], outputs[k], sems.at[k]) for k in range(count)]
    for move in moves:
        move.start()
    for move in moves:
        move.wait()


def load(*arrays):
    count = len(arrays)
    return pl.pallas_call(
        functools.partial(load_kernel, count),
        out_shape=tuple(pltpu.VMEM(x.shape, x.dtype) for x in arrays),
        in_specs=[pl.BlockSpec(memory_space=pl.ANY)] * count,
        out_specs=(pl.BlockSpec(memory_space=pltpu.VMEM),) * count,
        scratch_shapes=[pltpu.SemaphoreType.DMA((count,))],
        compiler_params=pltpu.CompilerParams(vmem_limit_bytes=2 * MIB),
        name="load",
    )(*arrays)


def join_kernel(count, *refs):
    inputs, both_ref, sems = refs[:count], refs[count], refs[count + 1]
    rows = inputs[0].shape[0]
    moves = [
        pltpu.make_async_copy(inputs[k], both_ref.at[pl.ds(k * rows, rows), :], sems.at[k])
        for k in range(count)
    ]
    for move in moves:
        move.start()
    for move in moves:
        move.wait()


def join(*parts):
    count = len(parts)
    rows, width = parts[0].shape
    return pl.pallas_call(
        functools.partial(join_kernel, count),
        out_shape=jax.ShapeDtypeStruct((count * rows, width), parts[0].dtype),
        in_specs=[pl.BlockSpec(memory_space=pl.ANY)] * count,
        out_specs=pl.BlockSpec(memory_space=pltpu.VMEM),
        scratch_shapes=[pltpu.SemaphoreType.DMA((count,))],
        name="join",
    )(*parts)


def ffn_kernel(blocks, *refs):
    inputs, refs = refs[:blocks], refs[blocks:]
    weights, refs = refs[:6], refs[6:]
    outputs, refs = refs[:blocks], refs[blocks:]
    held, turned, inner, total, given, sems = refs
    part = held.shape[0] // blocks
    moves = [
        pltpu.make_async_copy(inputs[k], held.at[pl.ds(k * part, part), :], sems.at[k])
        for k in range(blocks)
    ]
    for move in moves:
        move.start()
    for move in moves:
        move.wait()
    turned[...] = held[...].T
    for side in range(2):
        gate, up, down = weights[3 * side : 3 * side + 3]
        gate_out = jnp.dot(gate[...], turned[...], preferred_element_type=jnp.float32)
        up_out = jnp.dot(up[...], turned[...], preferred_element_type=jnp.float32)
        inner[...] = (gate_out / (1.0 + jnp.exp(-gate_out)) * up_out).astype(jnp.bfloat16)
        term = jnp.dot(inner[...].T, down[...], preferred_element_type=jnp.float32)
        if side == 0:
            total[...] = term
        else:
            given[...] = (term + total[...]).astype(jnp.bfloat16)
    moves = [
        pltpu.make_async_copy(given.at[pl.ds(k * part, part), :], outputs[k], sems.at[k])
        for k in range(blocks)
    ]
    for move in moves:
        move.start()
    for move in moves:
        move.wait()


def ffn(blocks, weights):
    count = len(blocks)
    rows, width = blocks[0].shape
    hidden = weights[0].shape[0]
    hbm = pl.BlockSpec(memory_space=pl.ANY)
    return pl.pallas_call(
        functools.partial(ffn_kernel, count),
        out_shape=tuple(jax.ShapeDtypeStruct(b.shape, jnp.bfloat16) for b in blocks),
        in_specs=[hbm] * count + [pl.BlockSpec(memory_space=pltpu.VMEM)] * 6,
        out_specs=(hbm,) * count,
        scratch_shapes=[
            pltpu.VMEM((count * rows, width), jnp.bfloat16),
            pltpu.VMEM((width, count * rows), jnp.bfloat16),
            pltpu.VMEM((hidden, count * rows), jnp.bfloat16),
            pltpu.VMEM((count * rows, width), jnp.float32),
            pltpu.VMEM((count * rows, width), jnp.bfloat16),
            pltpu.SemaphoreType.DMA((count,)),
        ],
        compiler_params=pltpu.CompilerParams(vmem_limit_bytes=16 * MIB),
        cost_estimate=pl.CostEstimate(flops=1000, transcendentals=0, bytes_accessed=1000),
        name="feed_forward",
    )(*blocks, *(pltpu.with_memory_space_constraint(w, pltpu.VMEM) for w in weights))


def feed_forward(ring, chunks, weights):
    half = ring.half

    def send(pair, way):
        first, second = hold(*pair)
        return ring.go(first, way), ring.go(second, -way)

    held = [[(chunks[0], chunks[1])], [(chunks[1], chunks[0])]]
    terms = [{}, {}]
    for group in range(2):
        held[group].append(send(held[group][0], 1))
    own = ffn(held[0][0], weights)
    last = own
    for step in range(1, half):
        last, pair = hold(last, held[0][step])
        held[0].append(send(pair, 1))
        if step + 1 < half:
            pair = held[1][step]
            if step == 1:
                last, pair = hold(last, pair)
            held[1].append(send(pair, 1))
        if step == 1:
            own = last
        else:
            terms[0][step - 1], terms[1][step - 1] = last[:2], last[2:]
        last = ffn(held[0][step] + held[1][step], weights)
    last, pair = hold(last, held[0][half])
    terms[0][half - 1], terms[1][half - 1] = last[:2], last[2:]
    terms[0][half] = ffn(pair, weights)

    def add(a, b):
        return (a.astype(jnp.float32) + b.astype(jnp.float32)).astype(jnp.bfloat16)

    home = [None, None]
    order = []
    for step in range(half - 1, 0, -1):
        order += [(1, step), (0, step + 1)]
    order.append((0, 1))
    for group, step in order:
        pair = terms[group][step]
        if home[group] is not None:
            pair = (add(home[group][0], pair[0]), add(home[group][1], pair[1]))
        if group == 0 and step in (half, 1):
            home[1], pair = hold(home[1], pair)
        home[group] = send(pair, -1)
    wide = [[x.astype(jnp.float32) for x in pair] for pair in (own, home[0], home[1])]
    return [wide[0][0] + wide[2][1] + wide[1][0], wide[0][1] + wide[2][0] + wide[1][1]]


def gather_kv(ring, keys, values, weights, extras):
    half = ring.half
    gate, up, down = weights
    both = join(in_hbm(keys), in_hbm(values), ring.go_mate(keys), ring.go_mate(values))
    gate, up, both = lax.optimization_barrier((gate, up, both))
    gate_mate, up_mate = ring.go_mate(gate), ring.go_mate(up)
    resident = load(*(in_hbm(w) for w in weights))
    held, mates = {0: both}, {}
    reach = 0
    while reach < half:
        fresh = range(reach + 1, min(reach + 2, half) + 1)
        for hops in fresh:
            jump = min(2, hops)
            held[hops] = ring.go_split(held[hops - jump], jump)
        for hops in range(max(1, reach - 1), reach + 1):
            mates[hops] = ring.go_mate(held[hops])
        held, mates, extras, resident = lax.optimization_barrier((held, mates, extras, resident))
        reach = fresh[-1]
    for hops in range(1, half):
        if hops not in mates:
            mates[hops] = ring.go_mate(held[hops])
    gate_mate, up_mate, down, held, mates = lax.optimization_barrier(
        (gate_mate, up_mate, down, held, mates)
    )
    down_mate = ring.go_mate(down)
    resident += load(gate_mate, up_mate)
    blocks = tuple(held[hops] for hops in range(half + 1))
    blocks += tuple(mates[hops] for hops in range(1, half))
    return blocks, resident, down_mate, extras


def block_owners(ring):
    half = ring.half
    owners = [ring.owners([(-hops, hops)]) for hops in range(half + 1)]
    owners += [ring.owners([(hops, -hops)], True) for hops in range(1, half)]
    return np.concatenate(owners, axis=1)


def on_device(
    ring,
    hidden_in,
    queries,
    keys,
    values,
    out_weight,
    norm_gain,
    gate_weight,
    up_weight,
    down_weight,
    pair_ids,
    roles,
    send_rows,
    send_counts,
):
    my_index = lax.axis_index("ctx")
    tok_rows = hidden_in.shape[0]
    own = (gate_weight.T, up_weight.T, down_weight)
    owners = jnp.asarray(block_owners(ring))[my_index]
    pairs = pair_ids.reshape(-1, tok_rows)
    parts = roles.reshape(-1, tok_rows)
    my_roles = lax.dynamic_slice_in_dim(roles, my_index * tok_rows, tok_rows)
    live = (my_roles != 0).astype(jnp.float32)
    blocks, resident, down_mate, extras = gather_kv(ring, keys, values, own, (owners, live))
    owners, live = extras
    residual, chunks = attend(
        owners, queries, pairs, parts, hidden_in, norm_gain, out_weight, blocks
    )
    summed = feed_forward(ring, chunks, resident + load(down_mate))
    ffn_back = jnp.concatenate(summed, axis=0).astype(jnp.bfloat16).astype(jnp.float32)
    return (residual.astype(jnp.float32) + ffn_back * live[:, None]).astype(jnp.bfloat16)


def solution(mesh):
    ring = Ring(mesh.shape["groups"], mesh.shape["ctx"])

    def run(*arrays):
        return on_device(ring, *arrays)

    return jax.shard_map(
        run,
        mesh=mesh,
        in_specs=(
            P(("groups", "ctx"), None),
            P(("groups", "ctx"), None),
            P(("groups", "ctx"), None),
            P(("groups", "ctx"), None),
            P(),
            P(),
            P(None, "ctx"),
            P(None, "ctx"),
            P("ctx", None),
            P("groups"),
            P("groups"),
            P(("groups", "ctx"), None),
            P("groups", None),
        ),
        out_specs=P(("groups", "ctx"), None),
        check_vma=False,
    )
```

```python
import functools
import math

import jax
import jax.numpy as jnp
import numpy as np
from jax import lax
from jax.experimental import pallas as pl
from jax.experimental.pallas import tpu as pltpu
from jax.sharding import PartitionSpec as P

NEG_FILL = -1e30
CORES = 2
PLANE = 4
MIB = 1 << 20


def in_hbm(x):
    return pltpu.with_memory_space_constraint(x, pltpu.HBM)


def hold(first, then):
    return lax.optimization_barrier((first, then))


class Ring:
    def __init__(self, groups, devices):
        chips = devices // CORES
        columns = max(1, PLANE // groups)
        if chips % columns:
            columns = 1
        depth = chips // columns
        order = []
        for column in range(columns):
            line = [level * columns + column for level in range(depth)]
            order += line if column % 2 == 0 else line[::-1]
        self.chips = chips
        self.half = chips // 2
        self.order = order
        self.swap = [(i, i ^ 1) for i in range(devices)]

    def go(self, block, hops):
        pairs = []
        for place in range(self.chips):
            here, there = self.order[place], self.order[(place + hops) % self.chips]
            pairs += [(here * CORES + core, there * CORES + core) for core in range(CORES)]
        return lax.ppermute(block, "ctx", pairs)

    def go_mate(self, block):
        return lax.ppermute(block, "ctx", self.swap)

    def go_split(self, block, hops):
        pairs = []
        for place in range(self.chips):
            for core, way in ((0, hops), (1, -hops)):
                here, there = self.order[place], self.order[(place + way) % self.chips]
                pairs.append((here * CORES + core, there * CORES + core))
        return lax.ppermute(block, "ctx", pairs)

    def owners(self, spots, swapped=False):
        place_of = {chip: place for place, chip in enumerate(self.order)}
        table = []
        for device in range(self.chips * CORES):
            chip, core = divmod(device, CORES)
            row = []
            for spot in spots:
                first = self.order[(place_of[chip] + spot[core]) % self.chips] * CORES + core
                row += [first ^ 1, first] if swapped else [first, first ^ 1]
            table.append(row)
        return np.asarray(table, np.int32)


def attention_kernel(
    count,
    pieces,
    heads,
    head_dim,
    owner_ref,
    pair_smem,
    role_smem,
    *refs,
):
    inputs, blocks_hbm, refs = refs[:6], refs[6 : 6 + pieces], refs[6 + pieces :]
    outputs, refs = refs[:2], refs[2:]
    locals_, refs = refs[:6], refs[6:]
    (given, kept, blocks, stacked, scores, top, total, summed, sems) = refs
    fetches = [
        pltpu.make_async_copy(inputs[k], locals_[k], sems.at[pieces + k]) for k in range(6)
    ]
    arrivals, begin = [], 0
    for j in range(pieces):
        size = blocks_hbm[j].shape[0]
        arrivals.append(
            pltpu.make_async_copy(blocks_hbm[j], blocks.at[pl.ds(begin, size), :], sems.at[j])
        )
        begin += size
    for k in range(3):
        fetches[k].start()
    for arrival in arrivals:
        arrival.start()
    query_ref, pair_ref, role_ref, hidden_ref, gain_ref, weight_ref = locals_
    rows = query_ref.shape[0]
    for k in range(3):
        fetches[k].wait()
    for arrival in arrivals:
        arrival.wait()
    for k in range(3, 6):
        fetches[k].start()
    me = owner_ref[0]
    for head in range(heads):
        stacked[pl.ds(head * rows, rows), :] = query_ref[:, head * head_dim : (head + 1) * head_dim]

    def column(ref):
        return jnp.broadcast_to(ref[pl.ds(me, 1), :], (rows, rows)).T

    query_pair, query_role = column(pair_ref), column(role_ref)
    query_pos = me * rows + lax.broadcasted_iota(jnp.int32, (rows, rows), 0)
    key_off = lax.broadcasted_iota(jnp.int32, (rows, rows), 1)

    def needed(owner):
        first_pair, last_pair = pair_smem[owner, 0], pair_smem[owner, rows - 1]
        first_role, last_role = role_smem[owner, 0], role_smem[owner, rows - 1]
        my_first, my_last = pair_smem[me, 0], pair_smem[me, rows - 1]
        my_role = role_smem[me, 0]
        apart = (
            (first_pair == last_pair)
            & (my_first == my_last)
            & (first_role == last_role)
            & (my_role == role_smem[me, rows - 1])
            & (first_role != 0)
            & (first_role != my_role)
        )
        return (owner <= me) & (last_pair >= my_first) & jnp.logical_not(apart)

    top[...] = jnp.full_like(top, NEG_FILL)
    total[...] = jnp.zeros_like(total)
    summed[...] = jnp.zeros_like(summed)
    for j in range(count):
        owner = owner_ref[j]

        @pl.when(needed(owner))
        def _():
            seen = (
                (query_pair == pair_ref[pl.ds(owner, 1), :])
                & (owner * rows + key_off <= query_pos)
                & (
                    (role_ref[pl.ds(owner, 1), :] == 0)
                    | (role_ref[pl.ds(owner, 1), :] == query_role)
                )
            )
            bias = jnp.where(seen, 0.0, NEG_FILL)
            raw = lax.dot_general(
                stacked[...],
                blocks[pl.ds(2 * j * rows, rows), :],
                (((1,), (1,)), ((), ())),
                preferred_element_type=jnp.float32,
            )
            masked = raw.reshape(heads, rows, rows) + bias[None]
            scores[j] = masked
            top[...] = jnp.maximum(top[...], masked)

    top[...] = jnp.broadcast_to(jnp.max(top[...], axis=-1, keepdims=True), top.shape)
    factor = math.log2(math.e) / math.sqrt(head_dim)
    for j in range(count):
        owner = owner_ref[j]

        @pl.when(needed(owner))
        def _():
            weights = jnp.exp2((scores[j] - top[...]) * factor)
            total[...] += weights
            summed[...] += jnp.dot(
                weights.astype(jnp.bfloat16).reshape(heads * rows, rows),
                blocks[pl.ds((2 * j + 1) * rows, rows), :],
                preferred_element_type=jnp.float32,
            ).reshape(heads, rows, head_dim)

    mixed = (summed[...] / jnp.sum(total[...], axis=-1, keepdims=True)).astype(jnp.bfloat16)
    mixed = jnp.concatenate([mixed[head] for head in range(heads)], axis=1)
    for k in range(3, 6):
        fetches[k].wait()
    projected = jnp.dot(mixed, weight_ref[...], preferred_element_type=jnp.float32)
    residual = (hidden_ref[...].astype(jnp.float32) + projected).astype(jnp.bfloat16)
    wide = residual.astype(jnp.float32)
    mean_sq = jnp.mean(wide * wide, axis=-1, keepdims=True)
    given[...] = (wide * lax.rsqrt(mean_sq + 1e-06) * gain_ref[...]).astype(jnp.bfloat16)
    kept[...] = residual
    moves = [
        pltpu.make_async_copy(given, outputs[0], sems.at[0]),
        pltpu.make_async_copy(kept, outputs[1], sems.at[1]),
    ]
    for move in moves:
        move.start()
    for move in moves:
        move.wait()


def attend(owners, queries, pairs, parts, hidden, gain, out_weight, blocks):
    rows, width = queries.shape
    head_dim = blocks[0].shape[1]
    heads = width // head_dim
    count = owners.shape[0]
    total_rows = sum(b.shape[0] for b in blocks)
    smem = pl.BlockSpec(memory_space=pltpu.SMEM)
    hbm = pl.BlockSpec(memory_space=pltpu.HBM)
    square = pltpu.VMEM((heads, rows, rows), jnp.float32)
    like_hidden = jax.ShapeDtypeStruct(hidden.shape, jnp.bfloat16)
    inputs = (queries, pairs, parts, hidden, gain.reshape(1, -1), out_weight)
    tall = heads * rows * rows * jnp.dtype(jnp.float32).itemsize
    need = (count + 3) * tall + sum(x.size * x.dtype.itemsize for x in inputs + blocks + (hidden,) * 2)
    return pl.pallas_call(
        functools.partial(attention_kernel, count, len(blocks), heads, head_dim),
        out_shape=(like_hidden, like_hidden),
        in_specs=[smem] * 3 + [hbm] * (len(inputs) + len(blocks)),
        out_specs=(hbm, hbm),
        scratch_shapes=[pltpu.VMEM(x.shape, x.dtype) for x in inputs]
        + [
            pltpu.VMEM(hidden.shape, jnp.bfloat16),
            pltpu.VMEM(hidden.shape, jnp.bfloat16),
            pltpu.VMEM((total_rows, head_dim), jnp.bfloat16),
            pltpu.VMEM((heads * rows, head_dim), jnp.bfloat16),
            pltpu.VMEM((count, heads, rows, rows), jnp.float32),
            square,
            square,
            pltpu.VMEM((heads, rows, head_dim), jnp.float32),
            pltpu.SemaphoreType.DMA((len(blocks) + len(inputs),)),
        ],
        compiler_params=pltpu.CompilerParams(vmem_limit_bytes=need + 6 * MIB),
        name="attention",
    )(owners, pairs, parts, *(in_hbm(x) for x in inputs), *blocks)


def load_kernel(count, *refs):
    inputs, outputs, sems = refs[:count], refs[count : 2 * count], refs[2 * count]
    moves = [pltpu.make_async_copy(inputs[k], outputs[k], sems.at[k]) for k in range(count)]
    for move in moves:
        move.start()
    for move in moves:
        move.wait()


def load(*arrays):
    count = len(arrays)
    return pl.pallas_call(
        functools.partial(load_kernel, count),
        out_shape=tuple(pltpu.VMEM(x.shape, x.dtype) for x in arrays),
        in_specs=[pl.BlockSpec(memory_space=pl.ANY)] * count,
        out_specs=(pl.BlockSpec(memory_space=pltpu.VMEM),) * count,
        scratch_shapes=[pltpu.SemaphoreType.DMA((count,))],
        compiler_params=pltpu.CompilerParams(vmem_limit_bytes=2 * MIB),
        name="load",
    )(*arrays)


def join_kernel(count, *refs):
    inputs, both_ref, sems = refs[:count], refs[count], refs[count + 1]
    rows = inputs[0].shape[0]
    moves = [
        pltpu.make_async_copy(inputs[k], both_ref.at[pl.ds(k * rows, rows), :], sems.at[k])
        for k in range(count)
    ]
    for move in moves:
        move.start()
    for move in moves:
        move.wait()


def join(*parts):
    count = len(parts)
    rows, width = parts[0].shape
    return pl.pallas_call(
        functools.partial(join_kernel, count),
        out_shape=jax.ShapeDtypeStruct((count * rows, width), parts[0].dtype),
        in_specs=[pl.BlockSpec(memory_space=pl.ANY)] * (count // CORES)
        + [pl.BlockSpec(memory_space=pltpu.VMEM)] * (count - count // CORES),
        out_specs=pl.BlockSpec(memory_space=pltpu.VMEM),
        scratch_shapes=[pltpu.SemaphoreType.DMA((count,))],
        name="join",
    )(*parts)


def ffn_kernel(blocks, *refs):
    inputs, refs = refs[:blocks], refs[blocks:]
    weights, refs = refs[:6], refs[6:]
    outputs, refs = refs[:blocks], refs[blocks:]
    held, turned, inner, total, given, sems = refs
    part = held.shape[0] // blocks
    moves = [
        pltpu.make_async_copy(inputs[k], held.at[pl.ds(k * part, part), :], sems.at[k])
        for k in range(blocks)
    ]
    for move in moves:
        move.start()
    for move in moves:
        move.wait()
    turned[...] = held[...].T
    for side in range(2):
        gate, up, down = weights[3 * side : 3 * side + 3]
        gate_out = jnp.dot(gate[...], turned[...], preferred_element_type=jnp.float32)
        up_out = jnp.dot(up[...], turned[...], preferred_element_type=jnp.float32)
        inner[...] = (gate_out / (1.0 + jnp.exp(-gate_out)) * up_out).astype(jnp.bfloat16)
        term = jnp.dot(inner[...].T, down[...], preferred_element_type=jnp.float32)
        if side == 0:
            total[...] = term
        else:
            given[...] = (term + total[...]).astype(jnp.bfloat16)
    moves = [
        pltpu.make_async_copy(given.at[pl.ds(k * part, part), :], outputs[k], sems.at[k])
        for k in range(blocks)
    ]
    for move in moves:
        move.start()
    for move in moves:
        move.wait()


def ffn(blocks, weights):
    count = len(blocks)
    rows, width = blocks[0].shape
    hidden = weights[0].shape[0]
    hbm = pl.BlockSpec(memory_space=pl.ANY)
    return pl.pallas_call(
        functools.partial(ffn_kernel, count),
        out_shape=tuple(jax.ShapeDtypeStruct(b.shape, jnp.bfloat16) for b in blocks),
        in_specs=[hbm] * count + [pl.BlockSpec(memory_space=pltpu.VMEM)] * 6,
        out_specs=(hbm,) * count,
        scratch_shapes=[
            pltpu.VMEM((count * rows, width), jnp.bfloat16),
            pltpu.VMEM((width, count * rows), jnp.bfloat16),
            pltpu.VMEM((hidden, count * rows), jnp.bfloat16),
            pltpu.VMEM((count * rows, width), jnp.float32),
            pltpu.VMEM((count * rows, width), jnp.bfloat16),
            pltpu.SemaphoreType.DMA((count,)),
        ],
        compiler_params=pltpu.CompilerParams(vmem_limit_bytes=16 * MIB),
        cost_estimate=pl.CostEstimate(flops=1000, transcendentals=0, bytes_accessed=1000),
        name="feed_forward",
    )(*blocks, *(pltpu.with_memory_space_constraint(w, pltpu.VMEM) for w in weights))


def feed_forward(ring, normed, weights):
    half = ring.half
    ways = (1, -1)
    held = [[normed, ring.go_split(normed, ways[group])] for group in range(2)]
    terms = [{}, {}]
    last = None
    for step in range(1, half):
        blocks = [held[0][step], held[1][step]]
        if last is not None:
            last, blocks[0] = hold(last, blocks[0])
            terms[0][step - 1], terms[1][step - 1] = last
        if step + 1 == half:
            blocks = list(hold(*blocks))
        held[0].append(ring.go_split(blocks[0], ways[0]))
        if step + 1 < half:
            held[1].append(ring.go_split(blocks[1], ways[1]))
        last = ffn(blocks, weights)
    last, far = hold(last, held[0][half])
    if half > 1:
        terms[0][half - 1], terms[1][half - 1] = last
    (terms[0][half],) = ffn([far], weights)

    order = []
    for step in range(half - 1, 0, -1):
        order += [(1, step), (0, step + 1)]
    order.append((0, 1))
    home = [None, None]
    own = None
    for group, step in order:
        term = terms[group][step]
        if home[group] is not None:
            if group == 0 and own is None:
                home[0], first = hold(home[0], normed)
                (own,) = ffn([first], weights)
            term = (home[group].astype(jnp.float32) + term.astype(jnp.float32)).astype(jnp.bfloat16)
        if group == 0 and step in (half, 2) and half > 2:
            home[1], term = hold(home[1], term)
        home[group] = ring.go_split(term, -ways[group])
    if own is None:
        (own,) = ffn([normed], weights)
    return sum(x.astype(jnp.float32) for x in (own, home[1], home[0]) if x is not None)


def gather_kv(ring, keys, values, weights, extras):
    half = ring.half
    gate, up, down = weights
    both = join(in_hbm(keys), in_hbm(values), ring.go_mate(keys), ring.go_mate(values))
    gate, up, both = lax.optimization_barrier((gate, up, both))
    gate_mate, up_mate = ring.go_mate(gate), ring.go_mate(up)
    held, mates = {0: both}, {}
    reach = 0
    while reach < half:
        fresh = range(reach + 1, min(reach + 2, half) + 1)
        for hops in fresh:
            jump = min(2, hops)
            held[hops] = ring.go_split(held[hops - jump], jump)
        for hops in range(max(1, reach - 1), reach + 1):
            mates[hops] = ring.go_mate(held[hops])
        held, mates, extras = lax.optimization_barrier((held, mates, extras))
        reach = fresh[-1]
    for hops in range(1, half):
        if hops not in mates:
            mates[hops] = ring.go_mate(held[hops])
    gate_mate, up_mate, down, held, mates = lax.optimization_barrier(
        (gate_mate, up_mate, down, held, mates)
    )
    down_mate = ring.go_mate(down)
    blocks = tuple(held[hops] for hops in range(half + 1))
    blocks += tuple(mates[hops] for hops in range(1, half))
    return blocks, (gate_mate, up_mate, down_mate), extras


def block_owners(ring):
    half = ring.half
    owners = [ring.owners([(-hops, hops)]) for hops in range(half + 1)]
    owners += [ring.owners([(hops, -hops)], True) for hops in range(1, half)]
    return np.concatenate(owners, axis=1)


def on_device(
    ring,
    hidden_in,
    queries,
    keys,
    values,
    out_weight,
    norm_gain,
    gate_weight,
    up_weight,
    down_weight,
    pair_ids,
    roles,
    send_rows,
    send_counts,
):
    my_index = lax.axis_index("ctx")
    tok_rows = hidden_in.shape[0]
    own = (gate_weight.T, up_weight.T, down_weight)
    owners = jnp.asarray(block_owners(ring))[my_index]
    pairs = pair_ids.reshape(-1, tok_rows)
    parts = roles.reshape(-1, tok_rows)
    my_roles = lax.dynamic_slice_in_dim(roles, my_index * tok_rows, tok_rows)
    live = (my_roles != 0).astype(jnp.float32)
    blocks, mates, extras = gather_kv(ring, keys, values, own, (owners, live))
    owners, live = extras
    normed, residual = attend(
        owners, queries, pairs, parts, hidden_in, norm_gain, out_weight, blocks
    )
    normed, own, mates = lax.optimization_barrier((normed, own, mates))
    weights = load(*(in_hbm(w) for w in own)) + load(*mates)
    summed = feed_forward(ring, normed, weights)
    ffn_back = summed.astype(jnp.bfloat16).astype(jnp.float32)
    return (residual.astype(jnp.float32) + ffn_back * live[:, None]).astype(jnp.bfloat16)


def solution(mesh):
    ring = Ring(mesh.shape["groups"], mesh.shape["ctx"])

    def run(*arrays):
        return on_device(ring, *arrays)

    return jax.shard_map(
        run,
        mesh=mesh,
        in_specs=(
            P(("groups", "ctx"), None),
            P(("groups", "ctx"), None),
            P(("groups", "ctx"), None),
            P(("groups", "ctx"), None),
            P(),
            P(),
            P(None, "ctx"),
            P(None, "ctx"),
            P("ctx", None),
            P("groups"),
            P("groups"),
            P(("groups", "ctx"), None),
            P("groups", None),
        ),
        out_specs=P(("groups", "ctx"), None),
        check_vma=False,
    )
```

```python
import functools
import math

import jax
import jax.numpy as jnp
import numpy as np
from jax import lax
from jax.experimental import pallas as pl
from jax.experimental.pallas import tpu as pltpu
from jax.sharding import PartitionSpec as P

NEG_FILL = -1e30
CORES = 2
PLANE = 4
MIB = 1 << 20
CHUNKS = 2


def in_hbm(x):
    return pltpu.with_memory_space_constraint(x, pltpu.HBM)


def in_vmem(x):
    return pltpu.with_memory_space_constraint(x, pltpu.VMEM)


def hold(first, then):
    return lax.optimization_barrier((first, then))


class Ring:
    def __init__(self, groups, devices):
        chips = devices // CORES
        columns = max(1, PLANE // groups)
        if chips % columns:
            columns = 1
        depth = chips // columns
        order = []
        for column in range(columns):
            line = [level * columns + column for level in range(depth)]
            order += line if column % 2 == 0 else line[::-1]
        self.chips = chips
        self.half = chips // 2
        self.order = order
        self.swap = [(i, i ^ 1) for i in range(devices)]

    def go(self, block, hops):
        pairs = []
        for place in range(self.chips):
            here, there = self.order[place], self.order[(place + hops) % self.chips]
            pairs += [(here * CORES + core, there * CORES + core) for core in range(CORES)]
        return lax.ppermute(block, "ctx", pairs)

    def go_mate(self, block):
        return lax.ppermute(block, "ctx", self.swap)

    def go_split(self, block, hops):
        pairs = []
        for place in range(self.chips):
            for core, way in ((0, hops), (1, -hops)):
                here, there = self.order[place], self.order[(place + way) % self.chips]
                pairs.append((here * CORES + core, there * CORES + core))
        return lax.ppermute(block, "ctx", pairs)

    def owners(self, spots, swapped=False):
        place_of = {chip: place for place, chip in enumerate(self.order)}
        table = []
        for device in range(self.chips * CORES):
            chip, core = divmod(device, CORES)
            row = []
            for spot in spots:
                first = self.order[(place_of[chip] + spot[core]) % self.chips] * CORES + core
                row += [first ^ 1, first] if swapped else [first, first ^ 1]
            table.append(row)
        return np.asarray(table, np.int32)


def attention_kernel(
    count,
    pieces,
    heads,
    head_dim,
    owner_ref,
    pair_smem,
    role_smem,
    query_ref,
    pair_ref,
    role_ref,
    hidden_ref,
    gain_ref,
    weight_ref,
    *refs,
):
    blocks, refs = refs[:pieces], refs[pieces:]
    chunk_refs, refs = refs[:CHUNKS], refs[CHUNKS:]
    (residual_ref, stacked, scores, top, total, summed) = refs
    rows = query_ref.shape[0]
    places = [(block, 2 * k) for block in blocks for k in range(block.shape[0] // (2 * rows))]
    me = owner_ref[0]
    for head in range(heads):
        stacked[pl.ds(head * rows, rows), :] = query_ref[:, head * head_dim : (head + 1) * head_dim]

    def column(ref):
        return jnp.broadcast_to(ref[pl.ds(me, 1), :], (rows, rows)).T

    query_pair, query_role = column(pair_ref), column(role_ref)
    query_pos = me * rows + lax.broadcasted_iota(jnp.int32, (rows, rows), 0)
    key_off = lax.broadcasted_iota(jnp.int32, (rows, rows), 1)

    def needed(owner):
        first_pair, last_pair = pair_smem[owner, 0], pair_smem[owner, rows - 1]
        first_role, last_role = role_smem[owner, 0], role_smem[owner, rows - 1]
        my_first, my_last = pair_smem[me, 0], pair_smem[me, rows - 1]
        my_role = role_smem[me, 0]
        apart = (
            (first_pair == last_pair)
            & (my_first == my_last)
            & (first_role == last_role)
            & (my_role == role_smem[me, rows - 1])
            & (first_role != 0)
            & (first_role != my_role)
        )
        return (owner <= me) & (last_pair >= my_first) & jnp.logical_not(apart)

    top[...] = jnp.full_like(top, NEG_FILL)
    total[...] = jnp.zeros_like(total)
    summed[...] = jnp.zeros_like(summed)
    for j in range(count):
        owner = owner_ref[j]

        @pl.when(needed(owner))
        def _():
            seen = (
                (query_pair == pair_ref[pl.ds(owner, 1), :])
                & (owner * rows + key_off <= query_pos)
                & (
                    (role_ref[pl.ds(owner, 1), :] == 0)
                    | (role_ref[pl.ds(owner, 1), :] == query_role)
                )
            )
            bias = jnp.where(seen, 0.0, NEG_FILL)
            raw = lax.dot_general(
                stacked[...],
                places[j][0][pl.ds(places[j][1] * rows, rows), :],
                (((1,), (1,)), ((), ())),
                preferred_element_type=jnp.float32,
            )
            masked = raw.reshape(heads, rows, rows) + bias[None]
            scores[j] = masked
            top[...] = jnp.maximum(top[...], masked)

    top[...] = jnp.broadcast_to(jnp.max(top[...], axis=-1, keepdims=True), top.shape)
    factor = math.log2(math.e) / math.sqrt(head_dim)
    for j in range(count):
        owner = owner_ref[j]

        @pl.when(needed(owner))
        def _():
            weights = jnp.exp2((scores[j] - top[...]) * factor)
            total[...] += weights
            summed[...] += jnp.dot(
                weights.astype(jnp.bfloat16).reshape(heads * rows, rows),
                places[j][0][pl.ds((places[j][1] + 1) * rows, rows), :],
                preferred_element_type=jnp.float32,
            ).reshape(heads, rows, head_dim)

    mixed = (summed[...] / jnp.sum(total[...], axis=-1, keepdims=True)).astype(jnp.bfloat16)
    mixed = jnp.concatenate([mixed[head] for head in range(heads)], axis=1)
    projected = jnp.dot(mixed, weight_ref[...], preferred_element_type=jnp.float32)
    residual = (hidden_ref[...].astype(jnp.float32) + projected).astype(jnp.bfloat16)
    residual_ref[...] = residual
    wide = residual.astype(jnp.float32)
    mean_sq = jnp.mean(wide * wide, axis=-1, keepdims=True)
    normed = (wide * lax.rsqrt(mean_sq + 1e-06) * gain_ref[...]).astype(jnp.bfloat16)
    part = rows // CHUNKS
    for chunk in range(CHUNKS):
        chunk_refs[chunk][...] = normed[chunk * part : (chunk + 1) * part]


def attend(owners, pairs, parts, inputs, blocks):
    queries, _, _, hidden, _, _ = inputs
    rows, width = queries.shape
    head_dim = blocks[0].shape[1]
    heads = width // head_dim
    count = owners.shape[0]
    tall = heads * rows * rows * jnp.dtype(jnp.float32).itemsize
    smem = pl.BlockSpec(memory_space=pltpu.SMEM)
    vmem = pl.BlockSpec(memory_space=pltpu.VMEM)
    square = pltpu.VMEM((heads, rows, rows), jnp.float32)
    chunk = jax.ShapeDtypeStruct((rows // CHUNKS, hidden.shape[1]), jnp.bfloat16)
    *chunks, residual = pl.pallas_call(
        functools.partial(attention_kernel, count, len(blocks), heads, head_dim),
        out_shape=(chunk,) * CHUNKS + (jax.ShapeDtypeStruct(hidden.shape, jnp.bfloat16),),
        in_specs=[smem] * 3 + [vmem] * (len(inputs) + len(blocks)),
        out_specs=(vmem,) * (CHUNKS + 1),
        scratch_shapes=[
            pltpu.VMEM((heads * rows, head_dim), jnp.bfloat16),
            pltpu.VMEM((count, heads, rows, rows), jnp.float32),
            square,
            square,
            pltpu.VMEM((heads, rows, head_dim), jnp.float32),
        ],
        compiler_params=pltpu.CompilerParams(vmem_limit_bytes=(count + 3) * tall + 10 * MIB),
        name="attention",
    )(owners, pairs, parts, *(in_vmem(x) for x in inputs), in_vmem(blocks[0]), *blocks[1:])
    return residual, chunks


def load_kernel(count, *refs):
    inputs, outputs, sems = refs[:count], refs[count : 2 * count], refs[2 * count]
    moves = [pltpu.make_async_copy(inputs[k], outputs[k], sems.at[k]) for k in range(count)]
    for move in moves:
        move.start()
    for move in moves:
        move.wait()


def load(*arrays):
    count = len(arrays)
    return pl.pallas_call(
        functools.partial(load_kernel, count),
        out_shape=tuple(pltpu.VMEM(x.shape, x.dtype) for x in arrays),
        in_specs=[pl.BlockSpec(memory_space=pl.ANY)] * count,
        out_specs=(pl.BlockSpec(memory_space=pltpu.VMEM),) * count,
        scratch_shapes=[pltpu.SemaphoreType.DMA((count,))],
        compiler_params=pltpu.CompilerParams(vmem_limit_bytes=2 * MIB),
        name="load",
    )(*arrays)


def join_kernel(count, *refs):
    inputs, both_ref, sems = refs[:count], refs[count], refs[count + 1]
    rows = inputs[0].shape[0]
    moves = [
        pltpu.make_async_copy(inputs[k], both_ref.at[pl.ds(k * rows, rows), :], sems.at[k])
        for k in range(count)
    ]
    for move in moves:
        move.start()
    for move in moves:
        move.wait()


def join(*parts):
    count = len(parts)
    rows, width = parts[0].shape
    return pl.pallas_call(
        functools.partial(join_kernel, count),
        out_shape=pltpu.VMEM((count * rows, width), parts[0].dtype),
        in_specs=[pl.BlockSpec(memory_space=pl.ANY)] * (count // CORES)
        + [pl.BlockSpec(memory_space=pltpu.VMEM)] * (count - count // CORES),
        out_specs=pl.BlockSpec(memory_space=pltpu.VMEM),
        scratch_shapes=[pltpu.SemaphoreType.DMA((count,))],
        name="join",
    )(*parts)


def ffn_kernel(blocks, *refs):
    inputs, refs = refs[:blocks], refs[blocks:]
    weights, refs = refs[:6], refs[6:]
    outputs, refs = refs[:blocks], refs[blocks:]
    turned, inner, total = refs
    part = inputs[0].shape[0]
    turned[...] = jnp.concatenate([ref[...] for ref in inputs], axis=0).T
    for side in range(2):
        gate, up, down = weights[3 * side : 3 * side + 3]
        gate_out = jnp.dot(gate[...], turned[...], preferred_element_type=jnp.float32)
        up_out = jnp.dot(up[...], turned[...], preferred_element_type=jnp.float32)
        inner[...] = (gate_out / (1.0 + jnp.exp(-gate_out)) * up_out).astype(jnp.bfloat16)
        term = jnp.dot(inner[...].T, down[...], preferred_element_type=jnp.float32)
        if side == 0:
            total[...] = term
        else:
            term = (term + total[...]).astype(jnp.bfloat16)
            for k in range(blocks):
                outputs[k][...] = term[k * part : (k + 1) * part]


def ffn(blocks, weights):
    count = len(blocks)
    rows, width = blocks[0].shape
    hidden = weights[0].shape[0]
    vmem = pl.BlockSpec(memory_space=pltpu.VMEM)
    return pl.pallas_call(
        functools.partial(ffn_kernel, count),
        out_shape=tuple(jax.ShapeDtypeStruct(b.shape, jnp.bfloat16) for b in blocks),
        in_specs=[vmem] * (count + 6),
        out_specs=(vmem,) * count,
        scratch_shapes=[
            pltpu.VMEM((width, count * rows), jnp.bfloat16),
            pltpu.VMEM((hidden, count * rows), jnp.bfloat16),
            pltpu.VMEM((count * rows, width), jnp.float32),
        ],
        compiler_params=pltpu.CompilerParams(vmem_limit_bytes=16 * MIB),
        cost_estimate=pl.CostEstimate(flops=1000, transcendentals=0, bytes_accessed=1000),
        name="feed_forward",
    )(*blocks, *(in_vmem(w) for w in weights))


def feed_forward(ring, chunks, own, mates):
    half = ring.half

    def send(pair, way):
        first, second = hold(*pair)
        return ring.go(first, way), ring.go(second, -way)

    chunks, own, mates = lax.optimization_barrier((chunks, own, mates))
    held = [[(chunks[0], chunks[1])], [(chunks[1], chunks[0])]]
    terms = [{}, {}]
    for group in range(2):
        held[group].append(send(held[group][0], 1))
    weights = load(*(in_hbm(w) for w in own)) + load(*mates)
    weights, held[0][1] = hold(weights, held[0][1])
    last = None
    for step in range(1, half):
        pair = held[0][step]
        if last is not None:
            last, pair = hold(last, pair)
            terms[0][step - 1], terms[1][step - 1] = last[:2], last[2:]
        held[0].append(send(pair, 1))
        if step + 1 < half:
            held[1].append(send(held[1][step], 1))
        last = ffn(held[0][step] + held[1][step], weights)
    last, pair = hold(last, held[0][half])
    if half > 1:
        terms[0][half - 1], terms[1][half - 1] = last[:2], last[2:]
    terms[0][half] = ffn(pair, weights)

    def add(a, b):
        return (a.astype(jnp.float32) + b.astype(jnp.float32)).astype(jnp.bfloat16)

    order = []
    for step in range(half - 1, 0, -1):
        order += [(1, step), (0, step + 1)]
    order.append((0, 1))
    home = [None, None]
    own_terms = None
    for group, step in order:
        pair = terms[group][step]
        if home[group] is not None:
            if group == 0 and own_terms is None:
                home[0], first = hold(home[0], held[0][0])
                own_terms = ffn(first, weights)
            pair = (add(home[group][0], pair[0]), add(home[group][1], pair[1]))
        if group == 0 and step in (half, 2) and half > 2:
            home[1], pair = hold(home[1], pair)
        if step == 1 and group == 0 and own_terms is not None:
            own_terms, pair = hold(own_terms, pair)
        home[group] = send(pair, -1)
    if own_terms is None:
        own_terms = ffn(held[0][0], weights)
    sums = [[x.astype(jnp.float32) for x in own_terms]]
    sums.append([x.astype(jnp.float32) for x in home[0]])
    if home[1] is not None:
        sums.append([x.astype(jnp.float32) for x in home[1][::-1]])
    return [sum(x[k] for x in sums) for k in range(2)]


def gather_kv(ring, keys, values, weights, extras):
    half = ring.half
    gate, up, down = weights
    both = join(in_hbm(keys), in_hbm(values), ring.go_mate(keys), ring.go_mate(values))
    gate, up, both = lax.optimization_barrier((gate, up, both))
    gate_mate, up_mate = ring.go_mate(gate), ring.go_mate(up)
    held, mates = {0: both}, {}
    reach = 0
    while reach < half:
        fresh = range(reach + 1, min(reach + 2, half) + 1)
        for hops in fresh:
            jump = min(2, hops)
            held[hops] = ring.go_split(held[hops - jump], jump)
        for hops in range(max(1, reach - 1), reach + 1):
            mates[hops] = ring.go_mate(held[hops])
        held, mates, extras = lax.optimization_barrier((held, mates, extras))
        reach = fresh[-1]
    for hops in range(1, half):
        if hops not in mates:
            mates[hops] = ring.go_mate(held[hops])
    gate_mate, up_mate, down, held, mates = lax.optimization_barrier(
        (gate_mate, up_mate, down, held, mates)
    )
    down_mate = ring.go_mate(down)
    blocks = tuple(held[hops] for hops in range(half + 1))
    blocks += tuple(mates[hops] for hops in range(1, half))
    return blocks, (gate_mate, up_mate, down_mate), extras


def block_owners(ring):
    half = ring.half
    owners = [ring.owners([(-hops, hops)]) for hops in range(half + 1)]
    owners += [ring.owners([(hops, -hops)], True) for hops in range(1, half)]
    return np.concatenate(owners, axis=1)


def on_device(
    ring,
    hidden_in,
    queries,
    keys,
    values,
    out_weight,
    norm_gain,
    gate_weight,
    up_weight,
    down_weight,
    pair_ids,
    roles,
    send_rows,
    send_counts,
):
    my_index = lax.axis_index("ctx")
    tok_rows = hidden_in.shape[0]
    own = (gate_weight.T, up_weight.T, down_weight)
    owners = jnp.asarray(block_owners(ring))[my_index]
    pairs = pair_ids.reshape(-1, tok_rows)
    parts = roles.reshape(-1, tok_rows)
    my_roles = lax.dynamic_slice_in_dim(roles, my_index * tok_rows, tok_rows)
    live = (my_roles != 0).astype(jnp.float32)
    inputs = load(
        *(in_hbm(x) for x in (queries, pairs, parts, hidden_in, norm_gain.reshape(1, -1), out_weight))
    )
    blocks, mates, extras = gather_kv(ring, keys, values, own, (owners, live, inputs))
    owners, live, inputs = extras
    residual, chunks = attend(owners, pairs, parts, inputs, blocks)
    summed = feed_forward(ring, chunks, own, mates)
    ffn_back = jnp.concatenate(summed, axis=0).astype(jnp.bfloat16).astype(jnp.float32)
    return (residual.astype(jnp.float32) + ffn_back * live[:, None]).astype(jnp.bfloat16)


def solution(mesh):
    ring = Ring(mesh.shape["groups"], mesh.shape["ctx"])

    def run(*arrays):
        return on_device(ring, *arrays)

    return jax.shard_map(
        run,
        mesh=mesh,
        in_specs=(
            P(("groups", "ctx"), None),
            P(("groups", "ctx"), None),
            P(("groups", "ctx"), None),
            P(("groups", "ctx"), None),
            P(),
            P(),
            P(None, "ctx"),
            P(None, "ctx"),
            P("ctx", None),
            P("groups"),
            P("groups"),
            P(("groups", "ctx"), None),
            P("groups", None),
        ),
        out_specs=P(("groups", "ctx"), None),
        check_vma=False,
    )
```

```python
import functools
import math

import jax
import jax.numpy as jnp
import numpy as np
from jax import lax
from jax.experimental import pallas as pl
from jax.experimental.pallas import tpu as pltpu
from jax.sharding import PartitionSpec as P

NEG_FILL = -1e30
CORES = 2
PLANE = 4
MIB = 1 << 20
CHUNKS = 2


def in_hbm(x):
    return pltpu.with_memory_space_constraint(x, pltpu.HBM)


def in_vmem(x):
    return pltpu.with_memory_space_constraint(x, pltpu.VMEM)


def hold(first, then):
    return lax.optimization_barrier((first, then))


class Ring:
    def __init__(self, groups, devices):
        chips = devices // CORES
        columns = max(1, PLANE // groups)
        if chips % columns:
            columns = 1
        depth = chips // columns
        order = []
        for column in range(columns):
            line = [level * columns + column for level in range(depth)]
            order += line if column % 2 == 0 else line[::-1]
        self.chips = chips
        self.half = chips // 2
        self.order = order
        self.swap = [(i, i ^ 1) for i in range(devices)]

    def go(self, block, hops):
        pairs = []
        for place in range(self.chips):
            here, there = self.order[place], self.order[(place + hops) % self.chips]
            pairs += [(here * CORES + core, there * CORES + core) for core in range(CORES)]
        return lax.ppermute(block, "ctx", pairs)

    def go_mate(self, block):
        return lax.ppermute(block, "ctx", self.swap)

    def go_split(self, block, hops):
        pairs = []
        for place in range(self.chips):
            for core, way in ((0, hops), (1, -hops)):
                here, there = self.order[place], self.order[(place + way) % self.chips]
                pairs.append((here * CORES + core, there * CORES + core))
        return lax.ppermute(block, "ctx", pairs)

    def owners(self, spots, swapped=False):
        place_of = {chip: place for place, chip in enumerate(self.order)}
        table = []
        for device in range(self.chips * CORES):
            chip, core = divmod(device, CORES)
            row = []
            for spot in spots:
                first = self.order[(place_of[chip] + spot[core]) % self.chips] * CORES + core
                row += [first ^ 1, first] if swapped else [first, first ^ 1]
            table.append(row)
        return np.asarray(table, np.int32)


def attention_kernel(
    count,
    pieces,
    heads,
    head_dim,
    owner_ref,
    pair_smem,
    role_smem,
    query_ref,
    pair_ref,
    role_ref,
    hidden_ref,
    gain_ref,
    weight_ref,
    *refs,
):
    blocks, refs = refs[:pieces], refs[pieces:]
    chunk_refs, refs = refs[:CHUNKS], refs[CHUNKS:]
    (residual_ref, stacked, scores, top, total, summed) = refs
    rows = query_ref.shape[0]
    places = [(block, 2 * k) for block in blocks for k in range(block.shape[0] // (2 * rows))]
    me = owner_ref[0]
    for head in range(heads):
        stacked[pl.ds(head * rows, rows), :] = query_ref[:, head * head_dim : (head + 1) * head_dim]

    def column(ref):
        return jnp.broadcast_to(ref[pl.ds(me, 1), :], (rows, rows)).T

    query_pair, query_role = column(pair_ref), column(role_ref)
    query_pos = me * rows + lax.broadcasted_iota(jnp.int32, (rows, rows), 0)
    key_off = lax.broadcasted_iota(jnp.int32, (rows, rows), 1)

    def needed(owner):
        first_pair, last_pair = pair_smem[owner, 0], pair_smem[owner, rows - 1]
        first_role, last_role = role_smem[owner, 0], role_smem[owner, rows - 1]
        my_first, my_last = pair_smem[me, 0], pair_smem[me, rows - 1]
        my_role = role_smem[me, 0]
        apart = (
            (first_pair == last_pair)
            & (my_first == my_last)
            & (first_role == last_role)
            & (my_role == role_smem[me, rows - 1])
            & (first_role != 0)
            & (first_role != my_role)
        )
        return (owner <= me) & (last_pair >= my_first) & jnp.logical_not(apart)

    top[...] = jnp.full_like(top, NEG_FILL)
    total[...] = jnp.zeros_like(total)
    summed[...] = jnp.zeros_like(summed)
    for j in range(count):
        owner = owner_ref[j]

        @pl.when(needed(owner))
        def _():
            seen = (
                (query_pair == pair_ref[pl.ds(owner, 1), :])
                & (owner * rows + key_off <= query_pos)
                & (
                    (role_ref[pl.ds(owner, 1), :] == 0)
                    | (role_ref[pl.ds(owner, 1), :] == query_role)
                )
            )
            bias = jnp.where(seen, 0.0, NEG_FILL)
            raw = lax.dot_general(
                stacked[...],
                places[j][0][pl.ds(places[j][1] * rows, rows), :],
                (((1,), (1,)), ((), ())),
                preferred_element_type=jnp.float32,
            )
            masked = raw.reshape(heads, rows, rows) + bias[None]
            scores[j] = masked
            top[...] = jnp.maximum(top[...], masked)

    top[...] = jnp.broadcast_to(jnp.max(top[...], axis=-1, keepdims=True), top.shape)
    factor = math.log2(math.e) / math.sqrt(head_dim)
    for j in range(count):
        owner = owner_ref[j]

        @pl.when(needed(owner))
        def _():
            weights = jnp.exp2((scores[j] - top[...]) * factor)
            total[...] += weights
            summed[...] += jnp.dot(
                weights.astype(jnp.bfloat16).reshape(heads * rows, rows),
                places[j][0][pl.ds((places[j][1] + 1) * rows, rows), :],
                preferred_element_type=jnp.float32,
            ).reshape(heads, rows, head_dim)

    mixed = (summed[...] / jnp.sum(total[...], axis=-1, keepdims=True)).astype(jnp.bfloat16)
    mixed = jnp.concatenate([mixed[head] for head in range(heads)], axis=1)
    projected = jnp.dot(mixed, weight_ref[...], preferred_element_type=jnp.float32)
    residual = (hidden_ref[...].astype(jnp.float32) + projected).astype(jnp.bfloat16)
    residual_ref[...] = residual
    wide = residual.astype(jnp.float32)
    mean_sq = jnp.mean(wide * wide, axis=-1, keepdims=True)
    normed = (wide * lax.rsqrt(mean_sq + 1e-06) * gain_ref[...]).astype(jnp.bfloat16)
    part = rows // CHUNKS
    for chunk in range(CHUNKS):
        chunk_refs[chunk][...] = normed[chunk * part : (chunk + 1) * part]


def attend(owners, pairs, parts, inputs, blocks):
    queries, _, _, hidden, _, _ = inputs
    rows, width = queries.shape
    head_dim = blocks[0].shape[1]
    heads = width // head_dim
    count = owners.shape[0]
    tall = heads * rows * rows * jnp.dtype(jnp.float32).itemsize
    smem = pl.BlockSpec(memory_space=pltpu.SMEM)
    vmem = pl.BlockSpec(memory_space=pltpu.VMEM)
    square = pltpu.VMEM((heads, rows, rows), jnp.float32)
    chunk = jax.ShapeDtypeStruct((rows // CHUNKS, hidden.shape[1]), jnp.bfloat16)
    *chunks, residual = pl.pallas_call(
        functools.partial(attention_kernel, count, len(blocks), heads, head_dim),
        out_shape=(chunk,) * CHUNKS + (jax.ShapeDtypeStruct(hidden.shape, jnp.bfloat16),),
        in_specs=[smem] * 3 + [vmem] * (len(inputs) + len(blocks)),
        out_specs=(vmem,) * (CHUNKS + 1),
        scratch_shapes=[
            pltpu.VMEM((heads * rows, head_dim), jnp.bfloat16),
            pltpu.VMEM((count, heads, rows, rows), jnp.float32),
            square,
            square,
            pltpu.VMEM((heads, rows, head_dim), jnp.float32),
        ],
        compiler_params=pltpu.CompilerParams(vmem_limit_bytes=(count + 3) * tall + 10 * MIB),
        name="attention",
    )(owners, pairs, parts, *(in_vmem(x) for x in inputs), in_vmem(blocks[0]), *blocks[1:])
    return residual, chunks


def load_kernel(count, *refs):
    inputs, outputs, sems = refs[:count], refs[count : 2 * count], refs[2 * count]
    moves = [pltpu.make_async_copy(inputs[k], outputs[k], sems.at[k]) for k in range(count)]
    for move in moves:
        move.start()
    for move in moves:
        move.wait()


def load(*arrays):
    count = len(arrays)
    return pl.pallas_call(
        functools.partial(load_kernel, count),
        out_shape=tuple(pltpu.VMEM(x.shape, x.dtype) for x in arrays),
        in_specs=[pl.BlockSpec(memory_space=pl.ANY)] * count,
        out_specs=(pl.BlockSpec(memory_space=pltpu.VMEM),) * count,
        scratch_shapes=[pltpu.SemaphoreType.DMA((count,))],
        compiler_params=pltpu.CompilerParams(vmem_limit_bytes=2 * MIB),
        name="load",
    )(*arrays)


def join_kernel(count, *refs):
    inputs, both_ref, sems = refs[:count], refs[count], refs[count + 1]
    rows = inputs[0].shape[0]
    moves = [
        pltpu.make_async_copy(inputs[k], both_ref.at[pl.ds(k * rows, rows), :], sems.at[k])
        for k in range(count)
    ]
    for move in moves:
        move.start()
    for move in moves:
        move.wait()


def join(*parts):
    count = len(parts)
    rows, width = parts[0].shape
    return pl.pallas_call(
        functools.partial(join_kernel, count),
        out_shape=pltpu.VMEM((count * rows, width), parts[0].dtype),
        in_specs=[pl.BlockSpec(memory_space=pl.ANY)] * (count // CORES)
        + [pl.BlockSpec(memory_space=pltpu.VMEM)] * (count - count // CORES),
        out_specs=pl.BlockSpec(memory_space=pltpu.VMEM),
        scratch_shapes=[pltpu.SemaphoreType.DMA((count,))],
        name="join",
    )(*parts)


def ffn_kernel(blocks, *refs):
    inputs, refs = refs[:blocks], refs[blocks:]
    weights, refs = refs[:6], refs[6:]
    outputs, refs = refs[:blocks], refs[blocks:]
    turned, inner, total = refs
    part = inputs[0].shape[0]
    turned[...] = jnp.concatenate([ref[...] for ref in inputs], axis=0).T
    for side in range(2):
        gate, up, down = weights[3 * side : 3 * side + 3]
        gate_out = jnp.dot(gate[...], turned[...], preferred_element_type=jnp.float32)
        up_out = jnp.dot(up[...], turned[...], preferred_element_type=jnp.float32)
        inner[...] = (gate_out / (1.0 + jnp.exp(-gate_out)) * up_out).astype(jnp.bfloat16)
        term = jnp.dot(inner[...].T, down[...], preferred_element_type=jnp.float32)
        if side == 0:
            total[...] = term
        else:
            term = (term + total[...]).astype(jnp.bfloat16)
            for k in range(blocks):
                outputs[k][...] = term[k * part : (k + 1) * part]


def ffn(blocks, weights):
    count = len(blocks)
    rows, width = blocks[0].shape
    hidden = weights[0].shape[0]
    vmem = pl.BlockSpec(memory_space=pltpu.VMEM)
    return pl.pallas_call(
        functools.partial(ffn_kernel, count),
        out_shape=tuple(jax.ShapeDtypeStruct(b.shape, jnp.bfloat16) for b in blocks),
        in_specs=[vmem] * (count + 6),
        out_specs=(vmem,) * count,
        scratch_shapes=[
            pltpu.VMEM((width, count * rows), jnp.bfloat16),
            pltpu.VMEM((hidden, count * rows), jnp.bfloat16),
            pltpu.VMEM((count * rows, width), jnp.float32),
        ],
        compiler_params=pltpu.CompilerParams(vmem_limit_bytes=16 * MIB),
        cost_estimate=pl.CostEstimate(flops=1000, transcendentals=0, bytes_accessed=1000),
        name="feed_forward",
    )(*blocks, *(in_vmem(w) for w in weights))


def feed_forward(ring, chunks, own, mates):
    half = ring.half

    def send(pair, way):
        first, second = hold(*pair)
        return ring.go(first, way), ring.go(second, -way)

    chunks, own, mates = lax.optimization_barrier((chunks, own, mates))
    held = [[(chunks[0], chunks[1])], [(chunks[1], chunks[0])]]
    terms = [{}, {}]
    for group in range(2):
        held[group].append(send(held[group][0], 1))
    weights = load(*(in_hbm(w) for w in own)) + load(*mates)
    weights, held[0][1] = hold(weights, held[0][1])
    for step in range(1, half):
        held[0].append(send(held[0][step], 1))
        older = held[1][step - 1] if step > 1 else held[0][0]
        done = ffn(held[0][step] + older, weights)
        if step + 1 < half:
            done, pair = hold(done, held[1][step])
            held[1].append(send(pair, 1))
        terms[0][step], terms[1][step - 1] = done[:2], done[2:]
    older = held[1][half - 1] if half > 1 else held[0][0]
    if half > 1:
        done, older = hold(done, older)
        terms[0][half - 1], terms[1][half - 2] = done[:2], done[2:]
    done = ffn(held[0][half] + older, weights)
    terms[0][half], terms[1][half - 1] = done[:2], done[2:]

    def add(a, b):
        return (a.astype(jnp.float32) + b.astype(jnp.float32)).astype(jnp.bfloat16)

    home = [None, None]
    for step in range(half, 0, -1):
        for group in range(2):
            place = step - group
            if place == 0:
                continue
            pair = terms[group][place]
            if home[group] is not None:
                pair = (add(home[group][0], pair[0]), add(home[group][1], pair[1]))
            home[group] = send(pair, -1)
    sums = [[x.astype(jnp.float32) for x in terms[1][0]]]
    if home[1] is not None:
        sums.append([x.astype(jnp.float32) for x in home[1][::-1]])
    sums.append([x.astype(jnp.float32) for x in home[0]])
    return [sum(x[k] for x in sums) for k in range(2)]


def gather_kv(ring, keys, values, weights, extras):
    half = ring.half
    gate, up, down = weights
    both = join(in_hbm(keys), in_hbm(values), *(in_vmem(ring.go_mate(x)) for x in (keys, values)))
    gate, up, both = lax.optimization_barrier((gate, up, both))
    gate_mate, up_mate = ring.go_mate(gate), ring.go_mate(up)
    held, mates = {0: both}, {}
    reach = 0
    while reach < half:
        fresh = range(reach + 1, min(reach + 2, half) + 1)
        for hops in fresh:
            jump = min(2, hops)
            held[hops] = ring.go_split(held[hops - jump], jump)
        for hops in range(max(1, reach - 1), reach + 1):
            mates[hops] = ring.go_mate(held[hops])
        held, mates, extras = lax.optimization_barrier((held, mates, extras))
        reach = fresh[-1]
    for hops in range(1, half):
        if hops not in mates:
            mates[hops] = ring.go_mate(held[hops])
    gate_mate, up_mate, down, held, mates = lax.optimization_barrier(
        (gate_mate, up_mate, down, held, mates)
    )
    down_mate = ring.go_mate(down)
    blocks = tuple(held[hops] for hops in range(half + 1))
    blocks += tuple(mates[hops] for hops in range(1, half))
    return blocks, (gate_mate, up_mate, down_mate), extras


def block_owners(ring):
    half = ring.half
    owners = [ring.owners([(-hops, hops)]) for hops in range(half + 1)]
    owners += [ring.owners([(hops, -hops)], True) for hops in range(1, half)]
    return np.concatenate(owners, axis=1)


def on_device(
    ring,
    hidden_in,
    queries,
    keys,
    values,
    out_weight,
    norm_gain,
    gate_weight,
    up_weight,
    down_weight,
    pair_ids,
    roles,
    send_rows,
    send_counts,
):
    my_index = lax.axis_index("ctx")
    tok_rows = hidden_in.shape[0]
    own = (gate_weight.T, up_weight.T, down_weight)
    owners = jnp.asarray(block_owners(ring))[my_index]
    pairs = pair_ids.reshape(-1, tok_rows)
    parts = roles.reshape(-1, tok_rows)
    my_roles = lax.dynamic_slice_in_dim(roles, my_index * tok_rows, tok_rows)
    live = (my_roles != 0).astype(jnp.float32)
    inputs = load(
        *(in_hbm(x) for x in (queries, pairs, parts, hidden_in, norm_gain.reshape(1, -1), out_weight))
    )
    blocks, mates, extras = gather_kv(ring, keys, values, own, (owners, live, inputs))
    owners, live, inputs = extras
    residual, chunks = attend(owners, pairs, parts, inputs, blocks)
    summed = feed_forward(ring, chunks, own, mates)
    ffn_back = jnp.concatenate(summed, axis=0).astype(jnp.bfloat16).astype(jnp.float32)
    return (residual.astype(jnp.float32) + ffn_back * live[:, None]).astype(jnp.bfloat16)


def solution(mesh):
    ring = Ring(mesh.shape["groups"], mesh.shape["ctx"])

    def run(*arrays):
        return on_device(ring, *arrays)

    return jax.shard_map(
        run,
        mesh=mesh,
        in_specs=(
            P(("groups", "ctx"), None),
            P(("groups", "ctx"), None),
            P(("groups", "ctx"), None),
            P(("groups", "ctx"), None),
            P(),
            P(),
            P(None, "ctx"),
            P(None, "ctx"),
            P("ctx", None),
            P("groups"),
            P("groups"),
            P(("groups", "ctx"), None),
            P("groups", None),
        ),
        out_specs=P(("groups", "ctx"), None),
        check_vma=False,
    )
```

```python
import functools
import math

import jax
import jax.numpy as jnp
import numpy as np
from jax import lax
from jax.experimental import pallas as pl
from jax.experimental.pallas import tpu as pltpu
from jax.sharding import PartitionSpec as P

NEG_FILL = -1e30
CORES = 2
PLANE = 4
MIB = 1 << 20
CHUNKS = 2


def in_hbm(x):
    return pltpu.with_memory_space_constraint(x, pltpu.HBM)


def in_vmem(x):
    return pltpu.with_memory_space_constraint(x, pltpu.VMEM)


def hold(first, then):
    return lax.optimization_barrier((first, then))


class Ring:
    def __init__(self, groups, devices):
        chips = devices // CORES
        columns = max(1, PLANE // groups)
        if chips % columns:
            columns = 1
        depth = chips // columns
        order = []
        for column in range(columns):
            line = [level * columns + column for level in range(depth)]
            order += line if column % 2 == 0 else line[::-1]
        self.chips = chips
        self.half = chips // 2
        self.order = order
        self.swap = [(i, i ^ 1) for i in range(devices)]

    def go(self, block, hops):
        pairs = []
        for place in range(self.chips):
            here, there = self.order[place], self.order[(place + hops) % self.chips]
            pairs += [(here * CORES + core, there * CORES + core) for core in range(CORES)]
        return lax.ppermute(block, "ctx", pairs)

    def go_mate(self, block):
        return lax.ppermute(block, "ctx", self.swap)

    def go_split(self, block, hops):
        pairs = []
        for place in range(self.chips):
            for core, way in ((0, hops), (1, -hops)):
                here, there = self.order[place], self.order[(place + way) % self.chips]
                pairs.append((here * CORES + core, there * CORES + core))
        return lax.ppermute(block, "ctx", pairs)

    def owners(self, spots, swapped=False):
        place_of = {chip: place for place, chip in enumerate(self.order)}
        table = []
        for device in range(self.chips * CORES):
            chip, core = divmod(device, CORES)
            row = []
            for spot in spots:
                first = self.order[(place_of[chip] + spot[core]) % self.chips] * CORES + core
                row += [first ^ 1, first] if swapped else [first, first ^ 1]
            table.append(row)
        return np.asarray(table, np.int32)


def attention_kernel(
    count,
    pieces,
    heads,
    head_dim,
    owner_ref,
    pair_smem,
    role_smem,
    query_ref,
    pair_ref,
    role_ref,
    hidden_ref,
    gain_ref,
    weight_ref,
    *refs,
):
    blocks, refs = refs[:pieces], refs[pieces:]
    chunk_refs, refs = refs[:CHUNKS], refs[CHUNKS:]
    (residual_ref, stacked, scores, top, total, summed) = refs
    rows = query_ref.shape[0]
    places = [(block, 2 * k) for block in blocks for k in range(block.shape[0] // (2 * rows))]
    me = owner_ref[0]
    for head in range(heads):
        stacked[pl.ds(head * rows, rows), :] = query_ref[:, head * head_dim : (head + 1) * head_dim]

    def column(ref):
        return jnp.broadcast_to(ref[pl.ds(me, 1), :], (rows, rows)).T

    query_pair, query_role = column(pair_ref), column(role_ref)
    query_pos = me * rows + lax.broadcasted_iota(jnp.int32, (rows, rows), 0)
    key_off = lax.broadcasted_iota(jnp.int32, (rows, rows), 1)

    def needed(owner):
        first_pair, last_pair = pair_smem[owner, 0], pair_smem[owner, rows - 1]
        first_role, last_role = role_smem[owner, 0], role_smem[owner, rows - 1]
        my_first, my_last = pair_smem[me, 0], pair_smem[me, rows - 1]
        my_role = role_smem[me, 0]
        apart = (
            (first_pair == last_pair)
            & (my_first == my_last)
            & (first_role == last_role)
            & (my_role == role_smem[me, rows - 1])
            & (first_role != 0)
            & (first_role != my_role)
        )
        return (owner <= me) & (last_pair >= my_first) & jnp.logical_not(apart)

    top[...] = jnp.full_like(top, NEG_FILL)
    total[...] = jnp.zeros_like(total)
    summed[...] = jnp.zeros_like(summed)
    for j in range(count):
        owner = owner_ref[j]

        @pl.when(needed(owner))
        def _():
            seen = (
                (query_pair == pair_ref[pl.ds(owner, 1), :])
                & (owner * rows + key_off <= query_pos)
                & (
                    (role_ref[pl.ds(owner, 1), :] == 0)
                    | (role_ref[pl.ds(owner, 1), :] == query_role)
                )
            )
            bias = jnp.where(seen, 0.0, NEG_FILL)
            raw = lax.dot_general(
                stacked[...],
                places[j][0][pl.ds(places[j][1] * rows, rows), :],
                (((1,), (1,)), ((), ())),
                preferred_element_type=jnp.float32,
            )
            masked = raw.reshape(heads, rows, rows) + bias[None]
            scores[j] = masked
            top[...] = jnp.maximum(top[...], masked)

    top[...] = jnp.broadcast_to(jnp.max(top[...], axis=-1, keepdims=True), top.shape)
    factor = math.log2(math.e) / math.sqrt(head_dim)
    for j in range(count):
        owner = owner_ref[j]

        @pl.when(needed(owner))
        def _():
            weights = jnp.exp2((scores[j] - top[...]) * factor)
            total[...] += weights
            summed[...] += jnp.dot(
                weights.astype(jnp.bfloat16).reshape(heads * rows, rows),
                places[j][0][pl.ds((places[j][1] + 1) * rows, rows), :],
                preferred_element_type=jnp.float32,
            ).reshape(heads, rows, head_dim)

    mixed = (summed[...] / jnp.sum(total[...], axis=-1, keepdims=True)).astype(jnp.bfloat16)
    mixed = jnp.concatenate([mixed[head] for head in range(heads)], axis=1)
    projected = jnp.dot(mixed, weight_ref[...], preferred_element_type=jnp.float32)
    residual = (hidden_ref[...].astype(jnp.float32) + projected).astype(jnp.bfloat16)
    residual_ref[...] = residual
    wide = residual.astype(jnp.float32)
    mean_sq = jnp.mean(wide * wide, axis=-1, keepdims=True)
    normed = (wide * lax.rsqrt(mean_sq + 1e-06) * gain_ref[...]).astype(jnp.bfloat16)
    part = rows // CHUNKS
    for chunk in range(CHUNKS):
        chunk_refs[chunk][...] = normed[chunk * part : (chunk + 1) * part]


def attend(owners, pairs, parts, inputs, blocks):
    queries, _, _, hidden, _, _ = inputs
    rows, width = queries.shape
    head_dim = blocks[0].shape[1]
    heads = width // head_dim
    count = owners.shape[0]
    tall = heads * rows * rows * jnp.dtype(jnp.float32).itemsize
    smem = pl.BlockSpec(memory_space=pltpu.SMEM)
    vmem = pl.BlockSpec(memory_space=pltpu.VMEM)
    square = pltpu.VMEM((heads, rows, rows), jnp.float32)
    chunk = jax.ShapeDtypeStruct((rows // CHUNKS, hidden.shape[1]), jnp.bfloat16)
    *chunks, residual = pl.pallas_call(
        functools.partial(attention_kernel, count, len(blocks), heads, head_dim),
        out_shape=(chunk,) * CHUNKS + (jax.ShapeDtypeStruct(hidden.shape, jnp.bfloat16),),
        in_specs=[smem] * 3 + [vmem] * (len(inputs) + len(blocks)),
        out_specs=(vmem,) * (CHUNKS + 1),
        scratch_shapes=[
            pltpu.VMEM((heads * rows, head_dim), jnp.bfloat16),
            pltpu.VMEM((count, heads, rows, rows), jnp.float32),
            square,
            square,
            pltpu.VMEM((heads, rows, head_dim), jnp.float32),
        ],
        compiler_params=pltpu.CompilerParams(vmem_limit_bytes=(count + 3) * tall + 10 * MIB),
        name="attention",
    )(owners, pairs, parts, *(in_vmem(x) for x in inputs), in_vmem(blocks[0]), *blocks[1:])
    return residual, chunks


def load_kernel(count, *refs):
    inputs, outputs, sems = refs[:count], refs[count : 2 * count], refs[2 * count]
    moves = [pltpu.make_async_copy(inputs[k], outputs[k], sems.at[k]) for k in range(count)]
    for move in moves:
        move.start()
    for move in moves:
        move.wait()


def load(*arrays):
    count = len(arrays)
    return pl.pallas_call(
        functools.partial(load_kernel, count),
        out_shape=tuple(pltpu.VMEM(x.shape, x.dtype) for x in arrays),
        in_specs=[pl.BlockSpec(memory_space=pl.ANY)] * count,
        out_specs=(pl.BlockSpec(memory_space=pltpu.VMEM),) * count,
        scratch_shapes=[pltpu.SemaphoreType.DMA((count,))],
        compiler_params=pltpu.CompilerParams(vmem_limit_bytes=2 * MIB),
        name="load",
    )(*arrays)


def join_kernel(count, *refs):
    inputs, both_ref, sems = refs[:count], refs[count], refs[count + 1]
    rows = inputs[0].shape[0]
    moves = [
        pltpu.make_async_copy(inputs[k], both_ref.at[pl.ds(k * rows, rows), :], sems.at[k])
        for k in range(count)
    ]
    for move in moves:
        move.start()
    for move in moves:
        move.wait()


def join(*parts):
    count = len(parts)
    rows, width = parts[0].shape
    return pl.pallas_call(
        functools.partial(join_kernel, count),
        out_shape=pltpu.VMEM((count * rows, width), parts[0].dtype),
        in_specs=[pl.BlockSpec(memory_space=pl.ANY)] * (count // CORES)
        + [pl.BlockSpec(memory_space=pltpu.VMEM)] * (count - count // CORES),
        out_specs=pl.BlockSpec(memory_space=pltpu.VMEM),
        scratch_shapes=[pltpu.SemaphoreType.DMA((count,))],
        name="join",
    )(*parts)


def ffn_kernel(blocks, *refs):
    inputs, refs = refs[:blocks], refs[blocks:]
    weights, refs = refs[:6], refs[6:]
    outputs, refs = refs[:blocks], refs[blocks:]
    turned, inner, total = refs
    part = inputs[0].shape[0]
    turned[...] = jnp.concatenate([ref[...] for ref in inputs], axis=0).T
    for side in range(2):
        gate, up, down = weights[3 * side : 3 * side + 3]
        gate_out = jnp.dot(gate[...], turned[...], preferred_element_type=jnp.float32)
        up_out = jnp.dot(up[...], turned[...], preferred_element_type=jnp.float32)
        inner[...] = (gate_out / (1.0 + jnp.exp(-gate_out)) * up_out).astype(jnp.bfloat16)
        term = jnp.dot(inner[...].T, down[...], preferred_element_type=jnp.float32)
        if side == 0:
            total[...] = term
        else:
            term = (term + total[...]).astype(jnp.bfloat16)
            for k in range(blocks):
                outputs[k][...] = term[k * part : (k + 1) * part]


def ffn(blocks, weights):
    count = len(blocks)
    rows, width = blocks[0].shape
    hidden = weights[0].shape[0]
    vmem = pl.BlockSpec(memory_space=pltpu.VMEM)
    return pl.pallas_call(
        functools.partial(ffn_kernel, count),
        out_shape=tuple(jax.ShapeDtypeStruct(b.shape, jnp.bfloat16) for b in blocks),
        in_specs=[vmem] * (count + 6),
        out_specs=(vmem,) * count,
        scratch_shapes=[
            pltpu.VMEM((width, count * rows), jnp.bfloat16),
            pltpu.VMEM((hidden, count * rows), jnp.bfloat16),
            pltpu.VMEM((count * rows, width), jnp.float32),
        ],
        compiler_params=pltpu.CompilerParams(vmem_limit_bytes=16 * MIB),
        cost_estimate=pl.CostEstimate(flops=1000, transcendentals=0, bytes_accessed=1000),
        name="feed_forward",
    )(*blocks, *(in_vmem(w) for w in weights))


def feed_forward(ring, chunks, own, mates):
    half = ring.half

    def send(pair, way):
        return ring.go(pair[0], way), ring.go(pair[1], -way)

    chunks, own, mates = lax.optimization_barrier((chunks, own, mates))
    held = [[(chunks[0], chunks[1])], [(chunks[1], chunks[0])]]
    terms = [{}, {}]
    for group in range(2):
        held[group].append(send(held[group][0], 1))
    weights = load(*(in_hbm(w) for w in own)) + load(*mates)
    weights, held[0][1] = hold(weights, held[0][1])
    for step in range(1, half):
        held[0].append(send(held[0][step], 1))
        older = held[1][step - 1] if step > 1 else held[0][0]
        done = ffn(held[0][step] + older, weights)
        if step + 1 < half:
            done, pair = hold(done, held[1][step])
            held[1].append(send(pair, 1))
        terms[0][step], terms[1][step - 1] = done[:2], done[2:]
    older = held[1][half - 1] if half > 1 else held[0][0]
    if half > 1:
        done, older = hold(done, older)
        terms[0][half - 1], terms[1][half - 2] = done[:2], done[2:]
    done = ffn(held[0][half] + older, weights)
    terms[0][half], terms[1][half - 1] = done[:2], done[2:]

    def add(a, b):
        return (a.astype(jnp.float32) + b.astype(jnp.float32)).astype(jnp.bfloat16)

    home = [None, None]
    for step in range(half, 0, -1):
        for group in range(2):
            place = step - group
            if place == 0:
                continue
            pair = terms[group][place]
            if home[group] is not None:
                pair = (add(home[group][0], pair[0]), add(home[group][1], pair[1]))
            home[group] = send(pair, -1)
    sums = [[x.astype(jnp.float32) for x in terms[1][0]]]
    if home[1] is not None:
        sums.append([x.astype(jnp.float32) for x in home[1][::-1]])
    sums.append([x.astype(jnp.float32) for x in home[0]])
    return [sum(x[k] for x in sums) for k in range(2)]


def gather_kv(ring, keys, values, weights, extras):
    half = ring.half
    gate, up, down = weights
    both = join(in_hbm(keys), in_hbm(values), *(in_vmem(ring.go_mate(x)) for x in (keys, values)))
    gate, up, both = lax.optimization_barrier((gate, up, both))
    gate_mate, up_mate = ring.go_mate(gate), ring.go_mate(up)
    held, mates = {0: both}, {}
    reach = 0
    while reach < half:
        fresh = range(reach + 1, min(reach + 2, half) + 1)
        for hops in fresh:
            jump = min(2, hops)
            held[hops] = ring.go_split(held[hops - jump], jump)
        for hops in range(max(1, reach - 1), reach + 1):
            mates[hops] = ring.go_mate(held[hops])
        held, mates, extras = lax.optimization_barrier((held, mates, extras))
        reach = fresh[-1]
    for hops in range(1, half):
        if hops not in mates:
            mates[hops] = ring.go_mate(held[hops])
    gate_mate, up_mate, down, held, mates = lax.optimization_barrier(
        (gate_mate, up_mate, down, held, mates)
    )
    down_mate = ring.go_mate(down)
    blocks = tuple(held[hops] for hops in range(half + 1))
    blocks += tuple(mates[hops] for hops in range(1, half))
    return blocks, (gate_mate, up_mate, down_mate), extras


def block_owners(ring):
    half = ring.half
    owners = [ring.owners([(-hops, hops)]) for hops in range(half + 1)]
    owners += [ring.owners([(hops, -hops)], True) for hops in range(1, half)]
    return np.concatenate(owners, axis=1)


def on_device(
    ring,
    hidden_in,
    queries,
    keys,
    values,
    out_weight,
    norm_gain,
    gate_weight,
    up_weight,
    down_weight,
    pair_ids,
    roles,
    send_rows,
    send_counts,
):
    my_index = lax.axis_index("ctx")
    tok_rows = hidden_in.shape[0]
    own = (gate_weight.T, up_weight.T, down_weight)
    owners = jnp.asarray(block_owners(ring))[my_index]
    pairs = pair_ids.reshape(-1, tok_rows)
    parts = roles.reshape(-1, tok_rows)
    my_roles = lax.dynamic_slice_in_dim(roles, my_index * tok_rows, tok_rows)
    live = (my_roles != 0).astype(jnp.float32)
    inputs = load(
        *(in_hbm(x) for x in (queries, pairs, parts, hidden_in, norm_gain.reshape(1, -1), out_weight))
    )
    blocks, mates, extras = gather_kv(ring, keys, values, own, (owners, live, inputs))
    owners, live, inputs = extras
    residual, chunks = attend(owners, pairs, parts, inputs, blocks)
    summed = feed_forward(ring, chunks, own, mates)
    ffn_back = jnp.concatenate(summed, axis=0).astype(jnp.bfloat16).astype(jnp.float32)
    return (residual.astype(jnp.float32) + ffn_back * live[:, None]).astype(jnp.bfloat16)


def solution(mesh):
    ring = Ring(mesh.shape["groups"], mesh.shape["ctx"])

    def run(*arrays):
        return on_device(ring, *arrays)

    return jax.shard_map(
        run,
        mesh=mesh,
        in_specs=(
            P(("groups", "ctx"), None),
            P(("groups", "ctx"), None),
            P(("groups", "ctx"), None),
            P(("groups", "ctx"), None),
            P(),
            P(),
            P(None, "ctx"),
            P(None, "ctx"),
            P("ctx", None),
            P("groups"),
            P("groups"),
            P(("groups", "ctx"), None),
            P("groups", None),
        ),
        out_specs=P(("groups", "ctx"), None),
        check_vma=False,
    )
```

```python
import functools
import math

import jax
import jax.numpy as jnp
import numpy as np
from jax import lax
from jax.experimental import pallas as pl
from jax.experimental.pallas import tpu as pltpu
from jax.sharding import PartitionSpec as P

NEG_FILL = -1e30
CORES = 2
PLANE = 4
MIB = 1 << 20
CHUNKS = 2


def in_hbm(x):
    return pltpu.with_memory_space_constraint(x, pltpu.HBM)


def in_vmem(x):
    return pltpu.with_memory_space_constraint(x, pltpu.VMEM)


def hold(first, then):
    return lax.optimization_barrier((first, then))


class Ring:
    def __init__(self, groups, devices):
        chips = devices // CORES
        columns = max(1, PLANE // groups)
        if chips % columns:
            columns = 1
        depth = chips // columns
        order = []
        for column in range(columns):
            line = [level * columns + column for level in range(depth)]
            order += line if column % 2 == 0 else line[::-1]
        self.chips = chips
        self.half = chips // 2
        self.order = order
        self.swap = [(i, i ^ 1) for i in range(devices)]

    def go(self, block, hops):
        pairs = []
        for place in range(self.chips):
            here, there = self.order[place], self.order[(place + hops) % self.chips]
            pairs += [(here * CORES + core, there * CORES + core) for core in range(CORES)]
        return lax.ppermute(block, "ctx", pairs)

    def go_mate(self, block):
        return lax.ppermute(block, "ctx", self.swap)

    def go_split(self, block, hops):
        pairs = []
        for place in range(self.chips):
            for core, way in ((0, hops), (1, -hops)):
                here, there = self.order[place], self.order[(place + way) % self.chips]
                pairs.append((here * CORES + core, there * CORES + core))
        return lax.ppermute(block, "ctx", pairs)

    def owners(self, spots, swapped=False):
        place_of = {chip: place for place, chip in enumerate(self.order)}
        table = []
        for device in range(self.chips * CORES):
            chip, core = divmod(device, CORES)
            row = []
            for spot in spots:
                first = self.order[(place_of[chip] + spot[core]) % self.chips] * CORES + core
                row += [first ^ 1, first] if swapped else [first, first ^ 1]
            table.append(row)
        return np.asarray(table, np.int32)


def attention_kernel(
    pieces,
    heads,
    head_dim,
    owner_ref,
    pair_smem,
    role_smem,
    query_ref,
    pair_ref,
    role_ref,
    hidden_ref,
    gain_ref,
    weight_ref,
    *refs,
):
    blocks, refs = refs[:pieces], refs[pieces:]
    chunk_refs, refs = refs[:CHUNKS], refs[CHUNKS:]
    (residual_ref, stacked, scores, top, total, summed) = refs
    rows = query_ref.shape[0]
    me = owner_ref[0]
    for head in range(heads):
        stacked[pl.ds(head * rows, rows), :] = query_ref[:, head * head_dim : (head + 1) * head_dim]

    def column(ref):
        return jnp.broadcast_to(ref[pl.ds(me, 1), :], (rows, rows)).T

    query_pair, query_role = column(pair_ref), column(role_ref)
    query_pos = me * rows + lax.broadcasted_iota(jnp.int32, (rows, rows), 0)
    key_off = lax.broadcasted_iota(jnp.int32, (rows, rows), 1)

    def needed(owner):
        first_pair, last_pair = pair_smem[owner, 0], pair_smem[owner, rows - 1]
        first_role, last_role = role_smem[owner, 0], role_smem[owner, rows - 1]
        my_first, my_last = pair_smem[me, 0], pair_smem[me, rows - 1]
        my_role = role_smem[me, 0]
        apart = (
            (first_pair == last_pair)
            & (my_first == my_last)
            & (first_role == last_role)
            & (my_role == role_smem[me, rows - 1])
            & (first_role != 0)
            & (first_role != my_role)
        )
        return (owner <= me) & (last_pair >= my_first) & jnp.logical_not(apart)

    def bias_of(owner):
        key_role = role_ref[pl.ds(owner, 1), :]
        seen = (
            (query_pair == pair_ref[pl.ds(owner, 1), :])
            & (owner * rows + key_off <= query_pos)
            & ((key_role == 0) | (key_role == query_role))
        )
        return jnp.where(seen, 0.0, NEG_FILL)

    top[...] = jnp.full_like(top, NEG_FILL)
    total[...] = jnp.zeros_like(total)
    summed[...] = jnp.zeros_like(summed)
    for j, block in enumerate(blocks):
        owners = owner_ref[2 * j], owner_ref[2 * j + 1]

        @pl.when(needed(owners[0]) | needed(owners[1]))
        def _():
            bias = jnp.concatenate([bias_of(owner) for owner in owners], axis=1)
            raw = lax.dot_general(
                stacked[...],
                block[pl.ds(0, 2 * rows), :],
                (((1,), (1,)), ((), ())),
                preferred_element_type=jnp.float32,
            )
            masked = raw.reshape(heads, rows, 2 * rows) + bias[None]
            scores[j] = masked
            top[...] = jnp.maximum(
                top[...], jnp.maximum(masked[:, :, :rows], masked[:, :, rows:])
            )

    top[...] = jnp.broadcast_to(jnp.max(top[...], axis=-1, keepdims=True), top.shape)
    factor = math.log2(math.e) / math.sqrt(head_dim)
    for j, block in enumerate(blocks):
        owners = owner_ref[2 * j], owner_ref[2 * j + 1]

        @pl.when(needed(owners[0]) | needed(owners[1]))
        def _():
            weights = jnp.exp2((scores[j] - jnp.concatenate([top[...]] * 2, axis=2)) * factor)
            total[...] += weights[:, :, :rows] + weights[:, :, rows:]
            summed[...] += jnp.dot(
                weights.astype(jnp.bfloat16).reshape(heads * rows, 2 * rows),
                block[pl.ds(2 * rows, 2 * rows), :],
                preferred_element_type=jnp.float32,
            ).reshape(heads, rows, head_dim)

    mixed = (summed[...] / jnp.sum(total[...], axis=-1, keepdims=True)).astype(jnp.bfloat16)
    mixed = jnp.concatenate([mixed[head] for head in range(heads)], axis=1)
    projected = jnp.dot(mixed, weight_ref[...], preferred_element_type=jnp.float32)
    residual = (hidden_ref[...].astype(jnp.float32) + projected).astype(jnp.bfloat16)
    residual_ref[...] = residual
    wide = residual.astype(jnp.float32)
    mean_sq = jnp.mean(wide * wide, axis=-1, keepdims=True)
    normed = (wide * lax.rsqrt(mean_sq + 1e-06) * gain_ref[...]).astype(jnp.bfloat16)
    part = rows // CHUNKS
    for chunk in range(CHUNKS):
        chunk_refs[chunk][...] = normed[chunk * part : (chunk + 1) * part]


def attend(owners, pairs, parts, inputs, blocks):
    queries, _, _, hidden, _, _ = inputs
    rows, width = queries.shape
    head_dim = blocks[0].shape[1]
    heads = width // head_dim
    count = owners.shape[0]
    tall = heads * rows * rows * jnp.dtype(jnp.float32).itemsize
    smem = pl.BlockSpec(memory_space=pltpu.SMEM)
    vmem = pl.BlockSpec(memory_space=pltpu.VMEM)
    square = pltpu.VMEM((heads, rows, rows), jnp.float32)
    chunk = jax.ShapeDtypeStruct((rows // CHUNKS, hidden.shape[1]), jnp.bfloat16)
    *chunks, residual = pl.pallas_call(
        functools.partial(attention_kernel, len(blocks), heads, head_dim),
        out_shape=(chunk,) * CHUNKS + (jax.ShapeDtypeStruct(hidden.shape, jnp.bfloat16),),
        in_specs=[smem] * 3 + [vmem] * (len(inputs) + len(blocks)),
        out_specs=(vmem,) * (CHUNKS + 1),
        scratch_shapes=[
            pltpu.VMEM((heads * rows, head_dim), jnp.bfloat16),
            pltpu.VMEM((len(blocks), heads, rows, 2 * rows), jnp.float32),
            square,
            square,
            pltpu.VMEM((heads, rows, head_dim), jnp.float32),
        ],
        compiler_params=pltpu.CompilerParams(vmem_limit_bytes=(count + 3) * tall + 10 * MIB),
        name="attention",
    )(owners, pairs, parts, *(in_vmem(x) for x in inputs), in_vmem(blocks[0]), *blocks[1:])
    return residual, chunks


def load_kernel(count, *refs):
    inputs, outputs, sems = refs[:count], refs[count : 2 * count], refs[2 * count]
    moves = [pltpu.make_async_copy(inputs[k], outputs[k], sems.at[k]) for k in range(count)]
    for move in moves:
        move.start()
    for move in moves:
        move.wait()


def load(*arrays):
    count = len(arrays)
    return pl.pallas_call(
        functools.partial(load_kernel, count),
        out_shape=tuple(pltpu.VMEM(x.shape, x.dtype) for x in arrays),
        in_specs=[pl.BlockSpec(memory_space=pl.ANY)] * count,
        out_specs=(pl.BlockSpec(memory_space=pltpu.VMEM),) * count,
        scratch_shapes=[pltpu.SemaphoreType.DMA((count,))],
        compiler_params=pltpu.CompilerParams(vmem_limit_bytes=2 * MIB),
        name="load",
    )(*arrays)


def join_kernel(count, *refs):
    inputs, both_ref, sems = refs[: 2 * count], refs[2 * count], refs[2 * count + 1]
    rows = inputs[0].shape[0]
    moves = []
    for k in range(2 * count):
        owner, kind = divmod(k, count)
        place = pl.ds((kind * 2 + owner) * rows, rows)
        moves.append(pltpu.make_async_copy(inputs[k], both_ref.at[place, :], sems.at[k]))
    for move in moves:
        move.start()
    for move in moves:
        move.wait()


def join(own, mate):
    count = len(own)
    rows, width = own[0].shape
    return pl.pallas_call(
        functools.partial(join_kernel, count),
        out_shape=pltpu.VMEM((2 * count * rows, width), own[0].dtype),
        in_specs=[pl.BlockSpec(memory_space=pl.ANY)] * count
        + [pl.BlockSpec(memory_space=pltpu.VMEM)] * count,
        out_specs=pl.BlockSpec(memory_space=pltpu.VMEM),
        scratch_shapes=[pltpu.SemaphoreType.DMA((2 * count,))],
        name="join",
    )(*own, *mate)


def ffn_kernel(blocks, *refs):
    inputs, refs = refs[:blocks], refs[blocks:]
    weights, refs = refs[:6], refs[6:]
    outputs, refs = refs[:blocks], refs[blocks:]
    turned, inner, total = refs
    part = inputs[0].shape[0]
    turned[...] = jnp.concatenate([ref[...] for ref in inputs], axis=0).T
    for side in range(2):
        gate, up, down = weights[3 * side : 3 * side + 3]
        gate_out = jnp.dot(gate[...], turned[...], preferred_element_type=jnp.float32)
        up_out = jnp.dot(up[...], turned[...], preferred_element_type=jnp.float32)
        inner[...] = (gate_out / (1.0 + jnp.exp(-gate_out)) * up_out).astype(jnp.bfloat16)
        term = jnp.dot(inner[...].T, down[...], preferred_element_type=jnp.float32)
        if side == 0:
            total[...] = term
        else:
            term = (term + total[...]).astype(jnp.bfloat16)
            for k in range(blocks):
                outputs[k][...] = term[k * part : (k + 1) * part]


def ffn(blocks, weights):
    count = len(blocks)
    rows, width = blocks[0].shape
    hidden = weights[0].shape[0]
    vmem = pl.BlockSpec(memory_space=pltpu.VMEM)
    return pl.pallas_call(
        functools.partial(ffn_kernel, count),
        out_shape=tuple(jax.ShapeDtypeStruct(b.shape, jnp.bfloat16) for b in blocks),
        in_specs=[vmem] * (count + 6),
        out_specs=(vmem,) * count,
        scratch_shapes=[
            pltpu.VMEM((width, count * rows), jnp.bfloat16),
            pltpu.VMEM((hidden, count * rows), jnp.bfloat16),
            pltpu.VMEM((count * rows, width), jnp.float32),
        ],
        compiler_params=pltpu.CompilerParams(vmem_limit_bytes=16 * MIB),
        cost_estimate=pl.CostEstimate(flops=1000, transcendentals=0, bytes_accessed=1000),
        name="feed_forward",
    )(*blocks, *(in_vmem(w) for w in weights))


def feed_forward(ring, chunks, own, mates):
    half = ring.half

    def send(pair, way):
        return ring.go(pair[0], way), ring.go(pair[1], -way)

    chunks, own, mates = lax.optimization_barrier((chunks, own, mates))
    held = [[(chunks[0], chunks[1])], [(chunks[1], chunks[0])]]
    terms = [{}, {}]
    for group in range(2):
        held[group].append(send(held[group][0], 1))
    weights = load(*(in_hbm(w) for w in own)) + load(*mates)
    weights, held[0][1] = hold(weights, held[0][1])
    for step in range(1, half):
        held[0].append(send(held[0][step], 1))
        older = held[1][step - 1] if step > 1 else held[0][0]
        done = ffn(held[0][step] + older, weights)
        if step + 1 < half:
            done, pair = hold(done, held[1][step])
            held[1].append(send(pair, 1))
        terms[0][step], terms[1][step - 1] = done[:2], done[2:]
    older = held[1][half - 1] if half > 1 else held[0][0]
    if half > 1:
        done, older = hold(done, older)
        terms[0][half - 1], terms[1][half - 2] = done[:2], done[2:]
    done = ffn(held[0][half] + older, weights)
    terms[0][half], terms[1][half - 1] = done[:2], done[2:]

    def add(a, b):
        return (a.astype(jnp.float32) + b.astype(jnp.float32)).astype(jnp.bfloat16)

    home = [None, None]
    for step in range(half, 0, -1):
        for group in range(2):
            place = step - group
            if place == 0:
                continue
            pair = terms[group][place]
            if home[group] is not None:
                pair = (add(home[group][0], pair[0]), add(home[group][1], pair[1]))
            home[group] = send(pair, -1)
    sums = [[x.astype(jnp.float32) for x in terms[1][0]]]
    if home[1] is not None:
        sums.append([x.astype(jnp.float32) for x in home[1][::-1]])
    sums.append([x.astype(jnp.float32) for x in home[0]])
    return [sum(x[k] for x in sums) for k in range(2)]


def gather_kv(ring, keys, values, weights, extras):
    half = ring.half
    gate, up, down = weights
    both = join(
        (in_hbm(keys), in_hbm(values)), (in_vmem(ring.go_mate(keys)), in_vmem(ring.go_mate(values)))
    )
    gate, up, both = lax.optimization_barrier((gate, up, both))
    gate_mate, up_mate = ring.go_mate(gate), ring.go_mate(up)
    held, mates = {0: both}, {}
    reach = 0
    while reach < half:
        fresh = range(reach + 1, min(reach + 2, half) + 1)
        for hops in fresh:
            jump = min(2, hops)
            held[hops] = ring.go_split(held[hops - jump], jump)
        for hops in range(max(1, reach - 1), reach + 1):
            mates[hops] = ring.go_mate(held[hops])
        held, mates, extras = lax.optimization_barrier((held, mates, extras))
        reach = fresh[-1]
    for hops in range(1, half):
        if hops not in mates:
            mates[hops] = ring.go_mate(held[hops])
    gate_mate, up_mate, down, held, mates = lax.optimization_barrier(
        (gate_mate, up_mate, down, held, mates)
    )
    down_mate = ring.go_mate(down)
    blocks = tuple(held[hops] for hops in range(half + 1))
    blocks += tuple(mates[hops] for hops in range(1, half))
    return blocks, (gate_mate, up_mate, down_mate), extras


def block_owners(ring):
    half = ring.half
    owners = [ring.owners([(-hops, hops)]) for hops in range(half + 1)]
    owners += [ring.owners([(hops, -hops)], True) for hops in range(1, half)]
    return np.concatenate(owners, axis=1)


def on_device(
    ring,
    hidden_in,
    queries,
    keys,
    values,
    out_weight,
    norm_gain,
    gate_weight,
    up_weight,
    down_weight,
    pair_ids,
    roles,
    send_rows,
    send_counts,
):
    my_index = lax.axis_index("ctx")
    tok_rows = hidden_in.shape[0]
    own = (gate_weight.T, up_weight.T, down_weight)
    owners = jnp.asarray(block_owners(ring))[my_index]
    pairs = pair_ids.reshape(-1, tok_rows)
    parts = roles.reshape(-1, tok_rows)
    my_roles = lax.dynamic_slice_in_dim(roles, my_index * tok_rows, tok_rows)
    live = (my_roles != 0).astype(jnp.float32)
    inputs = load(
        *(in_hbm(x) for x in (queries, pairs, parts, hidden_in, norm_gain.reshape(1, -1), out_weight))
    )
    blocks, mates, extras = gather_kv(ring, keys, values, own, (owners, live, inputs))
    owners, live, inputs = extras
    residual, chunks = attend(owners, pairs, parts, inputs, blocks)
    summed = feed_forward(ring, chunks, own, mates)
    ffn_back = jnp.concatenate(summed, axis=0).astype(jnp.bfloat16).astype(jnp.float32)
    return (residual.astype(jnp.float32) + ffn_back * live[:, None]).astype(jnp.bfloat16)


def solution(mesh):
    ring = Ring(mesh.shape["groups"], mesh.shape["ctx"])

    def run(*arrays):
        return on_device(ring, *arrays)

    return jax.shard_map(
        run,
        mesh=mesh,
        in_specs=(
            P(("groups", "ctx"), None),
            P(("groups", "ctx"), None),
            P(("groups", "ctx"), None),
            P(("groups", "ctx"), None),
            P(),
            P(),
            P(None, "ctx"),
            P(None, "ctx"),
            P("ctx", None),
            P("groups"),
            P("groups"),
            P(("groups", "ctx"), None),
            P("groups", None),
        ),
        out_specs=P(("groups", "ctx"), None),
        check_vma=False,
    )
```

```python
import functools
import math

import jax
import jax.numpy as jnp
import numpy as np
from jax import lax
from jax.experimental import pallas as pl
from jax.experimental.pallas import tpu as pltpu
from jax.sharding import PartitionSpec as P

NEG_FILL = -1e30
CORES = 2
PLANE = 4
MIB = 1 << 20
CHUNKS = 2


def in_hbm(x):
    return pltpu.with_memory_space_constraint(x, pltpu.HBM)


def in_vmem(x):
    return pltpu.with_memory_space_constraint(x, pltpu.VMEM)


def hold(first, then):
    return lax.optimization_barrier((first, then))


class Ring:
    def __init__(self, groups, devices):
        chips = devices // CORES
        columns = max(1, PLANE // groups)
        if chips % columns:
            columns = 1
        depth = chips // columns
        order = []
        for column in range(columns):
            line = [level * columns + column for level in range(depth)]
            order += line if column % 2 == 0 else line[::-1]
        self.chips = chips
        self.half = chips // 2
        self.order = order
        self.swap = [(i, i ^ 1) for i in range(devices)]

    def go(self, block, hops):
        pairs = []
        for place in range(self.chips):
            here, there = self.order[place], self.order[(place + hops) % self.chips]
            pairs += [(here * CORES + core, there * CORES + core) for core in range(CORES)]
        return lax.ppermute(block, "ctx", pairs)

    def go_mate(self, block):
        return lax.ppermute(block, "ctx", self.swap)

    def go_split(self, block, hops):
        pairs = []
        for place in range(self.chips):
            for core, way in ((0, hops), (1, -hops)):
                here, there = self.order[place], self.order[(place + way) % self.chips]
                pairs.append((here * CORES + core, there * CORES + core))
        return lax.ppermute(block, "ctx", pairs)

    def owners(self, spots, swapped=False):
        place_of = {chip: place for place, chip in enumerate(self.order)}
        table = []
        for device in range(self.chips * CORES):
            chip, core = divmod(device, CORES)
            row = []
            for spot in spots:
                first = self.order[(place_of[chip] + spot[core]) % self.chips] * CORES + core
                row += [first ^ 1, first] if swapped else [first, first ^ 1]
            table.append(row)
        return np.asarray(table, np.int32)


def attention_kernel(
    pieces,
    heads,
    head_dim,
    owner_ref,
    pair_smem,
    role_smem,
    query_ref,
    pair_ref,
    role_ref,
    hidden_ref,
    gain_ref,
    weight_ref,
    *refs,
):
    blocks, refs = refs[:pieces], refs[pieces:]
    chunk_refs, refs = refs[:CHUNKS], refs[CHUNKS:]
    (residual_ref, stacked, scores, top, total, summed) = refs
    rows = query_ref.shape[0]
    me = owner_ref[0]
    for head in range(heads):
        stacked[pl.ds(head * rows, rows), :] = query_ref[:, head * head_dim : (head + 1) * head_dim]

    def column(ref):
        return jnp.broadcast_to(ref[pl.ds(me, 1), :], (rows, rows)).T

    query_pair, query_role = column(pair_ref), column(role_ref)
    query_pos = me * rows + lax.broadcasted_iota(jnp.int32, (rows, rows), 0)
    key_off = lax.broadcasted_iota(jnp.int32, (rows, rows), 1)

    def needed(owner):
        first_pair, last_pair = pair_smem[owner, 0], pair_smem[owner, rows - 1]
        first_role, last_role = role_smem[owner, 0], role_smem[owner, rows - 1]
        my_first, my_last = pair_smem[me, 0], pair_smem[me, rows - 1]
        my_role = role_smem[me, 0]
        apart = (
            (first_pair == last_pair)
            & (my_first == my_last)
            & (first_role == last_role)
            & (my_role == role_smem[me, rows - 1])
            & (first_role != 0)
            & (first_role != my_role)
        )
        return (owner <= me) & (last_pair >= my_first) & jnp.logical_not(apart)

    def bias_of(owner):
        key_role = role_ref[pl.ds(owner, 1), :]
        seen = (
            (query_pair == pair_ref[pl.ds(owner, 1), :])
            & (owner * rows + key_off <= query_pos)
            & ((key_role == 0) | (key_role == query_role))
        )
        return jnp.where(seen, 0.0, NEG_FILL)

    top[...] = jnp.full_like(top, NEG_FILL)
    total[...] = jnp.zeros_like(total)
    summed[...] = jnp.zeros_like(summed)
    for j, block in enumerate(blocks):
        owners = owner_ref[2 * j], owner_ref[2 * j + 1]

        @pl.when(needed(owners[0]) | needed(owners[1]))
        def _():
            bias = jnp.concatenate([bias_of(owner) for owner in owners], axis=1)
            raw = lax.dot_general(
                stacked[...],
                block[pl.ds(0, 2 * rows), :],
                (((1,), (1,)), ((), ())),
                preferred_element_type=jnp.float32,
            )
            masked = raw.reshape(heads, rows, 2 * rows) + bias[None]
            scores[j] = masked
            top[...] = jnp.maximum(
                top[...], jnp.maximum(masked[:, :, :rows], masked[:, :, rows:])
            )

    top[...] = jnp.broadcast_to(jnp.max(top[...], axis=-1, keepdims=True), top.shape)
    factor = math.log2(math.e) / math.sqrt(head_dim)
    for j, block in enumerate(blocks):
        owners = owner_ref[2 * j], owner_ref[2 * j + 1]

        @pl.when(needed(owners[0]) | needed(owners[1]))
        def _():
            weights = jnp.exp2((scores[j] - jnp.concatenate([top[...]] * 2, axis=2)) * factor)
            total[...] += weights[:, :, :rows] + weights[:, :, rows:]
            summed[...] += jnp.dot(
                weights.astype(jnp.bfloat16).reshape(heads * rows, 2 * rows),
                block[pl.ds(2 * rows, 2 * rows), :],
                preferred_element_type=jnp.float32,
            ).reshape(heads, rows, head_dim)

    mixed = (summed[...] / jnp.sum(total[...], axis=-1, keepdims=True)).astype(jnp.bfloat16)
    mixed = jnp.concatenate([mixed[head] for head in range(heads)], axis=1)
    projected = jnp.dot(mixed, weight_ref[...], preferred_element_type=jnp.float32)
    residual = (hidden_ref[...].astype(jnp.float32) + projected).astype(jnp.bfloat16)
    residual_ref[...] = residual
    wide = residual.astype(jnp.float32)
    mean_sq = jnp.mean(wide * wide, axis=-1, keepdims=True)
    normed = (wide * lax.rsqrt(mean_sq + 1e-06) * gain_ref[...]).astype(jnp.bfloat16)
    part = rows // CHUNKS
    for chunk in range(CHUNKS):
        chunk_refs[chunk][...] = normed[chunk * part : (chunk + 1) * part]


def attend(owners, pairs, parts, inputs, blocks):
    queries, _, _, hidden, _, _ = inputs
    rows, width = queries.shape
    head_dim = blocks[0].shape[1]
    heads = width // head_dim
    count = owners.shape[0]
    tall = heads * rows * rows * jnp.dtype(jnp.float32).itemsize
    smem = pl.BlockSpec(memory_space=pltpu.SMEM)
    vmem = pl.BlockSpec(memory_space=pltpu.VMEM)
    square = pltpu.VMEM((heads, rows, rows), jnp.float32)
    chunk = jax.ShapeDtypeStruct((rows // CHUNKS, hidden.shape[1]), jnp.bfloat16)
    *chunks, residual = pl.pallas_call(
        functools.partial(attention_kernel, len(blocks), heads, head_dim),
        out_shape=(chunk,) * CHUNKS + (jax.ShapeDtypeStruct(hidden.shape, jnp.bfloat16),),
        in_specs=[smem] * 3 + [vmem] * (len(inputs) + len(blocks)),
        out_specs=(vmem,) * (CHUNKS + 1),
        scratch_shapes=[
            pltpu.VMEM((heads * rows, head_dim), jnp.bfloat16),
            pltpu.VMEM((len(blocks), heads, rows, 2 * rows), jnp.float32),
            square,
            square,
            pltpu.VMEM((heads, rows, head_dim), jnp.float32),
        ],
        compiler_params=pltpu.CompilerParams(vmem_limit_bytes=(count + 3) * tall + 10 * MIB),
        name="attention",
    )(owners, pairs, parts, *(in_vmem(x) for x in inputs), in_vmem(blocks[0]), *blocks[1:])
    return residual, chunks


def load_kernel(count, *refs):
    inputs, outputs, sems = refs[:count], refs[count : 2 * count], refs[2 * count]
    moves = [pltpu.make_async_copy(inputs[k], outputs[k], sems.at[k]) for k in range(count)]
    for move in moves:
        move.start()
    for move in moves:
        move.wait()


def load(*arrays):
    count = len(arrays)
    return pl.pallas_call(
        functools.partial(load_kernel, count),
        out_shape=tuple(pltpu.VMEM(x.shape, x.dtype) for x in arrays),
        in_specs=[pl.BlockSpec(memory_space=pl.ANY)] * count,
        out_specs=(pl.BlockSpec(memory_space=pltpu.VMEM),) * count,
        scratch_shapes=[pltpu.SemaphoreType.DMA((count,))],
        compiler_params=pltpu.CompilerParams(vmem_limit_bytes=2 * MIB),
        name="load",
    )(*arrays)


def join_kernel(count, *refs):
    inputs, both_ref, sems = refs[: 2 * count], refs[2 * count], refs[2 * count + 1]
    rows = inputs[0].shape[0]
    moves = []
    for k in range(2 * count):
        owner, kind = divmod(k, count)
        place = pl.ds((kind * 2 + owner) * rows, rows)
        moves.append(pltpu.make_async_copy(inputs[k], both_ref.at[place, :], sems.at[k]))
    for move in moves:
        move.start()
    for move in moves:
        move.wait()


def join(own, mate):
    count = len(own)
    rows, width = own[0].shape
    return pl.pallas_call(
        functools.partial(join_kernel, count),
        out_shape=pltpu.VMEM((2 * count * rows, width), own[0].dtype),
        in_specs=[pl.BlockSpec(memory_space=pl.ANY)] * count
        + [pl.BlockSpec(memory_space=pltpu.VMEM)] * count,
        out_specs=pl.BlockSpec(memory_space=pltpu.VMEM),
        scratch_shapes=[pltpu.SemaphoreType.DMA((2 * count,))],
        name="join",
    )(*own, *mate)


def ffn_kernel(blocks, *refs):
    inputs, refs = refs[:blocks], refs[blocks:]
    weights, refs = refs[:6], refs[6:]
    outputs, refs = refs[:blocks], refs[blocks:]
    turned, inner, total = refs
    part = inputs[0].shape[0]
    turned[...] = jnp.concatenate([ref[...] for ref in inputs], axis=0).T
    for side in range(2):
        gate, up, down = weights[3 * side : 3 * side + 3]
        gate_out = jnp.dot(gate[...], turned[...], preferred_element_type=jnp.float32)
        up_out = jnp.dot(up[...], turned[...], preferred_element_type=jnp.float32)
        inner[...] = (gate_out / (1.0 + jnp.exp(-gate_out)) * up_out).astype(jnp.bfloat16)
        term = jnp.dot(inner[...].T, down[...], preferred_element_type=jnp.float32)
        if side == 0:
            total[...] = term
        else:
            term = (term + total[...]).astype(jnp.bfloat16)
            for k in range(blocks):
                outputs[k][...] = term[k * part : (k + 1) * part]


def ffn(blocks, weights):
    count = len(blocks)
    rows, width = blocks[0].shape
    hidden = weights[0].shape[0]
    vmem = pl.BlockSpec(memory_space=pltpu.VMEM)
    return pl.pallas_call(
        functools.partial(ffn_kernel, count),
        out_shape=tuple(jax.ShapeDtypeStruct(b.shape, jnp.bfloat16) for b in blocks),
        in_specs=[vmem] * (count + 6),
        out_specs=(vmem,) * count,
        scratch_shapes=[
            pltpu.VMEM((width, count * rows), jnp.bfloat16),
            pltpu.VMEM((hidden, count * rows), jnp.bfloat16),
            pltpu.VMEM((count * rows, width), jnp.float32),
        ],
        compiler_params=pltpu.CompilerParams(vmem_limit_bytes=16 * MIB),
        cost_estimate=pl.CostEstimate(flops=1000, transcendentals=0, bytes_accessed=1000),
        name="feed_forward",
    )(*blocks, *(in_vmem(w) for w in weights))


def feed_forward(ring, chunks, own, mates):
    half = ring.half

    def send(pair, way):
        return ring.go(pair[0], way), ring.go(pair[1], -way)

    chunks, own, mates = lax.optimization_barrier((chunks, own, mates))
    held = [[(chunks[0], chunks[1])], [(chunks[1], chunks[0])]]
    terms = [{}, {}]
    for group in range(2):
        held[group].append(send(held[group][0], 1))
    weights = load(*(in_hbm(w) for w in own)) + load(*mates)
    weights, held[0][1] = hold(weights, held[0][1])
    for step in range(1, half):
        held[0].append(send(held[0][step], 1))
        older = held[1][step - 1] if step > 1 else held[0][0]
        done = ffn(held[0][step] + older, weights)
        if step + 1 < half:
            done, pair = hold(done, held[1][step])
            held[1].append(send(pair, 1))
        terms[0][step], terms[1][step - 1] = done[:2], done[2:]
    older = held[1][half - 1] if half > 1 else held[0][0]
    if half > 1:
        done, older = hold(done, older)
        terms[0][half - 1], terms[1][half - 2] = done[:2], done[2:]
    done, far = hold(ffn(older, weights), held[0][half])
    terms[1][half - 1] = done
    terms[0][half] = ffn(far, weights)

    def add(a, b):
        return (a.astype(jnp.float32) + b.astype(jnp.float32)).astype(jnp.bfloat16)

    home = [None, None]
    for step in range(half, 0, -1):
        for group in range(2):
            place = step - group
            if place == 0:
                continue
            pair = terms[group][place]
            if home[group] is not None:
                pair = (add(home[group][0], pair[0]), add(home[group][1], pair[1]))
            home[group] = send(pair, -1)
    sums = [[x.astype(jnp.float32) for x in terms[1][0]]]
    if home[1] is not None:
        sums.append([x.astype(jnp.float32) for x in home[1][::-1]])
    sums.append([x.astype(jnp.float32) for x in home[0]])
    return [sum(x[k] for x in sums) for k in range(2)]


def gather_kv(ring, keys, values, weights, extras):
    half = ring.half
    gate, up, down = weights
    both = join(
        (in_hbm(keys), in_hbm(values)), (in_vmem(ring.go_mate(keys)), in_vmem(ring.go_mate(values)))
    )
    gate, up, both = lax.optimization_barrier((gate, up, both))
    gate_mate, up_mate = ring.go_mate(gate), ring.go_mate(up)
    held, mates = {0: both}, {}
    reach = 0
    while reach < half:
        fresh = range(reach + 1, min(reach + 2, half) + 1)
        for hops in fresh:
            jump = min(2, hops)
            held[hops] = ring.go_split(held[hops - jump], jump)
        for hops in range(max(1, reach - 1), reach + 1):
            mates[hops] = ring.go_mate(held[hops])
        held, mates, extras = lax.optimization_barrier((held, mates, extras))
        if reach == 0:
            gate_mate, up_mate, down, held = lax.optimization_barrier(
                (gate_mate, up_mate, down, held)
            )
            down_mate = ring.go_mate(down)
        reach = fresh[-1]
    for hops in range(1, half):
        if hops not in mates:
            mates[hops] = ring.go_mate(held[hops])
    blocks = tuple(held[hops] for hops in range(half + 1))
    blocks += tuple(mates[hops] for hops in range(1, half))
    return blocks, (gate_mate, up_mate, down_mate), extras


def block_owners(ring):
    half = ring.half
    owners = [ring.owners([(-hops, hops)]) for hops in range(half + 1)]
    owners += [ring.owners([(hops, -hops)], True) for hops in range(1, half)]
    return np.concatenate(owners, axis=1)


def on_device(
    ring,
    hidden_in,
    queries,
    keys,
    values,
    out_weight,
    norm_gain,
    gate_weight,
    up_weight,
    down_weight,
    pair_ids,
    roles,
    send_rows,
    send_counts,
):
    my_index = lax.axis_index("ctx")
    tok_rows = hidden_in.shape[0]
    own = (gate_weight.T, up_weight.T, down_weight)
    owners = jnp.asarray(block_owners(ring))[my_index]
    pairs = pair_ids.reshape(-1, tok_rows)
    parts = roles.reshape(-1, tok_rows)
    my_roles = lax.dynamic_slice_in_dim(roles, my_index * tok_rows, tok_rows)
    live = (my_roles != 0).astype(jnp.float32)
    inputs = load(
        *(in_hbm(x) for x in (queries, pairs, parts, hidden_in, norm_gain.reshape(1, -1), out_weight))
    )
    blocks, mates, extras = gather_kv(ring, keys, values, own, (owners, live, inputs))
    owners, live, inputs = extras
    residual, chunks = attend(owners, pairs, parts, inputs, blocks)
    summed = feed_forward(ring, chunks, own, mates)
    ffn_back = jnp.concatenate(summed, axis=0).astype(jnp.bfloat16).astype(jnp.float32)
    return (residual.astype(jnp.float32) + ffn_back * live[:, None]).astype(jnp.bfloat16)


def solution(mesh):
    ring = Ring(mesh.shape["groups"], mesh.shape["ctx"])

    def run(*arrays):
        return on_device(ring, *arrays)

    return jax.shard_map(
        run,
        mesh=mesh,
        in_specs=(
            P(("groups", "ctx"), None),
            P(("groups", "ctx"), None),
            P(("groups", "ctx"), None),
            P(("groups", "ctx"), None),
            P(),
            P(),
            P(None, "ctx"),
            P(None, "ctx"),
            P("ctx", None),
            P("groups"),
            P("groups"),
            P(("groups", "ctx"), None),
            P("groups", None),
        ),
        out_specs=P(("groups", "ctx"), None),
        check_vma=False,
    )
```

```python
import functools
import math

import jax
import jax.numpy as jnp
import numpy as np
from jax import lax
from jax.experimental import pallas as pl
from jax.experimental.pallas import tpu as pltpu
from jax.sharding import PartitionSpec as P

NEG_FILL = -1e30
CORES = 2
PLANE = 4
MIB = 1 << 20
CHUNKS = 2


def in_hbm(x):
    return pltpu.with_memory_space_constraint(x, pltpu.HBM)


def in_vmem(x):
    return pltpu.with_memory_space_constraint(x, pltpu.VMEM)


def hold(first, then):
    return lax.optimization_barrier((first, then))


class Ring:
    def __init__(self, groups, devices):
        chips = devices // CORES
        columns = max(1, PLANE // groups)
        if chips % columns:
            columns = 1
        depth = chips // columns
        order = []
        for column in range(columns):
            line = [level * columns + column for level in range(depth)]
            order += line if column % 2 == 0 else line[::-1]
        self.chips = chips
        self.half = chips // 2
        self.order = order
        self.swap = [(i, i ^ 1) for i in range(devices)]

    def go(self, block, hops):
        pairs = []
        for place in range(self.chips):
            here, there = self.order[place], self.order[(place + hops) % self.chips]
            pairs += [(here * CORES + core, there * CORES + core) for core in range(CORES)]
        return lax.ppermute(block, "ctx", pairs)

    def go_mate(self, block):
        return lax.ppermute(block, "ctx", self.swap)

    def go_split(self, block, hops):
        pairs = []
        for place in range(self.chips):
            for core, way in ((0, hops), (1, -hops)):
                here, there = self.order[place], self.order[(place + way) % self.chips]
                pairs.append((here * CORES + core, there * CORES + core))
        return lax.ppermute(block, "ctx", pairs)

    def owners(self, spots, swapped=False):
        place_of = {chip: place for place, chip in enumerate(self.order)}
        table = []
        for device in range(self.chips * CORES):
            chip, core = divmod(device, CORES)
            row = []
            for spot in spots:
                first = self.order[(place_of[chip] + spot[core]) % self.chips] * CORES + core
                row += [first ^ 1, first] if swapped else [first, first ^ 1]
            table.append(row)
        return np.asarray(table, np.int32)


def attention_kernel(
    pieces,
    heads,
    head_dim,
    owner_ref,
    pair_smem,
    role_smem,
    query_ref,
    pair_ref,
    role_ref,
    hidden_ref,
    gain_ref,
    weight_ref,
    *refs,
):
    blocks, refs = refs[:pieces], refs[pieces:]
    chunk_refs, refs = refs[:CHUNKS], refs[CHUNKS:]
    (residual_ref, stacked, scores, top, total, summed) = refs
    rows = query_ref.shape[0]
    me = owner_ref[0]
    for head in range(heads):
        stacked[pl.ds(head * rows, rows), :] = query_ref[:, head * head_dim : (head + 1) * head_dim]

    def column(ref):
        return jnp.broadcast_to(ref[pl.ds(me, 1), :], (rows, rows)).T

    query_pair, query_role = column(pair_ref), column(role_ref)
    query_pos = me * rows + lax.broadcasted_iota(jnp.int32, (rows, rows), 0)
    key_off = lax.broadcasted_iota(jnp.int32, (rows, rows), 1)

    def needed(owner):
        first_pair, last_pair = pair_smem[owner, 0], pair_smem[owner, rows - 1]
        first_role, last_role = role_smem[owner, 0], role_smem[owner, rows - 1]
        my_first, my_last = pair_smem[me, 0], pair_smem[me, rows - 1]
        my_role = role_smem[me, 0]
        apart = (
            (first_pair == last_pair)
            & (my_first == my_last)
            & (first_role == last_role)
            & (my_role == role_smem[me, rows - 1])
            & (first_role != 0)
            & (first_role != my_role)
        )
        return (owner <= me) & (last_pair >= my_first) & jnp.logical_not(apart)

    def bias_of(owner):
        key_role = role_ref[pl.ds(owner, 1), :]
        seen = (
            (query_pair == pair_ref[pl.ds(owner, 1), :])
            & (owner * rows + key_off <= query_pos)
            & ((key_role == 0) | (key_role == query_role))
        )
        return jnp.where(seen, 0.0, NEG_FILL)

    top[...] = jnp.full_like(top, NEG_FILL)
    total[...] = jnp.zeros_like(total)
    summed[...] = jnp.zeros_like(summed)
    for j, block in enumerate(blocks):
        owners = owner_ref[2 * j], owner_ref[2 * j + 1]

        @pl.when(needed(owners[0]) | needed(owners[1]))
        def _():
            bias = jnp.concatenate([bias_of(owner) for owner in owners], axis=1)
            raw = lax.dot_general(
                stacked[...],
                block[pl.ds(0, 2 * rows), :],
                (((1,), (1,)), ((), ())),
                preferred_element_type=jnp.float32,
            )
            masked = raw.reshape(heads, rows, 2 * rows) + bias[None]
            scores[j] = masked
            top[...] = jnp.maximum(
                top[...], jnp.maximum(masked[:, :, :rows], masked[:, :, rows:])
            )

    top[...] = jnp.broadcast_to(jnp.max(top[...], axis=-1, keepdims=True), top.shape)
    factor = math.log2(math.e) / math.sqrt(head_dim)
    for j, block in enumerate(blocks):
        owners = owner_ref[2 * j], owner_ref[2 * j + 1]

        @pl.when(needed(owners[0]) | needed(owners[1]))
        def _():
            weights = jnp.exp2((scores[j] - jnp.concatenate([top[...]] * 2, axis=2)) * factor)
            total[...] += weights[:, :, :rows] + weights[:, :, rows:]
            summed[...] += jnp.dot(
                weights.astype(jnp.bfloat16).reshape(heads * rows, 2 * rows),
                block[pl.ds(2 * rows, 2 * rows), :],
                preferred_element_type=jnp.float32,
            ).reshape(heads, rows, head_dim)

    mixed = (summed[...] / jnp.sum(total[...], axis=-1, keepdims=True)).astype(jnp.bfloat16)
    mixed = jnp.concatenate([mixed[head] for head in range(heads)], axis=1)
    projected = jnp.dot(mixed, weight_ref[...], preferred_element_type=jnp.float32)
    residual = (hidden_ref[...].astype(jnp.float32) + projected).astype(jnp.bfloat16)
    residual_ref[...] = residual
    wide = residual.astype(jnp.float32)
    mean_sq = jnp.mean(wide * wide, axis=-1, keepdims=True)
    normed = (wide * lax.rsqrt(mean_sq + 1e-06) * gain_ref[...]).astype(jnp.bfloat16)
    part = rows // CHUNKS
    for chunk in range(CHUNKS):
        chunk_refs[chunk][...] = normed[chunk * part : (chunk + 1) * part]


def attend(owners, pairs, parts, inputs, blocks):
    queries, _, _, hidden, _, _ = inputs
    rows, width = queries.shape
    head_dim = blocks[0].shape[1]
    heads = width // head_dim
    count = owners.shape[0]
    tall = heads * rows * rows * jnp.dtype(jnp.float32).itemsize
    smem = pl.BlockSpec(memory_space=pltpu.SMEM)
    vmem = pl.BlockSpec(memory_space=pltpu.VMEM)
    square = pltpu.VMEM((heads, rows, rows), jnp.float32)
    chunk = jax.ShapeDtypeStruct((rows // CHUNKS, hidden.shape[1]), jnp.bfloat16)
    *chunks, residual = pl.pallas_call(
        functools.partial(attention_kernel, len(blocks), heads, head_dim),
        out_shape=(chunk,) * CHUNKS + (jax.ShapeDtypeStruct(hidden.shape, jnp.bfloat16),),
        in_specs=[smem] * 3 + [vmem] * (len(inputs) + len(blocks)),
        out_specs=(vmem,) * (CHUNKS + 1),
        scratch_shapes=[
            pltpu.VMEM((heads * rows, head_dim), jnp.bfloat16),
            pltpu.VMEM((len(blocks), heads, rows, 2 * rows), jnp.float32),
            square,
            square,
            pltpu.VMEM((heads, rows, head_dim), jnp.float32),
        ],
        compiler_params=pltpu.CompilerParams(vmem_limit_bytes=(count + 3) * tall + 10 * MIB),
        name="attention",
    )(owners, pairs, parts, *(in_vmem(x) for x in inputs), in_vmem(blocks[0]), *blocks[1:])
    return residual, chunks


def load_kernel(count, *refs):
    inputs, outputs, sems = refs[:count], refs[count : 2 * count], refs[2 * count]
    moves = [pltpu.make_async_copy(inputs[k], outputs[k], sems.at[k]) for k in range(count)]
    for move in moves:
        move.start()
    for move in moves:
        move.wait()


def load(*arrays):
    count = len(arrays)
    return pl.pallas_call(
        functools.partial(load_kernel, count),
        out_shape=tuple(pltpu.VMEM(x.shape, x.dtype) for x in arrays),
        in_specs=[pl.BlockSpec(memory_space=pl.ANY)] * count,
        out_specs=(pl.BlockSpec(memory_space=pltpu.VMEM),) * count,
        scratch_shapes=[pltpu.SemaphoreType.DMA((count,))],
        compiler_params=pltpu.CompilerParams(vmem_limit_bytes=2 * MIB),
        name="load",
    )(*arrays)


def join_kernel(count, *refs):
    inputs, both_ref, sems = refs[: 2 * count], refs[2 * count], refs[2 * count + 1]
    rows = inputs[0].shape[0]
    moves = []
    for k in range(2 * count):
        owner, kind = divmod(k, count)
        place = pl.ds((kind * 2 + owner) * rows, rows)
        moves.append(pltpu.make_async_copy(inputs[k], both_ref.at[place, :], sems.at[k]))
    for move in moves:
        move.start()
    for move in moves:
        move.wait()


def join(own, mate):
    count = len(own)
    rows, width = own[0].shape
    return pl.pallas_call(
        functools.partial(join_kernel, count),
        out_shape=pltpu.VMEM((2 * count * rows, width), own[0].dtype),
        in_specs=[pl.BlockSpec(memory_space=pl.ANY)] * count
        + [pl.BlockSpec(memory_space=pltpu.VMEM)] * count,
        out_specs=pl.BlockSpec(memory_space=pltpu.VMEM),
        scratch_shapes=[pltpu.SemaphoreType.DMA((2 * count,))],
        name="join",
    )(*own, *mate)


def ffn_kernel(blocks, *refs):
    inputs, refs = refs[:blocks], refs[blocks:]
    weights, refs = refs[:6], refs[6:]
    outputs, refs = refs[:blocks], refs[blocks:]
    turned, inner, total = refs
    part = inputs[0].shape[0]
    turned[...] = jnp.concatenate([ref[...] for ref in inputs], axis=0).T
    for side in range(2):
        gate, up, down = weights[3 * side : 3 * side + 3]
        gate_out = jnp.dot(gate[...], turned[...], preferred_element_type=jnp.float32)
        up_out = jnp.dot(up[...], turned[...], preferred_element_type=jnp.float32)
        inner[...] = (gate_out / (1.0 + jnp.exp(-gate_out)) * up_out).astype(jnp.bfloat16)
        term = jnp.dot(inner[...].T, down[...], preferred_element_type=jnp.float32)
        if side == 0:
            total[...] = term
        else:
            term = (term + total[...]).astype(jnp.bfloat16)
            for k in range(blocks):
                outputs[k][...] = term[k * part : (k + 1) * part]


def ffn(blocks, weights):
    count = len(blocks)
    rows, width = blocks[0].shape
    hidden = weights[0].shape[0]
    vmem = pl.BlockSpec(memory_space=pltpu.VMEM)
    return pl.pallas_call(
        functools.partial(ffn_kernel, count),
        out_shape=tuple(jax.ShapeDtypeStruct(b.shape, jnp.bfloat16) for b in blocks),
        in_specs=[vmem] * (count + 6),
        out_specs=(vmem,) * count,
        scratch_shapes=[
            pltpu.VMEM((width, count * rows), jnp.bfloat16),
            pltpu.VMEM((hidden, count * rows), jnp.bfloat16),
            pltpu.VMEM((count * rows, width), jnp.float32),
        ],
        compiler_params=pltpu.CompilerParams(vmem_limit_bytes=16 * MIB),
        cost_estimate=pl.CostEstimate(flops=1000, transcendentals=0, bytes_accessed=1000),
        name="feed_forward",
    )(*blocks, *(in_vmem(w) for w in weights))


def feed_forward(ring, chunks, own, mates):
    half = ring.half

    def send(pair, way):
        return ring.go(pair[0], way), ring.go(pair[1], -way)

    chunks, own, mates = lax.optimization_barrier((chunks, own, mates))
    held = [[(chunks[0], chunks[1])], [(chunks[1], chunks[0])]]
    terms = [{}, {}]
    for group in range(2):
        held[group].append(send(held[group][0], 1))
    weights = load(*(in_hbm(w) for w in own)) + load(*mates)
    weights, held[0][1] = hold(weights, held[0][1])
    for step in range(1, half):
        held[0].append(send(held[0][step], 1))
        older = held[1][step - 1] if step > 1 else held[0][0]
        done = ffn(held[0][step] + older, weights)
        if step + 1 < half:
            done, pair = hold(done, held[1][step])
            held[1].append(send(pair, 1))
        terms[0][step], terms[1][step - 1] = done[:2], done[2:]
    older = held[1][half - 1] if half > 1 else held[0][0]
    if half > 1:
        done, older = hold(done, older)
        terms[0][half - 1], terms[1][half - 2] = done[:2], done[2:]
    done = ffn(held[0][half] + older, weights)
    terms[0][half], terms[1][half - 1] = done[:2], done[2:]

    def add(a, b):
        return (a.astype(jnp.float32) + b.astype(jnp.float32)).astype(jnp.bfloat16)

    home = [None, None]
    for step in range(half, 0, -1):
        for group in range(2):
            place = step - group
            if place == 0:
                continue
            pair = terms[group][place]
            if home[group] is not None:
                pair = (add(home[group][0], pair[0]), add(home[group][1], pair[1]))
            home[group] = send(pair, -1)
    sums = [[x.astype(jnp.float32) for x in terms[1][0]]]
    if home[1] is not None:
        sums.append([x.astype(jnp.float32) for x in home[1][::-1]])
    sums.append([x.astype(jnp.float32) for x in home[0]])
    return [sum(x[k] for x in sums) for k in range(2)]


def gather_kv(ring, keys, values, weights, inputs, live, table):
    half = ring.half
    gate, up, down = weights
    both = join(
        (in_hbm(keys), in_hbm(values)), (in_vmem(ring.go_mate(keys)), in_vmem(ring.go_mate(values)))
    )
    live, gate = hold(live, gate)
    gate_mate = ring.go_mate(gate)
    held, mates, owners = {0: both}, {}, None
    reach = 0
    while reach < half:
        fresh = range(reach + 1, min(reach + 2, half) + 1)
        for hops in fresh:
            jump = min(2, hops)
            held[hops] = ring.go_split(held[hops - jump], jump)
            if hops == half - 1 or half == 1:
                held[hops], up = hold(held[hops], up)
                up_mate = ring.go_mate(up)
        for hops in range(max(1, reach - 1), reach + 1):
            mates[hops] = ring.go_mate(held[hops])
        held, mates, inputs = lax.optimization_barrier((held, mates, inputs))
        if owners is None:
            table, held = hold(table, held)
            owners = lax.dynamic_index_in_dim(table, lax.axis_index("ctx"), keepdims=False)
        reach = fresh[-1]
    for hops in range(1, half):
        if hops not in mates:
            mates[hops] = ring.go_mate(held[hops])
    gate_mate, up_mate, down, held, mates = lax.optimization_barrier(
        (gate_mate, up_mate, down, held, mates)
    )
    down_mate = ring.go_mate(down)
    blocks = tuple(held[hops] for hops in range(half + 1))
    blocks += tuple(mates[hops] for hops in range(1, half))
    return blocks, (gate_mate, up_mate, down_mate), inputs, live, owners


def block_owners(ring):
    half = ring.half
    owners = [ring.owners([(-hops, hops)]) for hops in range(half + 1)]
    owners += [ring.owners([(hops, -hops)], True) for hops in range(1, half)]
    return np.concatenate(owners, axis=1)


def on_device(
    ring,
    hidden_in,
    queries,
    keys,
    values,
    out_weight,
    norm_gain,
    gate_weight,
    up_weight,
    down_weight,
    pair_ids,
    roles,
    send_rows,
    send_counts,
):
    my_index = lax.axis_index("ctx")
    tok_rows = hidden_in.shape[0]
    own = (gate_weight.T, up_weight.T, down_weight)
    pairs = pair_ids.reshape(-1, tok_rows)
    parts = roles.reshape(-1, tok_rows)
    my_roles = lax.dynamic_slice_in_dim(roles, my_index * tok_rows, tok_rows)
    live = (my_roles != 0).astype(jnp.float32)
    inputs = load(
        *(in_hbm(x) for x in (queries, pairs, parts, hidden_in, norm_gain.reshape(1, -1), out_weight))
    )
    blocks, mates, inputs, live, owners = gather_kv(
        ring, keys, values, own, inputs, live, jnp.asarray(block_owners(ring))
    )
    residual, chunks = attend(owners, pairs, parts, inputs, blocks)
    summed = feed_forward(ring, chunks, own, mates)
    ffn_back = jnp.concatenate(summed, axis=0).astype(jnp.bfloat16).astype(jnp.float32)
    return (residual.astype(jnp.float32) + ffn_back * live[:, None]).astype(jnp.bfloat16)


def solution(mesh):
    ring = Ring(mesh.shape["groups"], mesh.shape["ctx"])

    def run(*arrays):
        return on_device(ring, *arrays)

    return jax.shard_map(
        run,
        mesh=mesh,
        in_specs=(
            P(("groups", "ctx"), None),
            P(("groups", "ctx"), None),
            P(("groups", "ctx"), None),
            P(("groups", "ctx"), None),
            P(),
            P(),
            P(None, "ctx"),
            P(None, "ctx"),
            P("ctx", None),
            P("groups"),
            P("groups"),
            P(("groups", "ctx"), None),
            P("groups", None),
        ),
        out_specs=P(("groups", "ctx"), None),
        check_vma=False,
    )
```

```python
import functools
import math

import jax
import jax.numpy as jnp
import numpy as np
from jax import lax
from jax.experimental import pallas as pl
from jax.experimental.pallas import tpu as pltpu
from jax.sharding import PartitionSpec as P

NEG_FILL = -1e30
CORES = 2
PLANE = 4
MIB = 1 << 20
CHUNKS = 2


def in_hbm(x):
    return pltpu.with_memory_space_constraint(x, pltpu.HBM)


def in_vmem(x):
    return pltpu.with_memory_space_constraint(x, pltpu.VMEM)


def hold(first, then):
    return lax.optimization_barrier((first, then))


class Ring:
    def __init__(self, groups, devices):
        chips = devices // CORES
        columns = max(1, PLANE // groups)
        if chips % columns:
            columns = 1
        depth = chips // columns
        order = []
        for column in range(columns):
            line = [level * columns + column for level in range(depth)]
            order += line if column % 2 == 0 else line[::-1]
        self.chips = chips
        self.half = chips // 2
        self.order = order
        self.swap = [(i, i ^ 1) for i in range(devices)]

    def go(self, block, hops):
        pairs = []
        for place in range(self.chips):
            here, there = self.order[place], self.order[(place + hops) % self.chips]
            pairs += [(here * CORES + core, there * CORES + core) for core in range(CORES)]
        return lax.ppermute(block, "ctx", pairs)

    def go_mate(self, block):
        return lax.ppermute(block, "ctx", self.swap)

    def go_split(self, block, hops):
        pairs = []
        for place in range(self.chips):
            for core, way in ((0, hops), (1, -hops)):
                here, there = self.order[place], self.order[(place + way) % self.chips]
                pairs.append((here * CORES + core, there * CORES + core))
        return lax.ppermute(block, "ctx", pairs)

    def owners(self, spots, swapped=False):
        place_of = {chip: place for place, chip in enumerate(self.order)}
        table = []
        for device in range(self.chips * CORES):
            chip, core = divmod(device, CORES)
            row = []
            for spot in spots:
                first = self.order[(place_of[chip] + spot[core]) % self.chips] * CORES + core
                row += [first ^ 1, first] if swapped else [first, first ^ 1]
            table.append(row)
        return np.asarray(table, np.int32)


def attention_kernel(
    pieces,
    heads,
    head_dim,
    owner_ref,
    pair_smem,
    role_smem,
    query_ref,
    pair_ref,
    role_ref,
    hidden_ref,
    gain_ref,
    weight_ref,
    *refs,
):
    blocks, refs = refs[:pieces], refs[pieces:]
    chunk_refs, refs = refs[:CHUNKS], refs[CHUNKS:]
    (residual_ref, stacked, scores, top, total, summed) = refs
    rows = query_ref.shape[0]
    me = owner_ref[0]
    for head in range(heads):
        stacked[pl.ds(head * rows, rows), :] = query_ref[:, head * head_dim : (head + 1) * head_dim]

    def column(ref):
        return jnp.broadcast_to(ref[pl.ds(me, 1), :], (rows, rows)).T

    query_pair, query_role = column(pair_ref), column(role_ref)
    query_pos = me * rows + lax.broadcasted_iota(jnp.int32, (rows, rows), 0)
    key_off = lax.broadcasted_iota(jnp.int32, (rows, rows), 1)

    def needed(owner):
        first_pair, last_pair = pair_smem[owner, 0], pair_smem[owner, rows - 1]
        first_role, last_role = role_smem[owner, 0], role_smem[owner, rows - 1]
        my_first, my_last = pair_smem[me, 0], pair_smem[me, rows - 1]
        my_role = role_smem[me, 0]
        apart = (
            (first_pair == last_pair)
            & (my_first == my_last)
            & (first_role == last_role)
            & (my_role == role_smem[me, rows - 1])
            & (first_role != 0)
            & (first_role != my_role)
        )
        return (owner <= me) & (last_pair >= my_first) & jnp.logical_not(apart)

    def bias_of(owner):
        key_role = role_ref[pl.ds(owner, 1), :]
        seen = (
            (query_pair == pair_ref[pl.ds(owner, 1), :])
            & (owner * rows + key_off <= query_pos)
            & ((key_role == 0) | (key_role == query_role))
        )
        return jnp.where(seen, 0.0, NEG_FILL)

    top[...] = jnp.full_like(top, NEG_FILL)
    total[...] = jnp.zeros_like(total)
    summed[...] = jnp.zeros_like(summed)
    for j, block in enumerate(blocks):
        owners = owner_ref[2 * j], owner_ref[2 * j + 1]

        @pl.when(needed(owners[0]) | needed(owners[1]))
        def _():
            bias = jnp.concatenate([bias_of(owner) for owner in owners], axis=1)
            raw = lax.dot_general(
                stacked[...],
                block[pl.ds(0, 2 * rows), :],
                (((1,), (1,)), ((), ())),
                preferred_element_type=jnp.float32,
            )
            masked = raw.reshape(heads, rows, 2 * rows) + bias[None]
            scores[j] = masked
            top[...] = jnp.maximum(
                top[...], jnp.maximum(masked[:, :, :rows], masked[:, :, rows:])
            )

    top[...] = jnp.broadcast_to(jnp.max(top[...], axis=-1, keepdims=True), top.shape)
    factor = math.log2(math.e) / math.sqrt(head_dim)
    for j, block in enumerate(blocks):
        owners = owner_ref[2 * j], owner_ref[2 * j + 1]

        @pl.when(needed(owners[0]) | needed(owners[1]))
        def _():
            weights = jnp.exp2((scores[j] - jnp.concatenate([top[...]] * 2, axis=2)) * factor)
            total[...] += weights[:, :, :rows] + weights[:, :, rows:]
            summed[...] += jnp.dot(
                weights.astype(jnp.bfloat16).reshape(heads * rows, 2 * rows),
                block[pl.ds(2 * rows, 2 * rows), :],
                preferred_element_type=jnp.float32,
            ).reshape(heads, rows, head_dim)

    mixed = (summed[...] / jnp.sum(total[...], axis=-1, keepdims=True)).astype(jnp.bfloat16)
    mixed = jnp.concatenate([mixed[head] for head in range(heads)], axis=1)
    projected = jnp.dot(mixed, weight_ref[...], preferred_element_type=jnp.float32)
    residual = (hidden_ref[...].astype(jnp.float32) + projected).astype(jnp.bfloat16)
    residual_ref[...] = residual
    wide = residual.astype(jnp.float32)
    mean_sq = jnp.mean(wide * wide, axis=-1, keepdims=True)
    normed = (wide * lax.rsqrt(mean_sq + 1e-06) * gain_ref[...]).astype(jnp.bfloat16)
    part = rows // CHUNKS
    for chunk in range(CHUNKS):
        chunk_refs[chunk][...] = normed[chunk * part : (chunk + 1) * part]


def attend(owners, pairs, parts, inputs, blocks):
    queries, _, _, hidden, _, _ = inputs
    rows, width = queries.shape
    head_dim = blocks[0].shape[1]
    heads = width // head_dim
    count = owners.shape[0]
    tall = heads * rows * rows * jnp.dtype(jnp.float32).itemsize
    smem = pl.BlockSpec(memory_space=pltpu.SMEM)
    vmem = pl.BlockSpec(memory_space=pltpu.VMEM)
    square = pltpu.VMEM((heads, rows, rows), jnp.float32)
    chunk = jax.ShapeDtypeStruct((rows // CHUNKS, hidden.shape[1]), jnp.bfloat16)
    *chunks, residual = pl.pallas_call(
        functools.partial(attention_kernel, len(blocks), heads, head_dim),
        out_shape=(chunk,) * CHUNKS + (jax.ShapeDtypeStruct(hidden.shape, jnp.bfloat16),),
        in_specs=[smem] * 3 + [vmem] * (len(inputs) + len(blocks)),
        out_specs=(vmem,) * (CHUNKS + 1),
        scratch_shapes=[
            pltpu.VMEM((heads * rows, head_dim), jnp.bfloat16),
            pltpu.VMEM((len(blocks), heads, rows, 2 * rows), jnp.float32),
            square,
            square,
            pltpu.VMEM((heads, rows, head_dim), jnp.float32),
        ],
        compiler_params=pltpu.CompilerParams(vmem_limit_bytes=(count + 3) * tall + 10 * MIB),
        name="attention",
    )(owners, pairs, parts, *(in_vmem(x) for x in inputs), in_vmem(blocks[0]), *blocks[1:])
    return residual, chunks


def load_kernel(count, *refs):
    inputs, outputs, sems = refs[:count], refs[count : 2 * count], refs[2 * count]
    moves = [pltpu.make_async_copy(inputs[k], outputs[k], sems.at[k]) for k in range(count)]
    for move in moves:
        move.start()
    for move in moves:
        move.wait()


def load(*arrays):
    count = len(arrays)
    return pl.pallas_call(
        functools.partial(load_kernel, count),
        out_shape=tuple(pltpu.VMEM(x.shape, x.dtype) for x in arrays),
        in_specs=[pl.BlockSpec(memory_space=pl.ANY)] * count,
        out_specs=(pl.BlockSpec(memory_space=pltpu.VMEM),) * count,
        scratch_shapes=[pltpu.SemaphoreType.DMA((count,))],
        compiler_params=pltpu.CompilerParams(vmem_limit_bytes=2 * MIB),
        name="load",
    )(*arrays)


def join_kernel(count, *refs):
    inputs, both_ref, sems = refs[: 2 * count], refs[2 * count], refs[2 * count + 1]
    rows = inputs[0].shape[0]
    moves = []
    for k in range(2 * count):
        owner, kind = divmod(k, count)
        place = pl.ds((kind * 2 + owner) * rows, rows)
        moves.append(pltpu.make_async_copy(inputs[k], both_ref.at[place, :], sems.at[k]))
    for move in moves:
        move.start()
    for move in moves:
        move.wait()


def join(own, mate):
    count = len(own)
    rows, width = own[0].shape
    return pl.pallas_call(
        functools.partial(join_kernel, count),
        out_shape=pltpu.VMEM((2 * count * rows, width), own[0].dtype),
        in_specs=[pl.BlockSpec(memory_space=pl.ANY)] * count
        + [pl.BlockSpec(memory_space=pltpu.VMEM)] * count,
        out_specs=pl.BlockSpec(memory_space=pltpu.VMEM),
        scratch_shapes=[pltpu.SemaphoreType.DMA((2 * count,))],
        name="join",
    )(*own, *mate)


def ffn_kernel(blocks, *refs):
    inputs, refs = refs[:blocks], refs[blocks:]
    weights, refs = refs[:6], refs[6:]
    outputs, refs = refs[:blocks], refs[blocks:]
    turned, inner, total = refs
    part = inputs[0].shape[0]
    turned[...] = jnp.concatenate([ref[...] for ref in inputs], axis=0).T
    for side in range(2):
        gate, up, down = weights[3 * side : 3 * side + 3]
        gate_out = jnp.dot(gate[...], turned[...], preferred_element_type=jnp.float32)
        up_out = jnp.dot(up[...], turned[...], preferred_element_type=jnp.float32)
        inner[...] = (gate_out / (1.0 + jnp.exp(-gate_out)) * up_out).astype(jnp.bfloat16)
        term = jnp.dot(inner[...].T, down[...], preferred_element_type=jnp.float32)
        if side == 0:
            total[...] = term
        else:
            term = (term + total[...]).astype(jnp.bfloat16)
            for k in range(blocks):
                outputs[k][...] = term[k * part : (k + 1) * part]


def ffn(blocks, weights):
    count = len(blocks)
    rows, width = blocks[0].shape
    hidden = weights[0].shape[0]
    vmem = pl.BlockSpec(memory_space=pltpu.VMEM)
    return pl.pallas_call(
        functools.partial(ffn_kernel, count),
        out_shape=tuple(jax.ShapeDtypeStruct(b.shape, jnp.bfloat16) for b in blocks),
        in_specs=[vmem] * (count + 6),
        out_specs=(vmem,) * count,
        scratch_shapes=[
            pltpu.VMEM((width, count * rows), jnp.bfloat16),
            pltpu.VMEM((hidden, count * rows), jnp.bfloat16),
            pltpu.VMEM((count * rows, width), jnp.float32),
        ],
        compiler_params=pltpu.CompilerParams(vmem_limit_bytes=16 * MIB),
        cost_estimate=pl.CostEstimate(flops=1000, transcendentals=0, bytes_accessed=1000),
        name="feed_forward",
    )(*blocks, *(in_vmem(w) for w in weights))


def feed_forward(ring, chunks, own, mates):
    half = ring.half

    def send(pair, way):
        return ring.go(pair[0], way), ring.go(pair[1], -way)

    chunks, own, mates = lax.optimization_barrier((chunks, own, mates))
    held = [[(chunks[0], chunks[1])], [(chunks[1], chunks[0])]]
    terms = [{}, {}]
    for group in range(2):
        held[group].append(send(held[group][0], 1))
    weights = load(*(in_hbm(w) for w in own)) + load(*mates)
    weights, held[0][1] = hold(weights, held[0][1])
    for step in range(1, half):
        held[0].append(send(held[0][step], 1))
        older = held[1][step - 1] if step > 1 else held[0][0]
        done = ffn(held[0][step] + older, weights)
        if step + 1 < half:
            done, pair = hold(done, held[1][step])
            held[1].append(send(pair, 1))
        terms[0][step], terms[1][step - 1] = done[:2], done[2:]
    older = held[1][half - 1] if half > 1 else held[0][0]
    if half > 1:
        done, older = hold(done, older)
        terms[0][half - 1], terms[1][half - 2] = done[:2], done[2:]
    done = ffn(held[0][half] + older, weights)
    terms[0][half], terms[1][half - 1] = done[:2], done[2:]

    def add(a, b):
        return (a.astype(jnp.float32) + b.astype(jnp.float32)).astype(jnp.bfloat16)

    home = [None, None]
    for step in range(half, 0, -1):
        for group in range(2):
            place = step - group
            if place == 0:
                continue
            pair = terms[group][place]
            if home[group] is not None:
                pair = (add(home[group][0], pair[0]), add(home[group][1], pair[1]))
            home[group] = send(pair, -1)
    sums = [[x.astype(jnp.float32) for x in terms[1][0]]]
    if home[1] is not None:
        sums.append([x.astype(jnp.float32) for x in home[1][::-1]])
    sums.append([x.astype(jnp.float32) for x in home[0]])
    return [sum(x[k] for x in sums) for k in range(2)]


def kv_phases(half):
    if half < 4:
        return [[(hops, 0) for hops in range(1, half + 1)]]
    phases = [[(1, 0), (3, 0)], [(2, 1), (4, 3)]]
    for hops in range(5, half + 1, 2):
        phases.append([(k, k - 2) for k in (hops, hops + 1) if k <= half])
    return phases


def gather_kv(ring, keys, values, weights, extras):
    half = ring.half
    gate, up, down = weights
    both = join(
        (in_hbm(keys), in_hbm(values)), (in_vmem(ring.go_mate(keys)), in_vmem(ring.go_mate(values)))
    )
    gate, up, both = lax.optimization_barrier((gate, up, both))
    gate_mate, up_mate = ring.go_mate(gate), ring.go_mate(up)
    held, mates = {0: both}, {}
    for phase in kv_phases(half):
        for block in [b for b in held if 0 < b and b not in mates]:
            mates[block] = ring.go_mate(held[block])
        for hops, source in phase:
            held[hops] = ring.go_split(held[source], hops - source)
        held, mates, extras = lax.optimization_barrier((held, mates, extras))
    for hops in range(1, half):
        if hops not in mates:
            mates[hops] = ring.go_mate(held[hops])
    gate_mate, up_mate, down, held, mates = lax.optimization_barrier(
        (gate_mate, up_mate, down, held, mates)
    )
    down_mate = ring.go_mate(down)
    blocks = tuple(held[hops] for hops in range(half + 1))
    blocks += tuple(mates[hops] for hops in range(1, half))
    return blocks, (gate_mate, up_mate, down_mate), extras


def block_owners(ring):
    half = ring.half
    owners = [ring.owners([(-hops, hops)]) for hops in range(half + 1)]
    owners += [ring.owners([(hops, -hops)], True) for hops in range(1, half)]
    return np.concatenate(owners, axis=1)


def on_device(
    ring,
    hidden_in,
    queries,
    keys,
    values,
    out_weight,
    norm_gain,
    gate_weight,
    up_weight,
    down_weight,
    pair_ids,
    roles,
    send_rows,
    send_counts,
):
    my_index = lax.axis_index("ctx")
    tok_rows = hidden_in.shape[0]
    own = (gate_weight.T, up_weight.T, down_weight)
    owners = jnp.asarray(block_owners(ring))[my_index]
    pairs = pair_ids.reshape(-1, tok_rows)
    parts = roles.reshape(-1, tok_rows)
    my_roles = lax.dynamic_slice_in_dim(roles, my_index * tok_rows, tok_rows)
    live = (my_roles != 0).astype(jnp.float32)
    inputs = load(
        *(in_hbm(x) for x in (queries, pairs, parts, hidden_in, norm_gain.reshape(1, -1), out_weight))
    )
    blocks, mates, extras = gather_kv(ring, keys, values, own, (owners, live, inputs))
    owners, live, inputs = extras
    residual, chunks = attend(owners, pairs, parts, inputs, blocks)
    summed = feed_forward(ring, chunks, own, mates)
    ffn_back = jnp.concatenate(summed, axis=0).astype(jnp.bfloat16).astype(jnp.float32)
    return (residual.astype(jnp.float32) + ffn_back * live[:, None]).astype(jnp.bfloat16)


def solution(mesh):
    ring = Ring(mesh.shape["groups"], mesh.shape["ctx"])

    def run(*arrays):
        return on_device(ring, *arrays)

    return jax.shard_map(
        run,
        mesh=mesh,
        in_specs=(
            P(("groups", "ctx"), None),
            P(("groups", "ctx"), None),
            P(("groups", "ctx"), None),
            P(("groups", "ctx"), None),
            P(),
            P(),
            P(None, "ctx"),
            P(None, "ctx"),
            P("ctx", None),
            P("groups"),
            P("groups"),
            P(("groups", "ctx"), None),
            P("groups", None),
        ),
        out_specs=P(("groups", "ctx"), None),
        check_vma=False,
    )
```

```python
import functools
import math

import jax
import jax.numpy as jnp
import numpy as np
from jax import lax
from jax.experimental import pallas as pl
from jax.experimental.pallas import tpu as pltpu
from jax.sharding import PartitionSpec as P

NEG_FILL = -1e30
CORES = 2
PLANE = 4
MIB = 1 << 20
CHUNKS = 2


def in_hbm(x):
    return pltpu.with_memory_space_constraint(x, pltpu.HBM)


def in_vmem(x):
    return pltpu.with_memory_space_constraint(x, pltpu.VMEM)


def hold(first, then):
    return lax.optimization_barrier((first, then))


class Ring:
    def __init__(self, groups, devices):
        chips = devices // CORES
        columns = max(1, PLANE // groups)
        if chips % columns:
            columns = 1
        depth = chips // columns
        order = []
        for column in range(columns):
            line = [level * columns + column for level in range(depth)]
            order += line if column % 2 == 0 else line[::-1]
        self.chips = chips
        self.half = chips // 2
        self.order = order
        self.swap = [(i, i ^ 1) for i in range(devices)]

    def go(self, block, hops):
        pairs = []
        for place in range(self.chips):
            here, there = self.order[place], self.order[(place + hops) % self.chips]
            pairs += [(here * CORES + core, there * CORES + core) for core in range(CORES)]
        return lax.ppermute(block, "ctx", pairs)

    def go_mate(self, block):
        return lax.ppermute(block, "ctx", self.swap)

    def go_split(self, block, hops):
        pairs = []
        for place in range(self.chips):
            for core, way in ((0, hops), (1, -hops)):
                here, there = self.order[place], self.order[(place + way) % self.chips]
                pairs.append((here * CORES + core, there * CORES + core))
        return lax.ppermute(block, "ctx", pairs)

    def owners(self, spots, swapped=False):
        place_of = {chip: place for place, chip in enumerate(self.order)}
        table = []
        for device in range(self.chips * CORES):
            chip, core = divmod(device, CORES)
            row = []
            for spot in spots:
                first = self.order[(place_of[chip] + spot[core]) % self.chips] * CORES + core
                row += [first ^ 1, first] if swapped else [first, first ^ 1]
            table.append(row)
        return np.asarray(table, np.int32)


def attention_kernel(
    pieces,
    heads,
    head_dim,
    owner_ref,
    pair_smem,
    role_smem,
    query_ref,
    pair_ref,
    role_ref,
    hidden_ref,
    gain_ref,
    weight_ref,
    *refs,
):
    blocks, refs = refs[:pieces], refs[pieces:]
    chunk_refs, refs = refs[:CHUNKS], refs[CHUNKS:]
    (residual_ref, stacked, scores, top, total, summed) = refs
    rows = query_ref.shape[0]
    me = owner_ref[0]
    for head in range(heads):
        stacked[pl.ds(head * rows, rows), :] = query_ref[:, head * head_dim : (head + 1) * head_dim]

    def column(ref):
        return jnp.broadcast_to(ref[pl.ds(me, 1), :], (rows, rows)).T

    query_pair, query_role = column(pair_ref), column(role_ref)
    query_pos = me * rows + lax.broadcasted_iota(jnp.int32, (rows, rows), 0)
    key_off = lax.broadcasted_iota(jnp.int32, (rows, rows), 1)

    def needed(owner):
        first_pair, last_pair = pair_smem[owner, 0], pair_smem[owner, rows - 1]
        first_role, last_role = role_smem[owner, 0], role_smem[owner, rows - 1]
        my_first, my_last = pair_smem[me, 0], pair_smem[me, rows - 1]
        my_role = role_smem[me, 0]
        apart = (
            (first_pair == last_pair)
            & (my_first == my_last)
            & (first_role == last_role)
            & (my_role == role_smem[me, rows - 1])
            & (first_role != 0)
            & (first_role != my_role)
        )
        return (owner <= me) & (last_pair >= my_first) & jnp.logical_not(apart)

    def bias_of(owner):
        key_role = role_ref[pl.ds(owner, 1), :]
        seen = (
            (query_pair == pair_ref[pl.ds(owner, 1), :])
            & (owner * rows + key_off <= query_pos)
            & ((key_role == 0) | (key_role == query_role))
        )
        return jnp.where(seen, 0.0, NEG_FILL)

    top[...] = jnp.full_like(top, NEG_FILL)
    total[...] = jnp.zeros_like(total)
    summed[...] = jnp.zeros_like(summed)
    for j, block in enumerate(blocks):
        owners = owner_ref[2 * j], owner_ref[2 * j + 1]

        @pl.when(needed(owners[0]) | needed(owners[1]))
        def _():
            bias = jnp.concatenate([bias_of(owner) for owner in owners], axis=1)
            raw = lax.dot_general(
                stacked[...],
                block[pl.ds(0, 2 * rows), :],
                (((1,), (1,)), ((), ())),
                preferred_element_type=jnp.float32,
            )
            masked = raw.reshape(heads, rows, 2 * rows) + bias[None]
            scores[j] = masked
            top[...] = jnp.maximum(
                top[...], jnp.maximum(masked[:, :, :rows], masked[:, :, rows:])
            )

    top[...] = jnp.broadcast_to(jnp.max(top[...], axis=-1, keepdims=True), top.shape)
    factor = math.log2(math.e) / math.sqrt(head_dim)
    for j, block in enumerate(blocks):
        owners = owner_ref[2 * j], owner_ref[2 * j + 1]

        @pl.when(needed(owners[0]) | needed(owners[1]))
        def _():
            weights = jnp.exp2((scores[j] - jnp.concatenate([top[...]] * 2, axis=2)) * factor)
            total[...] += weights[:, :, :rows] + weights[:, :, rows:]
            summed[...] += jnp.dot(
                weights.astype(jnp.bfloat16).reshape(heads * rows, 2 * rows),
                block[pl.ds(2 * rows, 2 * rows), :],
                preferred_element_type=jnp.float32,
            ).reshape(heads, rows, head_dim)

    mixed = (summed[...] / jnp.sum(total[...], axis=-1, keepdims=True)).astype(jnp.bfloat16)
    mixed = jnp.concatenate([mixed[head] for head in range(heads)], axis=1)
    projected = jnp.dot(mixed, weight_ref[...], preferred_element_type=jnp.float32)
    residual = (hidden_ref[...].astype(jnp.float32) + projected).astype(jnp.bfloat16)
    residual_ref[...] = residual
    wide = residual.astype(jnp.float32)
    mean_sq = jnp.mean(wide * wide, axis=-1, keepdims=True)
    normed = (wide * lax.rsqrt(mean_sq + 1e-06) * gain_ref[...]).astype(jnp.bfloat16)
    part = rows // CHUNKS
    for chunk in range(CHUNKS):
        chunk_refs[chunk][...] = normed[chunk * part : (chunk + 1) * part]


def attend(owners, pairs, parts, inputs, blocks):
    queries, _, _, hidden, _, _ = inputs
    rows, width = queries.shape
    head_dim = blocks[0].shape[1]
    heads = width // head_dim
    count = owners.shape[0]
    tall = heads * rows * rows * jnp.dtype(jnp.float32).itemsize
    smem = pl.BlockSpec(memory_space=pltpu.SMEM)
    vmem = pl.BlockSpec(memory_space=pltpu.VMEM)
    square = pltpu.VMEM((heads, rows, rows), jnp.float32)
    chunk = jax.ShapeDtypeStruct((rows // CHUNKS, hidden.shape[1]), jnp.bfloat16)
    *chunks, residual = pl.pallas_call(
        functools.partial(attention_kernel, len(blocks), heads, head_dim),
        out_shape=(chunk,) * CHUNKS + (jax.ShapeDtypeStruct(hidden.shape, jnp.bfloat16),),
        in_specs=[smem] * 3 + [vmem] * (len(inputs) + len(blocks)),
        out_specs=(vmem,) * (CHUNKS + 1),
        scratch_shapes=[
            pltpu.VMEM((heads * rows, head_dim), jnp.bfloat16),
            pltpu.VMEM((len(blocks), heads, rows, 2 * rows), jnp.float32),
            square,
            square,
            pltpu.VMEM((heads, rows, head_dim), jnp.float32),
        ],
        compiler_params=pltpu.CompilerParams(vmem_limit_bytes=(count + 3) * tall + 10 * MIB),
        name="attention",
    )(owners, pairs, parts, *(in_vmem(x) for x in inputs), in_vmem(blocks[0]), *blocks[1:])
    return residual, chunks


def load_kernel(count, *refs):
    inputs, outputs, sems = refs[:count], refs[count : 2 * count], refs[2 * count]
    moves = [pltpu.make_async_copy(inputs[k], outputs[k], sems.at[k]) for k in range(count)]
    for move in moves:
        move.start()
    for move in moves:
        move.wait()


def load(*arrays):
    count = len(arrays)
    return pl.pallas_call(
        functools.partial(load_kernel, count),
        out_shape=tuple(pltpu.VMEM(x.shape, x.dtype) for x in arrays),
        in_specs=[pl.BlockSpec(memory_space=pl.ANY)] * count,
        out_specs=(pl.BlockSpec(memory_space=pltpu.VMEM),) * count,
        scratch_shapes=[pltpu.SemaphoreType.DMA((count,))],
        compiler_params=pltpu.CompilerParams(vmem_limit_bytes=2 * MIB),
        name="load",
    )(*arrays)


def join_kernel(count, *refs):
    inputs, both_ref, sems = refs[: 2 * count], refs[2 * count], refs[2 * count + 1]
    rows = inputs[0].shape[0]
    moves = []
    for k in range(2 * count):
        owner, kind = divmod(k, count)
        place = pl.ds((kind * 2 + owner) * rows, rows)
        moves.append(pltpu.make_async_copy(inputs[k], both_ref.at[place, :], sems.at[k]))
    for move in moves:
        move.start()
    for move in moves:
        move.wait()


def join(own, mate):
    count = len(own)
    rows, width = own[0].shape
    return pl.pallas_call(
        functools.partial(join_kernel, count),
        out_shape=pltpu.VMEM((2 * count * rows, width), own[0].dtype),
        in_specs=[pl.BlockSpec(memory_space=pl.ANY)] * count
        + [pl.BlockSpec(memory_space=pltpu.VMEM)] * count,
        out_specs=pl.BlockSpec(memory_space=pltpu.VMEM),
        scratch_shapes=[pltpu.SemaphoreType.DMA((2 * count,))],
        name="join",
    )(*own, *mate)


def ffn_kernel(blocks, *refs):
    inputs, refs = refs[:blocks], refs[blocks:]
    weights, refs = refs[:6], refs[6:]
    outputs, refs = refs[:blocks], refs[blocks:]
    turned, inner = refs
    part = inputs[0].shape[0]
    turned[...] = jnp.concatenate([ref[...] for ref in inputs], axis=0).T
    for side in range(2):
        gate, up = weights[3 * side : 3 * side + 2]
        gate_out = jnp.dot(gate[...], turned[...], preferred_element_type=jnp.float32)
        up_out = jnp.dot(up[...], turned[...], preferred_element_type=jnp.float32)
        inner[side] = (gate_out / (1.0 + jnp.exp(-gate_out)) * up_out).astype(jnp.bfloat16)
    term = sum(
        jnp.dot(inner[side].T, weights[3 * side + 2][...], preferred_element_type=jnp.float32)
        for side in range(2)
    ).astype(jnp.bfloat16)
    for k in range(blocks):
        outputs[k][...] = term[k * part : (k + 1) * part]


def ffn(blocks, weights):
    count = len(blocks)
    rows, width = blocks[0].shape
    hidden = weights[0].shape[0]
    vmem = pl.BlockSpec(memory_space=pltpu.VMEM)
    return pl.pallas_call(
        functools.partial(ffn_kernel, count),
        out_shape=tuple(jax.ShapeDtypeStruct(b.shape, jnp.bfloat16) for b in blocks),
        in_specs=[vmem] * (count + 6),
        out_specs=(vmem,) * count,
        scratch_shapes=[
            pltpu.VMEM((width, count * rows), jnp.bfloat16),
            pltpu.VMEM((2, hidden, count * rows), jnp.bfloat16),
        ],
        compiler_params=pltpu.CompilerParams(vmem_limit_bytes=16 * MIB),
        cost_estimate=pl.CostEstimate(flops=1000, transcendentals=0, bytes_accessed=1000),
        name="feed_forward",
    )(*blocks, *(in_vmem(w) for w in weights))


def feed_forward(ring, chunks, own, mates):
    half = ring.half

    def send(pair, way):
        return ring.go(pair[0], way), ring.go(pair[1], -way)

    chunks, own, mates = lax.optimization_barrier((chunks, own, mates))
    held = [[(chunks[0], chunks[1])], [(chunks[1], chunks[0])]]
    terms = [{}, {}]
    for group in range(2):
        held[group].append(send(held[group][0], 1))
    weights = load(*(in_hbm(w) for w in own)) + load(*mates)
    weights, held[0][1] = hold(weights, held[0][1])
    for step in range(1, half):
        held[0].append(send(held[0][step], 1))
        older = held[1][step - 1] if step > 1 else held[0][0]
        done = ffn(held[0][step] + older, weights)
        if step + 1 < half:
            done, pair = hold(done, held[1][step])
            held[1].append(send(pair, 1))
        terms[0][step], terms[1][step - 1] = done[:2], done[2:]
    older = held[1][half - 1] if half > 1 else held[0][0]
    if half > 1:
        done, older = hold(done, older)
        terms[0][half - 1], terms[1][half - 2] = done[:2], done[2:]
    done = ffn(held[0][half] + older, weights)
    terms[0][half], terms[1][half - 1] = done[:2], done[2:]

    def add(a, b):
        return (a.astype(jnp.float32) + b.astype(jnp.float32)).astype(jnp.bfloat16)

    home = [None, None]
    for step in range(half, 0, -1):
        for group in range(2):
            place = step - group
            if place == 0:
                continue
            pair = terms[group][place]
            if home[group] is not None:
                pair = (add(home[group][0], pair[0]), add(home[group][1], pair[1]))
            home[group] = send(pair, -1)
    sums = [[x.astype(jnp.float32) for x in terms[1][0]]]
    if home[1] is not None:
        sums.append([x.astype(jnp.float32) for x in home[1][::-1]])
    sums.append([x.astype(jnp.float32) for x in home[0]])
    return [sum(x[k] for x in sums) for k in range(2)]


def kv_phases(half):
    if half < 4:
        return [[(hops, 0) for hops in range(1, half + 1)]]
    phases = [[(1, 0), (3, 0)], [(2, 1), (4, 3)]]
    for hops in range(5, half + 1, 2):
        phases.append([(k, k - 2) for k in (hops, hops + 1) if k <= half])
    return phases


def gather_kv(ring, keys, values, weights, extras):
    half = ring.half
    gate, up, down = weights
    both = join(
        (in_hbm(keys), in_hbm(values)), (in_vmem(ring.go_mate(keys)), in_vmem(ring.go_mate(values)))
    )
    gate, up, both = lax.optimization_barrier((gate, up, both))
    gate_mate, up_mate = ring.go_mate(gate), ring.go_mate(up)
    held, mates = {0: both}, {}
    for phase in kv_phases(half):
        for block in [b for b in held if 0 < b and b not in mates]:
            mates[block] = ring.go_mate(held[block])
        for hops, source in phase:
            held[hops] = ring.go_split(held[source], hops - source)
        held, mates, extras = lax.optimization_barrier((held, mates, extras))
    for hops in range(1, half):
        if hops not in mates:
            mates[hops] = ring.go_mate(held[hops])
    gate_mate, up_mate, down, held, mates = lax.optimization_barrier(
        (gate_mate, up_mate, down, held, mates)
    )
    down_mate = ring.go_mate(down)
    blocks = tuple(held[hops] for hops in range(half + 1))
    blocks += tuple(mates[hops] for hops in range(1, half))
    return blocks, (gate_mate, up_mate, down_mate), extras


def block_owners(ring):
    half = ring.half
    owners = [ring.owners([(-hops, hops)]) for hops in range(half + 1)]
    owners += [ring.owners([(hops, -hops)], True) for hops in range(1, half)]
    return np.concatenate(owners, axis=1)


def on_device(
    ring,
    hidden_in,
    queries,
    keys,
    values,
    out_weight,
    norm_gain,
    gate_weight,
    up_weight,
    down_weight,
    pair_ids,
    roles,
    send_rows,
    send_counts,
):
    my_index = lax.axis_index("ctx")
    tok_rows = hidden_in.shape[0]
    own = (gate_weight.T, up_weight.T, down_weight)
    owners = jnp.asarray(block_owners(ring))[my_index]
    pairs = pair_ids.reshape(-1, tok_rows)
    parts = roles.reshape(-1, tok_rows)
    my_roles = lax.dynamic_slice_in_dim(roles, my_index * tok_rows, tok_rows)
    live = (my_roles != 0).astype(jnp.float32)
    inputs = load(
        *(in_hbm(x) for x in (queries, pairs, parts, hidden_in, norm_gain.reshape(1, -1), out_weight))
    )
    blocks, mates, extras = gather_kv(ring, keys, values, own, (owners, live, inputs))
    owners, live, inputs = extras
    residual, chunks = attend(owners, pairs, parts, inputs, blocks)
    summed = feed_forward(ring, chunks, own, mates)
    ffn_back = jnp.concatenate(summed, axis=0).astype(jnp.bfloat16).astype(jnp.float32)
    return (residual.astype(jnp.float32) + ffn_back * live[:, None]).astype(jnp.bfloat16)


def solution(mesh):
    ring = Ring(mesh.shape["groups"], mesh.shape["ctx"])

    def run(*arrays):
        return on_device(ring, *arrays)

    return jax.shard_map(
        run,
        mesh=mesh,
        in_specs=(
            P(("groups", "ctx"), None),
            P(("groups", "ctx"), None),
            P(("groups", "ctx"), None),
            P(("groups", "ctx"), None),
            P(),
            P(),
            P(None, "ctx"),
            P(None, "ctx"),
            P("ctx", None),
            P("groups"),
            P("groups"),
            P(("groups", "ctx"), None),
            P("groups", None),
        ),
        out_specs=P(("groups", "ctx"), None),
        check_vma=False,
    )
```

```python
import functools
import math

import jax
import jax.numpy as jnp
import numpy as np
from jax import lax
from jax.experimental import pallas as pl
from jax.experimental.pallas import tpu as pltpu
from jax.sharding import PartitionSpec as P

NEG_FILL = -1e30
CORES = 2
PLANE = 4
MIB = 1 << 20
CHUNKS = 2


def in_hbm(x):
    return pltpu.with_memory_space_constraint(x, pltpu.HBM)


def in_vmem(x):
    return pltpu.with_memory_space_constraint(x, pltpu.VMEM)


def hold(first, then):
    return lax.optimization_barrier((first, then))


class Ring:
    def __init__(self, groups, devices):
        chips = devices // CORES
        columns = max(1, PLANE // groups)
        if chips % columns:
            columns = 1
        depth = chips // columns
        order = []
        for column in range(columns):
            line = [level * columns + column for level in range(depth)]
            order += line if column % 2 == 0 else line[::-1]
        self.chips = chips
        self.half = chips // 2
        self.order = order
        self.swap = [(i, i ^ 1) for i in range(devices)]

    def go(self, block, hops):
        pairs = []
        for place in range(self.chips):
            here, there = self.order[place], self.order[(place + hops) % self.chips]
            pairs += [(here * CORES + core, there * CORES + core) for core in range(CORES)]
        return lax.ppermute(block, "ctx", pairs)

    def go_mate(self, block):
        return lax.ppermute(block, "ctx", self.swap)

    def go_split(self, block, hops):
        pairs = []
        for place in range(self.chips):
            for core, way in ((0, hops), (1, -hops)):
                here, there = self.order[place], self.order[(place + way) % self.chips]
                pairs.append((here * CORES + core, there * CORES + core))
        return lax.ppermute(block, "ctx", pairs)

    def owners(self, spots, swapped=False):
        place_of = {chip: place for place, chip in enumerate(self.order)}
        table = []
        for device in range(self.chips * CORES):
            chip, core = divmod(device, CORES)
            row = []
            for spot in spots:
                first = self.order[(place_of[chip] + spot[core]) % self.chips] * CORES + core
                row += [first ^ 1, first] if swapped else [first, first ^ 1]
            table.append(row)
        return np.asarray(table, np.int32)


def attention_kernel(
    pieces,
    heads,
    head_dim,
    owner_ref,
    pair_smem,
    role_smem,
    query_ref,
    pair_ref,
    role_ref,
    hidden_ref,
    gain_ref,
    weight_ref,
    *refs,
):
    blocks, refs = refs[:pieces], refs[pieces:]
    chunk_refs, refs = refs[:CHUNKS], refs[CHUNKS:]
    (residual_ref, stacked, scores, top, total, summed) = refs
    rows = query_ref.shape[0]
    me = owner_ref[0]
    for head in range(heads):
        stacked[pl.ds(head * rows, rows), :] = query_ref[:, head * head_dim : (head + 1) * head_dim]

    def column(ref):
        return jnp.broadcast_to(ref[pl.ds(me, 1), :], (rows, rows)).T

    query_pair, query_role = column(pair_ref), column(role_ref)
    query_pos = me * rows + lax.broadcasted_iota(jnp.int32, (rows, rows), 0)
    key_off = lax.broadcasted_iota(jnp.int32, (rows, rows), 1)

    def needed(owner):
        first_pair, last_pair = pair_smem[owner, 0], pair_smem[owner, rows - 1]
        first_role, last_role = role_smem[owner, 0], role_smem[owner, rows - 1]
        my_first, my_last = pair_smem[me, 0], pair_smem[me, rows - 1]
        my_role = role_smem[me, 0]
        apart = (
            (first_pair == last_pair)
            & (my_first == my_last)
            & (first_role == last_role)
            & (my_role == role_smem[me, rows - 1])
            & (first_role != 0)
            & (first_role != my_role)
        )
        return (owner <= me) & (last_pair >= my_first) & jnp.logical_not(apart)

    def bias_of(owner):
        key_role = role_ref[pl.ds(owner, 1), :]
        seen = (
            (query_pair == pair_ref[pl.ds(owner, 1), :])
            & (owner * rows + key_off <= query_pos)
            & ((key_role == 0) | (key_role == query_role))
        )
        return jnp.where(seen, 0.0, NEG_FILL)

    top[...] = jnp.full_like(top, NEG_FILL)
    total[...] = jnp.zeros_like(total)
    summed[...] = jnp.zeros_like(summed)
    for j, block in enumerate(blocks):
        owners = owner_ref[2 * j], owner_ref[2 * j + 1]

        @pl.when(needed(owners[0]) | needed(owners[1]))
        def _():
            bias = jnp.concatenate([bias_of(owner) for owner in owners], axis=1)
            raw = lax.dot_general(
                stacked[...],
                block[pl.ds(0, 2 * rows), :],
                (((1,), (1,)), ((), ())),
                preferred_element_type=jnp.float32,
            )
            masked = raw.reshape(heads, rows, 2 * rows) + bias[None]
            scores[j] = masked
            top[...] = jnp.maximum(
                top[...], jnp.maximum(masked[:, :, :rows], masked[:, :, rows:])
            )

    top[...] = jnp.broadcast_to(jnp.max(top[...], axis=-1, keepdims=True), top.shape)
    factor = math.log2(math.e) / math.sqrt(head_dim)
    for j, block in enumerate(blocks):
        owners = owner_ref[2 * j], owner_ref[2 * j + 1]

        @pl.when(needed(owners[0]) | needed(owners[1]))
        def _():
            weights = jnp.exp2((scores[j] - jnp.concatenate([top[...]] * 2, axis=2)) * factor)
            total[...] += weights[:, :, :rows] + weights[:, :, rows:]
            summed[...] += jnp.dot(
                weights.astype(jnp.bfloat16).reshape(heads * rows, 2 * rows),
                block[pl.ds(2 * rows, 2 * rows), :],
                preferred_element_type=jnp.float32,
            ).reshape(heads, rows, head_dim)

    mixed = (summed[...] / jnp.sum(total[...], axis=-1, keepdims=True)).astype(jnp.bfloat16)
    mixed = jnp.concatenate([mixed[head] for head in range(heads)], axis=1)
    projected = jnp.dot(mixed, weight_ref[...], preferred_element_type=jnp.float32)
    residual = (hidden_ref[...].astype(jnp.float32) + projected).astype(jnp.bfloat16)
    residual_ref[...] = residual
    wide = residual.astype(jnp.float32)
    mean_sq = jnp.mean(wide * wide, axis=-1, keepdims=True)
    normed = (wide * lax.rsqrt(mean_sq + 1e-06) * gain_ref[...]).astype(jnp.bfloat16)
    part = rows // CHUNKS
    for chunk in range(CHUNKS):
        chunk_refs[chunk][...] = normed[chunk * part : (chunk + 1) * part]


def attend(owners, pairs, parts, inputs, blocks):
    queries, _, _, hidden, _, _ = inputs
    rows, width = queries.shape
    head_dim = blocks[0].shape[1]
    heads = width // head_dim
    count = owners.shape[0]
    tall = heads * rows * rows * jnp.dtype(jnp.float32).itemsize
    smem = pl.BlockSpec(memory_space=pltpu.SMEM)
    vmem = pl.BlockSpec(memory_space=pltpu.VMEM)
    square = pltpu.VMEM((heads, rows, rows), jnp.float32)
    chunk = jax.ShapeDtypeStruct((rows // CHUNKS, hidden.shape[1]), jnp.bfloat16)
    *chunks, residual = pl.pallas_call(
        functools.partial(attention_kernel, len(blocks), heads, head_dim),
        out_shape=(chunk,) * CHUNKS + (jax.ShapeDtypeStruct(hidden.shape, jnp.bfloat16),),
        in_specs=[smem] * 3 + [vmem] * (len(inputs) + len(blocks)),
        out_specs=(vmem,) * (CHUNKS + 1),
        scratch_shapes=[
            pltpu.VMEM((heads * rows, head_dim), jnp.bfloat16),
            pltpu.VMEM((len(blocks), heads, rows, 2 * rows), jnp.float32),
            square,
            square,
            pltpu.VMEM((heads, rows, head_dim), jnp.float32),
        ],
        compiler_params=pltpu.CompilerParams(vmem_limit_bytes=(count + 3) * tall + 10 * MIB),
        name="attention",
    )(owners, pairs, parts, *(in_vmem(x) for x in inputs), in_vmem(blocks[0]), *blocks[1:])
    return residual, chunks


def load_kernel(count, *refs):
    inputs, outputs, sems = refs[:count], refs[count : 2 * count], refs[2 * count]
    moves = [pltpu.make_async_copy(inputs[k], outputs[k], sems.at[k]) for k in range(count)]
    for move in moves:
        move.start()
    for move in moves:
        move.wait()


def load(*arrays):
    count = len(arrays)
    return pl.pallas_call(
        functools.partial(load_kernel, count),
        out_shape=tuple(pltpu.VMEM(x.shape, x.dtype) for x in arrays),
        in_specs=[pl.BlockSpec(memory_space=pl.ANY)] * count,
        out_specs=(pl.BlockSpec(memory_space=pltpu.VMEM),) * count,
        scratch_shapes=[pltpu.SemaphoreType.DMA((count,))],
        compiler_params=pltpu.CompilerParams(vmem_limit_bytes=2 * MIB),
        name="load",
    )(*arrays)


def join_kernel(count, *refs):
    inputs, both_ref, sems = refs[: 2 * count], refs[2 * count], refs[2 * count + 1]
    rows = inputs[0].shape[0]
    moves = []
    for k in range(2 * count):
        owner, kind = divmod(k, count)
        place = pl.ds((kind * 2 + owner) * rows, rows)
        moves.append(pltpu.make_async_copy(inputs[k], both_ref.at[place, :], sems.at[k]))
    for move in moves:
        move.start()
    for move in moves:
        move.wait()


def join(own, mate):
    count = len(own)
    rows, width = own[0].shape
    return pl.pallas_call(
        functools.partial(join_kernel, count),
        out_shape=pltpu.VMEM((2 * count * rows, width), own[0].dtype),
        in_specs=[pl.BlockSpec(memory_space=pl.ANY)] * count
        + [pl.BlockSpec(memory_space=pltpu.VMEM)] * count,
        out_specs=pl.BlockSpec(memory_space=pltpu.VMEM),
        scratch_shapes=[pltpu.SemaphoreType.DMA((2 * count,))],
        name="join",
    )(*own, *mate)


def ffn_kernel(blocks, *refs):
    inputs, refs = refs[:blocks], refs[blocks:]
    weights, refs = refs[:6], refs[6:]
    outputs, refs = refs[:blocks], refs[blocks:]
    turned, inner = refs
    part = inputs[0].shape[0]
    turned[...] = jnp.concatenate([ref[...] for ref in inputs], axis=0).T
    for side in range(2):
        gate, up = weights[3 * side : 3 * side + 2]
        gate_out = jnp.dot(gate[...], turned[...], preferred_element_type=jnp.float32)
        up_out = jnp.dot(up[...], turned[...], preferred_element_type=jnp.float32)
        inner[side] = (gate_out / (1.0 + jnp.exp(-gate_out)) * up_out).astype(jnp.bfloat16)
    term = sum(
        jnp.dot(inner[side].T, weights[3 * side + 2][...], preferred_element_type=jnp.float32)
        for side in range(2)
    ).astype(jnp.bfloat16)
    for k in range(blocks):
        outputs[k][...] = term[k * part : (k + 1) * part]


def ffn(blocks, weights):
    count = len(blocks)
    rows, width = blocks[0].shape
    hidden = weights[0].shape[0]
    vmem = pl.BlockSpec(memory_space=pltpu.VMEM)
    return pl.pallas_call(
        functools.partial(ffn_kernel, count),
        out_shape=tuple(jax.ShapeDtypeStruct(b.shape, jnp.bfloat16) for b in blocks),
        in_specs=[vmem] * (count + 6),
        out_specs=(vmem,) * count,
        scratch_shapes=[
            pltpu.VMEM((width, count * rows), jnp.bfloat16),
            pltpu.VMEM((2, hidden, count * rows), jnp.bfloat16),
        ],
        compiler_params=pltpu.CompilerParams(vmem_limit_bytes=16 * MIB),
        cost_estimate=pl.CostEstimate(flops=1000, transcendentals=0, bytes_accessed=1000),
        name="feed_forward",
    )(*blocks, *(in_vmem(w) for w in weights))


def feed_forward(ring, chunks, own, mates):
    half = ring.half

    def send(pair, way):
        return ring.go(pair[0], way), ring.go(pair[1], -way)

    chunks, own, mates = lax.optimization_barrier((chunks, own, mates))
    held = [[(chunks[0], chunks[1])], [(chunks[1], chunks[0])]]
    terms = [{}, {}]
    for group in range(2):
        held[group].append(send(held[group][0], 1))
    weights = load(*(in_hbm(w) for w in own)) + load(*mates)
    weights, held[0][1] = hold(weights, held[0][1])
    for step in range(1, half):
        held[0].append(send(held[0][step], 1))
        older = held[1][step - 1] if step > 1 else held[0][0]
        done = ffn(held[0][step] + older, weights)
        if step + 1 < half:
            done, pair = hold(done, held[1][step])
            held[1].append(send(pair, 1))
        terms[0][step], terms[1][step - 1] = done[:2], done[2:]
    older = held[1][half - 1] if half > 1 else held[0][0]
    if half > 1:
        done, older = hold(done, older)
        terms[0][half - 1], terms[1][half - 2] = done[:2], done[2:]
    done = ffn(held[0][half] + older, weights)
    terms[0][half], terms[1][half - 1] = done[:2], done[2:]

    def add(a, b):
        return (a.astype(jnp.float32) + b.astype(jnp.float32)).astype(jnp.bfloat16)

    home = [None, None]
    for step in range(half, 0, -1):
        for group in range(2):
            place = step - group
            if place == 0:
                continue
            pair = terms[group][place]
            if home[group] is not None:
                pair = (add(home[group][0], pair[0]), add(home[group][1], pair[1]))
            home[group] = send(pair, -1)
    sums = [[x.astype(jnp.float32) for x in terms[1][0]]]
    if home[1] is not None:
        sums.append([x.astype(jnp.float32) for x in home[1][::-1]])
    sums.append([x.astype(jnp.float32) for x in home[0]])
    return [sum(x[k] for x in sums) for k in range(2)]


def kv_phases(half):
    if half < 4:
        return [[(hops, 0) for hops in range(1, half + 1)]]
    phases = [[(1, 0), (3, 0)], [(2, 1), (4, 3)]]
    for hops in range(5, half + 1, 2):
        phases.append([(k, k - 2) for k in (hops, hops + 1) if k <= half])
    return phases


def gather_kv(ring, keys, values, weights, extras):
    half = ring.half
    gate, up, down = weights
    both = join(
        (in_hbm(keys), in_hbm(values)), (in_vmem(ring.go_mate(keys)), in_vmem(ring.go_mate(values)))
    )
    gate, up, both = lax.optimization_barrier((gate, up, both))
    gate_mate, up_mate = ring.go_mate(gate), ring.go_mate(up)
    held, mates = {0: both}, {}
    for phase in kv_phases(half):
        for block in [b for b in held if 0 < b and b not in mates]:
            mates[block] = ring.go_mate(held[block])
        for hops, source in phase:
            held[hops] = ring.go_split(held[source], hops - source)
    held[1], extras = hold(held[1], extras)
    for hops in range(1, half):
        if hops not in mates:
            mates[hops] = ring.go_mate(held[hops])
    gate_mate, up_mate, down, held, mates = lax.optimization_barrier(
        (gate_mate, up_mate, down, held, mates)
    )
    down_mate = ring.go_mate(down)
    blocks = tuple(held[hops] for hops in range(half + 1))
    blocks += tuple(mates[hops] for hops in range(1, half))
    return blocks, (gate_mate, up_mate, down_mate), extras


def block_owners(ring):
    half = ring.half
    owners = [ring.owners([(-hops, hops)]) for hops in range(half + 1)]
    owners += [ring.owners([(hops, -hops)], True) for hops in range(1, half)]
    return np.concatenate(owners, axis=1)


def on_device(
    ring,
    hidden_in,
    queries,
    keys,
    values,
    out_weight,
    norm_gain,
    gate_weight,
    up_weight,
    down_weight,
    pair_ids,
    roles,
    send_rows,
    send_counts,
):
    my_index = lax.axis_index("ctx")
    tok_rows = hidden_in.shape[0]
    own = (gate_weight.T, up_weight.T, down_weight)
    owners = jnp.asarray(block_owners(ring))[my_index]
    pairs = pair_ids.reshape(-1, tok_rows)
    parts = roles.reshape(-1, tok_rows)
    my_roles = lax.dynamic_slice_in_dim(roles, my_index * tok_rows, tok_rows)
    live = (my_roles != 0).astype(jnp.float32)
    inputs = load(
        *(in_hbm(x) for x in (queries, pairs, parts, hidden_in, norm_gain.reshape(1, -1), out_weight))
    )
    blocks, mates, extras = gather_kv(ring, keys, values, own, (owners, live, inputs))
    owners, live, inputs = extras
    residual, chunks = attend(owners, pairs, parts, inputs, blocks)
    summed = feed_forward(ring, chunks, own, mates)
    ffn_back = jnp.concatenate(summed, axis=0).astype(jnp.bfloat16).astype(jnp.float32)
    return (residual.astype(jnp.float32) + ffn_back * live[:, None]).astype(jnp.bfloat16)


def solution(mesh):
    ring = Ring(mesh.shape["groups"], mesh.shape["ctx"])

    def run(*arrays):
        return on_device(ring, *arrays)

    return jax.shard_map(
        run,
        mesh=mesh,
        in_specs=(
            P(("groups", "ctx"), None),
            P(("groups", "ctx"), None),
            P(("groups", "ctx"), None),
            P(("groups", "ctx"), None),
            P(),
            P(),
            P(None, "ctx"),
            P(None, "ctx"),
            P("ctx", None),
            P("groups"),
            P("groups"),
            P(("groups", "ctx"), None),
            P("groups", None),
        ),
        out_specs=P(("groups", "ctx"), None),
        check_vma=False,
    )
```

```python
import functools
import math

import jax
import jax.numpy as jnp
import numpy as np
from jax import lax
from jax.experimental import pallas as pl
from jax.experimental.pallas import tpu as pltpu
from jax.sharding import PartitionSpec as P

NEG_FILL = -1e30
CORES = 2
PLANE = 4
MIB = 1 << 20
CHUNKS = 2


def in_hbm(x):
    return pltpu.with_memory_space_constraint(x, pltpu.HBM)


def in_vmem(x):
    return pltpu.with_memory_space_constraint(x, pltpu.VMEM)


def hold(first, then):
    return lax.optimization_barrier((first, then))


class Ring:
    def __init__(self, groups, devices):
        chips = devices // CORES
        columns = max(1, PLANE // groups)
        if chips % columns:
            columns = 1
        depth = chips // columns
        order = []
        for column in range(columns):
            line = [level * columns + column for level in range(depth)]
            order += line if column % 2 == 0 else line[::-1]
        self.chips = chips
        self.half = chips // 2
        self.order = order
        self.swap = [(i, i ^ 1) for i in range(devices)]

    def go(self, block, hops):
        pairs = []
        for place in range(self.chips):
            here, there = self.order[place], self.order[(place + hops) % self.chips]
            pairs += [(here * CORES + core, there * CORES + core) for core in range(CORES)]
        return lax.ppermute(block, "ctx", pairs)

    def go_mate(self, block):
        return lax.ppermute(block, "ctx", self.swap)

    def go_split(self, block, hops):
        pairs = []
        for place in range(self.chips):
            for core, way in ((0, hops), (1, -hops)):
                here, there = self.order[place], self.order[(place + way) % self.chips]
                pairs.append((here * CORES + core, there * CORES + core))
        return lax.ppermute(block, "ctx", pairs)

    def owners(self, spots, swapped=False):
        place_of = {chip: place for place, chip in enumerate(self.order)}
        table = []
        for device in range(self.chips * CORES):
            chip, core = divmod(device, CORES)
            row = []
            for spot in spots:
                first = self.order[(place_of[chip] + spot[core]) % self.chips] * CORES + core
                row += [first ^ 1, first] if swapped else [first, first ^ 1]
            table.append(row)
        return np.asarray(table, np.int32)


def attention_kernel(
    pieces,
    heads,
    head_dim,
    owner_ref,
    pair_smem,
    role_smem,
    query_ref,
    pair_ref,
    role_ref,
    hidden_ref,
    gain_ref,
    weight_ref,
    *refs,
):
    blocks, refs = refs[:pieces], refs[pieces:]
    chunk_refs, refs = refs[:CHUNKS], refs[CHUNKS:]
    (residual_ref, stacked, scores, top, total, summed) = refs
    rows = query_ref.shape[0]
    me = owner_ref[0]
    for head in range(heads):
        stacked[pl.ds(head * rows, rows), :] = query_ref[:, head * head_dim : (head + 1) * head_dim]

    def column(ref):
        return jnp.broadcast_to(ref[pl.ds(me, 1), :], (rows, rows)).T

    query_pair, query_role = column(pair_ref), column(role_ref)
    query_pos = me * rows + lax.broadcasted_iota(jnp.int32, (rows, rows), 0)
    key_off = lax.broadcasted_iota(jnp.int32, (rows, rows), 1)

    def needed(owner):
        first_pair, last_pair = pair_smem[owner, 0], pair_smem[owner, rows - 1]
        first_role, last_role = role_smem[owner, 0], role_smem[owner, rows - 1]
        my_first, my_last = pair_smem[me, 0], pair_smem[me, rows - 1]
        my_role = role_smem[me, 0]
        apart = (
            (first_pair == last_pair)
            & (my_first == my_last)
            & (first_role == last_role)
            & (my_role == role_smem[me, rows - 1])
            & (first_role != 0)
            & (first_role != my_role)
        )
        return (owner <= me) & (last_pair >= my_first) & jnp.logical_not(apart)

    def bias_of(owner):
        key_role = role_ref[pl.ds(owner, 1), :]
        seen = (
            (query_pair == pair_ref[pl.ds(owner, 1), :])
            & (owner * rows + key_off <= query_pos)
            & ((key_role == 0) | (key_role == query_role))
        )
        return jnp.where(seen, 0.0, NEG_FILL)

    top[...] = jnp.full_like(top, NEG_FILL)
    total[...] = jnp.zeros_like(total)
    summed[...] = jnp.zeros_like(summed)
    for j, block in enumerate(blocks):
        owners = owner_ref[2 * j], owner_ref[2 * j + 1]

        @pl.when(needed(owners[0]) | needed(owners[1]))
        def _():
            bias = jnp.concatenate([bias_of(owner) for owner in owners], axis=1)
            raw = lax.dot_general(
                stacked[...],
                block[pl.ds(0, 2 * rows), :],
                (((1,), (1,)), ((), ())),
                preferred_element_type=jnp.float32,
            )
            masked = raw.reshape(heads, rows, 2 * rows) + bias[None]
            scores[j] = masked
            top[...] = jnp.maximum(
                top[...], jnp.maximum(masked[:, :, :rows], masked[:, :, rows:])
            )

    top[...] = jnp.broadcast_to(jnp.max(top[...], axis=-1, keepdims=True), top.shape)
    factor = math.log2(math.e) / math.sqrt(head_dim)
    for j, block in enumerate(blocks):
        owners = owner_ref[2 * j], owner_ref[2 * j + 1]

        @pl.when(needed(owners[0]) | needed(owners[1]))
        def _():
            weights = jnp.exp2((scores[j] - jnp.concatenate([top[...]] * 2, axis=2)) * factor)
            total[...] += weights[:, :, :rows] + weights[:, :, rows:]
            summed[...] += jnp.dot(
                weights.astype(jnp.bfloat16).reshape(heads * rows, 2 * rows),
                block[pl.ds(2 * rows, 2 * rows), :],
                preferred_element_type=jnp.float32,
            ).reshape(heads, rows, head_dim)

    mixed = (summed[...] / jnp.sum(total[...], axis=-1, keepdims=True)).astype(jnp.bfloat16)
    mixed = jnp.concatenate([mixed[head] for head in range(heads)], axis=1)
    projected = jnp.dot(mixed, weight_ref[...], preferred_element_type=jnp.float32)
    residual = (hidden_ref[...].astype(jnp.float32) + projected).astype(jnp.bfloat16)
    residual_ref[...] = residual
    wide = residual.astype(jnp.float32)
    mean_sq = jnp.mean(wide * wide, axis=-1, keepdims=True)
    normed = (wide * lax.rsqrt(mean_sq + 1e-06) * gain_ref[...]).astype(jnp.bfloat16)
    part = rows // CHUNKS
    for chunk in range(CHUNKS):
        chunk_refs[chunk][...] = normed[chunk * part : (chunk + 1) * part]


def attend(owners, pairs, parts, inputs, blocks):
    queries, _, _, hidden, _, _ = inputs
    rows, width = queries.shape
    head_dim = blocks[0].shape[1]
    heads = width // head_dim
    count = owners.shape[0]
    tall = heads * rows * rows * jnp.dtype(jnp.float32).itemsize
    smem = pl.BlockSpec(memory_space=pltpu.SMEM)
    vmem = pl.BlockSpec(memory_space=pltpu.VMEM)
    square = pltpu.VMEM((heads, rows, rows), jnp.float32)
    chunk = jax.ShapeDtypeStruct((rows // CHUNKS, hidden.shape[1]), jnp.bfloat16)
    *chunks, residual = pl.pallas_call(
        functools.partial(attention_kernel, len(blocks), heads, head_dim),
        out_shape=(chunk,) * CHUNKS + (jax.ShapeDtypeStruct(hidden.shape, jnp.bfloat16),),
        in_specs=[smem] * 3 + [vmem] * (len(inputs) + len(blocks)),
        out_specs=(vmem,) * (CHUNKS + 1),
        scratch_shapes=[
            pltpu.VMEM((heads * rows, head_dim), jnp.bfloat16),
            pltpu.VMEM((len(blocks), heads, rows, 2 * rows), jnp.float32),
            square,
            square,
            pltpu.VMEM((heads, rows, head_dim), jnp.float32),
        ],
        compiler_params=pltpu.CompilerParams(vmem_limit_bytes=(count + 3) * tall + 10 * MIB),
        name="attention",
    )(owners, pairs, parts, *(in_vmem(x) for x in inputs), in_vmem(blocks[0]), *blocks[1:])
    return residual, chunks


def load_kernel(count, *refs):
    inputs, outputs, sems = refs[:count], refs[count : 2 * count], refs[2 * count]
    moves = [pltpu.make_async_copy(inputs[k], outputs[k], sems.at[k]) for k in range(count)]
    for move in moves:
        move.start()
    for move in moves:
        move.wait()


def load(*arrays):
    count = len(arrays)
    return pl.pallas_call(
        functools.partial(load_kernel, count),
        out_shape=tuple(pltpu.VMEM(x.shape, x.dtype) for x in arrays),
        in_specs=[pl.BlockSpec(memory_space=pl.ANY)] * count,
        out_specs=(pl.BlockSpec(memory_space=pltpu.VMEM),) * count,
        scratch_shapes=[pltpu.SemaphoreType.DMA((count,))],
        compiler_params=pltpu.CompilerParams(vmem_limit_bytes=2 * MIB),
        name="load",
    )(*arrays)


def join_kernel(count, *refs):
    inputs, both_ref, sems = refs[: 2 * count], refs[2 * count], refs[2 * count + 1]
    rows = inputs[0].shape[0]
    moves = []
    for k in range(2 * count):
        owner, kind = divmod(k, count)
        place = pl.ds((kind * 2 + owner) * rows, rows)
        moves.append(pltpu.make_async_copy(inputs[k], both_ref.at[place, :], sems.at[k]))
    for move in moves:
        move.start()
    for move in moves:
        move.wait()


def join(own, mate):
    count = len(own)
    rows, width = own[0].shape
    return pl.pallas_call(
        functools.partial(join_kernel, count),
        out_shape=pltpu.VMEM((2 * count * rows, width), own[0].dtype),
        in_specs=[pl.BlockSpec(memory_space=pl.ANY)] * count
        + [pl.BlockSpec(memory_space=pltpu.VMEM)] * count,
        out_specs=pl.BlockSpec(memory_space=pltpu.VMEM),
        scratch_shapes=[pltpu.SemaphoreType.DMA((2 * count,))],
        name="join",
    )(*own, *mate)


def ffn_kernel(blocks, *refs):
    inputs, refs = refs[:blocks], refs[blocks:]
    weights, refs = refs[:6], refs[6:]
    outputs, refs = refs[:blocks], refs[blocks:]
    turned, inner = refs
    part = inputs[0].shape[0]
    turned[...] = jnp.concatenate([ref[...] for ref in inputs], axis=0).T
    for side in range(2):
        gate, up = weights[3 * side : 3 * side + 2]
        gate_out = jnp.dot(gate[...], turned[...], preferred_element_type=jnp.float32)
        up_out = jnp.dot(up[...], turned[...], preferred_element_type=jnp.float32)
        inner[side] = (gate_out / (1.0 + jnp.exp(-gate_out)) * up_out).astype(jnp.bfloat16)
    term = sum(
        jnp.dot(inner[side].T, weights[3 * side + 2][...], preferred_element_type=jnp.float32)
        for side in range(2)
    ).astype(jnp.bfloat16)
    for k in range(blocks):
        outputs[k][...] = term[k * part : (k + 1) * part]


def ffn(blocks, weights):
    count = len(blocks)
    rows, width = blocks[0].shape
    hidden = weights[0].shape[0]
    vmem = pl.BlockSpec(memory_space=pltpu.VMEM)
    return pl.pallas_call(
        functools.partial(ffn_kernel, count),
        out_shape=tuple(jax.ShapeDtypeStruct(b.shape, jnp.bfloat16) for b in blocks),
        in_specs=[vmem] * (count + 6),
        out_specs=(vmem,) * count,
        scratch_shapes=[
            pltpu.VMEM((width, count * rows), jnp.bfloat16),
            pltpu.VMEM((2, hidden, count * rows), jnp.bfloat16),
        ],
        compiler_params=pltpu.CompilerParams(vmem_limit_bytes=16 * MIB),
        cost_estimate=pl.CostEstimate(flops=1000, transcendentals=0, bytes_accessed=1000),
        name="feed_forward",
    )(*blocks, *(in_vmem(w) for w in weights))


def feed_forward(ring, chunks, own, mates):
    half = ring.half

    def send(pair, way):
        return ring.go(pair[0], way), ring.go(pair[1], -way)

    chunks, own, mates = lax.optimization_barrier((chunks, own, mates))
    held = [[(chunks[0], chunks[1])], [(chunks[1], chunks[0])]]
    terms = [{}, {}]
    for group in range(2):
        held[group].append(send(held[group][0], 1))
    weights = load(*(in_hbm(w) for w in own)) + load(*mates)
    weights, held[0][1] = hold(weights, held[0][1])
    for step in range(1, half):
        held[0].append(send(held[0][step], 1))
        older = held[1][step - 1] if step > 1 else held[0][0]
        done = ffn(held[0][step] + older, weights)
        if step + 1 < half:
            done, pair = hold(done, held[1][step])
            held[1].append(send(pair, 1))
        terms[0][step], terms[1][step - 1] = done[:2], done[2:]
    older = held[1][half - 1] if half > 1 else held[0][0]
    if half > 1:
        done, older = hold(done, older)
        terms[0][half - 1], terms[1][half - 2] = done[:2], done[2:]
    done = ffn(held[0][half] + older, weights)
    terms[0][half], terms[1][half - 1] = done[:2], done[2:]

    def add(a, b):
        return (a.astype(jnp.float32) + b.astype(jnp.float32)).astype(jnp.bfloat16)

    home = [None, None]
    for step in range(half, 0, -1):
        for group in range(2):
            place = step - group
            if place == 0:
                continue
            pair = terms[group][place]
            if home[group] is not None:
                pair = (add(home[group][0], pair[0]), add(home[group][1], pair[1]))
            home[group] = send(pair, -1)
    sums = [[x.astype(jnp.float32) for x in terms[1][0]]]
    if home[1] is not None:
        sums.append([x.astype(jnp.float32) for x in home[1][::-1]])
    sums.append([x.astype(jnp.float32) for x in home[0]])
    return [sum(x[k] for x in sums) for k in range(2)]


def kv_phases(half):
    if half < 4:
        return [[(hops, 0) for hops in range(1, half + 1)]]
    phases = [[(1, 0), (3, 0)], [(2, 1), (4, 3)]]
    for hops in range(5, half + 1, 2):
        phases.append([(k, k - 2) for k in (hops, hops + 1) if k <= half])
    return phases


def gather_kv(ring, keys, values, weights, inputs, extras):
    half = ring.half
    gate, up, down = weights
    both = join(
        (in_hbm(keys), in_hbm(values)), (in_vmem(ring.go_mate(keys)), in_vmem(ring.go_mate(values)))
    )
    gate, up, both = lax.optimization_barrier((gate, up, both))
    gate_mate, up_mate = ring.go_mate(gate), ring.go_mate(up)
    held, mates = {0: both}, {}
    for phase in kv_phases(half):
        for block in [b for b in held if 0 < b and b not in mates]:
            mates[block] = ring.go_mate(held[block])
        for hops, source in phase:
            if (hops, source) == (4, 3):
                held[2], held[3], inputs, extras = lax.optimization_barrier(
                    (held[2], held[3], inputs, extras)
                )
            held[hops] = ring.go_split(held[source], hops - source)
        if phase[0][1] == 0:
            held[1], inputs = hold(held[1], inputs)
            inputs = load(*(in_hbm(x) for x in inputs))
    for hops in range(1, half):
        if hops not in mates:
            mates[hops] = ring.go_mate(held[hops])
    gate_mate, up_mate, down, held, mates = lax.optimization_barrier(
        (gate_mate, up_mate, down, held, mates)
    )
    down_mate = ring.go_mate(down)
    blocks = tuple(held[hops] for hops in range(half + 1))
    blocks += tuple(mates[hops] for hops in range(1, half))
    return blocks, (gate_mate, up_mate, down_mate), inputs, extras


def block_owners(ring):
    half = ring.half
    owners = [ring.owners([(-hops, hops)]) for hops in range(half + 1)]
    owners += [ring.owners([(hops, -hops)], True) for hops in range(1, half)]
    return np.concatenate(owners, axis=1)


def on_device(
    ring,
    hidden_in,
    queries,
    keys,
    values,
    out_weight,
    norm_gain,
    gate_weight,
    up_weight,
    down_weight,
    pair_ids,
    roles,
    send_rows,
    send_counts,
):
    my_index = lax.axis_index("ctx")
    tok_rows = hidden_in.shape[0]
    own = (gate_weight.T, up_weight.T, down_weight)
    owners = jnp.asarray(block_owners(ring))[my_index]
    pairs = pair_ids.reshape(-1, tok_rows)
    parts = roles.reshape(-1, tok_rows)
    my_roles = lax.dynamic_slice_in_dim(roles, my_index * tok_rows, tok_rows)
    live = (my_roles != 0).astype(jnp.float32)
    inputs = (queries, pairs, parts, hidden_in, norm_gain.reshape(1, -1), out_weight)
    blocks, mates, inputs, extras = gather_kv(ring, keys, values, own, inputs, (owners, live))
    owners, live = extras
    residual, chunks = attend(owners, pairs, parts, inputs, blocks)
    summed = feed_forward(ring, chunks, own, mates)
    ffn_back = jnp.concatenate(summed, axis=0).astype(jnp.bfloat16).astype(jnp.float32)
    return (residual.astype(jnp.float32) + ffn_back * live[:, None]).astype(jnp.bfloat16)


def solution(mesh):
    ring = Ring(mesh.shape["groups"], mesh.shape["ctx"])

    def run(*arrays):
        return on_device(ring, *arrays)

    return jax.shard_map(
        run,
        mesh=mesh,
        in_specs=(
            P(("groups", "ctx"), None),
            P(("groups", "ctx"), None),
            P(("groups", "ctx"), None),
            P(("groups", "ctx"), None),
            P(),
            P(),
            P(None, "ctx"),
            P(None, "ctx"),
            P("ctx", None),
            P("groups"),
            P("groups"),
            P(("groups", "ctx"), None),
            P("groups", None),
        ),
        out_specs=P(("groups", "ctx"), None),
        check_vma=False,
    )
```

```python
import functools
import math

import jax
import jax.numpy as jnp
import numpy as np
from jax import lax
from jax.experimental import pallas as pl
from jax.experimental.pallas import tpu as pltpu
from jax.sharding import PartitionSpec as P

NEG_FILL = -1e30
CORES = 2
PLANE = 4
MIB = 1 << 20
CHUNKS = 2


def in_hbm(x):
    return pltpu.with_memory_space_constraint(x, pltpu.HBM)


def in_vmem(x):
    return pltpu.with_memory_space_constraint(x, pltpu.VMEM)


def hold(first, then):
    return lax.optimization_barrier((first, then))


class Ring:
    def __init__(self, groups, devices):
        chips = devices // CORES
        columns = max(1, PLANE // groups)
        if chips % columns:
            columns = 1
        depth = chips // columns
        order = []
        for column in range(columns):
            line = [level * columns + column for level in range(depth)]
            order += line if column % 2 == 0 else line[::-1]
        self.chips = chips
        self.half = chips // 2
        self.order = order
        self.swap = [(i, i ^ 1) for i in range(devices)]

    def go(self, block, hops):
        pairs = []
        for place in range(self.chips):
            here, there = self.order[place], self.order[(place + hops) % self.chips]
            pairs += [(here * CORES + core, there * CORES + core) for core in range(CORES)]
        return lax.ppermute(block, "ctx", pairs)

    def go_mate(self, block):
        return lax.ppermute(block, "ctx", self.swap)

    def go_split(self, block, hops):
        pairs = []
        for place in range(self.chips):
            for core, way in ((0, hops), (1, -hops)):
                here, there = self.order[place], self.order[(place + way) % self.chips]
                pairs.append((here * CORES + core, there * CORES + core))
        return lax.ppermute(block, "ctx", pairs)

    def owners(self, spots, swapped=False):
        place_of = {chip: place for place, chip in enumerate(self.order)}
        table = []
        for device in range(self.chips * CORES):
            chip, core = divmod(device, CORES)
            row = []
            for spot in spots:
                first = self.order[(place_of[chip] + spot[core]) % self.chips] * CORES + core
                row += [first ^ 1, first] if swapped else [first, first ^ 1]
            table.append(row)
        return np.asarray(table, np.int32)


def attention_kernel(
    pieces,
    heads,
    head_dim,
    owner_ref,
    pair_smem,
    role_smem,
    query_ref,
    pair_ref,
    role_ref,
    hidden_ref,
    gain_ref,
    weight_ref,
    *refs,
):
    blocks, refs = refs[:pieces], refs[pieces:]
    chunk_refs, refs = refs[:CHUNKS], refs[CHUNKS:]
    (residual_ref, stacked, scores, top, total, summed) = refs
    rows = query_ref.shape[0]
    me = owner_ref[0]
    for head in range(heads):
        stacked[pl.ds(head * rows, rows), :] = query_ref[:, head * head_dim : (head + 1) * head_dim]

    def column(ref):
        return jnp.broadcast_to(ref[pl.ds(me, 1), :], (rows, rows)).T

    query_pair, query_role = column(pair_ref), column(role_ref)
    query_pos = me * rows + lax.broadcasted_iota(jnp.int32, (rows, rows), 0)
    key_off = lax.broadcasted_iota(jnp.int32, (rows, rows), 1)

    def needed(owner):
        first_pair, last_pair = pair_smem[owner, 0], pair_smem[owner, rows - 1]
        first_role, last_role = role_smem[owner, 0], role_smem[owner, rows - 1]
        my_first, my_last = pair_smem[me, 0], pair_smem[me, rows - 1]
        my_role = role_smem[me, 0]
        apart = (
            (first_pair == last_pair)
            & (my_first == my_last)
            & (first_role == last_role)
            & (my_role == role_smem[me, rows - 1])
            & (first_role != 0)
            & (first_role != my_role)
        )
        return (owner <= me) & (last_pair >= my_first) & jnp.logical_not(apart)

    def bias_of(owner):
        key_role = role_ref[pl.ds(owner, 1), :]
        seen = (
            (query_pair == pair_ref[pl.ds(owner, 1), :])
            & (owner * rows + key_off <= query_pos)
            & ((key_role == 0) | (key_role == query_role))
        )
        return jnp.where(seen, 0.0, NEG_FILL)

    top[...] = jnp.full_like(top, NEG_FILL)
    total[...] = jnp.zeros_like(total)
    summed[...] = jnp.zeros_like(summed)
    for j, block in enumerate(blocks):
        owners = owner_ref[2 * j], owner_ref[2 * j + 1]

        @pl.when(needed(owners[0]) | needed(owners[1]))
        def _():
            bias = jnp.concatenate([bias_of(owner) for owner in owners], axis=1)
            raw = lax.dot_general(
                stacked[...],
                block[pl.ds(0, 2 * rows), :],
                (((1,), (1,)), ((), ())),
                preferred_element_type=jnp.float32,
            )
            masked = raw.reshape(heads, rows, 2 * rows) + bias[None]
            scores[j] = masked
            top[...] = jnp.maximum(
                top[...], jnp.maximum(masked[:, :, :rows], masked[:, :, rows:])
            )

    top[...] = jnp.broadcast_to(jnp.max(top[...], axis=-1, keepdims=True), top.shape)
    factor = math.log2(math.e) / math.sqrt(head_dim)
    for j, block in enumerate(blocks):
        owners = owner_ref[2 * j], owner_ref[2 * j + 1]

        @pl.when(needed(owners[0]) | needed(owners[1]))
        def _():
            weights = jnp.exp2((scores[j] - jnp.concatenate([top[...]] * 2, axis=2)) * factor)
            total[...] += weights[:, :, :rows] + weights[:, :, rows:]
            summed[...] += jnp.dot(
                weights.astype(jnp.bfloat16).reshape(heads * rows, 2 * rows),
                block[pl.ds(2 * rows, 2 * rows), :],
                preferred_element_type=jnp.float32,
            ).reshape(heads, rows, head_dim)

    mixed = (summed[...] / jnp.sum(total[...], axis=-1, keepdims=True)).astype(jnp.bfloat16)
    mixed = jnp.concatenate([mixed[head] for head in range(heads)], axis=1)
    projected = jnp.dot(mixed, weight_ref[...], preferred_element_type=jnp.float32)
    residual = (hidden_ref[...].astype(jnp.float32) + projected).astype(jnp.bfloat16)
    residual_ref[...] = residual
    wide = residual.astype(jnp.float32)
    mean_sq = jnp.mean(wide * wide, axis=-1, keepdims=True)
    normed = (wide * lax.rsqrt(mean_sq + 1e-06) * gain_ref[...]).astype(jnp.bfloat16)
    part = rows // CHUNKS
    for chunk in range(CHUNKS):
        chunk_refs[chunk][...] = normed[chunk * part : (chunk + 1) * part]


def attend(owners, pairs, parts, inputs, blocks):
    queries, _, _, hidden, _, _ = inputs
    rows, width = queries.shape
    head_dim = blocks[0].shape[1]
    heads = width // head_dim
    count = owners.shape[0]
    tall = heads * rows * rows * jnp.dtype(jnp.float32).itemsize
    smem = pl.BlockSpec(memory_space=pltpu.SMEM)
    vmem = pl.BlockSpec(memory_space=pltpu.VMEM)
    square = pltpu.VMEM((heads, rows, rows), jnp.float32)
    chunk = jax.ShapeDtypeStruct((rows // CHUNKS, hidden.shape[1]), jnp.bfloat16)
    *chunks, residual = pl.pallas_call(
        functools.partial(attention_kernel, len(blocks), heads, head_dim),
        out_shape=(chunk,) * CHUNKS + (jax.ShapeDtypeStruct(hidden.shape, jnp.bfloat16),),
        in_specs=[smem] * 3 + [vmem] * (len(inputs) + len(blocks)),
        out_specs=(vmem,) * (CHUNKS + 1),
        scratch_shapes=[
            pltpu.VMEM((heads * rows, head_dim), jnp.bfloat16),
            pltpu.VMEM((len(blocks), heads, rows, 2 * rows), jnp.float32),
            square,
            square,
            pltpu.VMEM((heads, rows, head_dim), jnp.float32),
        ],
        compiler_params=pltpu.CompilerParams(vmem_limit_bytes=(count + 3) * tall + 10 * MIB),
        name="attention",
    )(owners, pairs, parts, *(in_vmem(x) for x in inputs), in_vmem(blocks[0]), *blocks[1:])
    return residual, chunks


def load_kernel(count, *refs):
    inputs, outputs, sems = refs[:count], refs[count : 2 * count], refs[2 * count]
    moves = [pltpu.make_async_copy(inputs[k], outputs[k], sems.at[k]) for k in range(count)]
    for move in moves:
        move.start()
    for move in moves:
        move.wait()


def load(*arrays):
    count = len(arrays)
    return pl.pallas_call(
        functools.partial(load_kernel, count),
        out_shape=tuple(pltpu.VMEM(x.shape, x.dtype) for x in arrays),
        in_specs=[pl.BlockSpec(memory_space=pl.ANY)] * count,
        out_specs=(pl.BlockSpec(memory_space=pltpu.VMEM),) * count,
        scratch_shapes=[pltpu.SemaphoreType.DMA((count,))],
        compiler_params=pltpu.CompilerParams(vmem_limit_bytes=2 * MIB),
        name="load",
    )(*arrays)


def join_kernel(count, *refs):
    inputs, both_ref, sems = refs[: 2 * count], refs[2 * count], refs[2 * count + 1]
    rows = inputs[0].shape[0]
    moves = []
    for k in range(2 * count):
        owner, kind = divmod(k, count)
        place = pl.ds((kind * 2 + owner) * rows, rows)
        moves.append(pltpu.make_async_copy(inputs[k], both_ref.at[place, :], sems.at[k]))
    for move in moves:
        move.start()
    for move in moves:
        move.wait()


def join(own, mate):
    count = len(own)
    rows, width = own[0].shape
    return pl.pallas_call(
        functools.partial(join_kernel, count),
        out_shape=pltpu.VMEM((2 * count * rows, width), own[0].dtype),
        in_specs=[pl.BlockSpec(memory_space=pl.ANY)] * count
        + [pl.BlockSpec(memory_space=pltpu.VMEM)] * count,
        out_specs=pl.BlockSpec(memory_space=pltpu.VMEM),
        scratch_shapes=[pltpu.SemaphoreType.DMA((2 * count,))],
        name="join",
    )(*own, *mate)


def ffn_kernel(blocks, *refs):
    inputs, refs = refs[:blocks], refs[blocks:]
    weights, refs = refs[:6], refs[6:]
    outputs, refs = refs[:blocks], refs[blocks:]
    turned, inner = refs
    part = inputs[0].shape[0]
    turned[...] = jnp.concatenate([ref[...] for ref in inputs], axis=0).T
    for side in range(2):
        gate, up = weights[3 * side : 3 * side + 2]
        gate_out = jnp.dot(gate[...], turned[...], preferred_element_type=jnp.float32)
        up_out = jnp.dot(up[...], turned[...], preferred_element_type=jnp.float32)
        inner[side] = (gate_out / (1.0 + jnp.exp(-gate_out)) * up_out).astype(jnp.bfloat16)
    term = sum(
        jnp.dot(inner[side].T, weights[3 * side + 2][...], preferred_element_type=jnp.float32)
        for side in range(2)
    ).astype(jnp.bfloat16)
    for k in range(blocks):
        outputs[k][...] = term[k * part : (k + 1) * part]


def ffn(blocks, weights):
    count = len(blocks)
    rows, width = blocks[0].shape
    hidden = weights[0].shape[0]
    vmem = pl.BlockSpec(memory_space=pltpu.VMEM)
    return pl.pallas_call(
        functools.partial(ffn_kernel, count),
        out_shape=tuple(jax.ShapeDtypeStruct(b.shape, jnp.bfloat16) for b in blocks),
        in_specs=[vmem] * (count + 6),
        out_specs=(vmem,) * count,
        scratch_shapes=[
            pltpu.VMEM((width, count * rows), jnp.bfloat16),
            pltpu.VMEM((2, hidden, count * rows), jnp.bfloat16),
        ],
        compiler_params=pltpu.CompilerParams(vmem_limit_bytes=16 * MIB),
        cost_estimate=pl.CostEstimate(flops=1000, transcendentals=0, bytes_accessed=1000),
        name="feed_forward",
    )(*blocks, *(in_vmem(w) for w in weights))


def feed_forward(ring, chunks, own, mates):
    half = ring.half

    def send(pair, way):
        return ring.go(pair[0], way), ring.go(pair[1], -way)

    chunks, own, mates = lax.optimization_barrier((chunks, own, mates))
    held = [[(chunks[0], chunks[1])], [(chunks[1], chunks[0])]]
    terms = [{}, {}]
    for group in range(2):
        held[group].append(send(held[group][0], 1))
    weights = load(*(in_hbm(w) for w in own)) + load(*mates)
    weights, held[0][1] = hold(weights, held[0][1])
    for step in range(1, half):
        held[0].append(send(held[0][step], 1))
        older = held[1][step - 1] if step > 1 else held[0][0]
        done = ffn(held[0][step] + older, weights)
        if step + 1 < half:
            done, pair = hold(done, held[1][step])
            held[1].append(send(pair, 1))
        terms[0][step], terms[1][step - 1] = done[:2], done[2:]
    older = held[1][half - 1] if half > 1 else held[0][0]
    if half > 1:
        done, older = hold(done, older)
        terms[0][half - 1], terms[1][half - 2] = done[:2], done[2:]
    done = ffn(held[0][half] + older, weights)
    terms[0][half], terms[1][half - 1] = done[:2], done[2:]

    def add(a, b):
        return (a.astype(jnp.float32) + b.astype(jnp.float32)).astype(jnp.bfloat16)

    home = [None, None]
    for step in range(half, 0, -1):
        for group in range(2):
            place = step - group
            if place == 0:
                continue
            pair = terms[group][place]
            if home[group] is not None:
                pair = (add(home[group][0], pair[0]), add(home[group][1], pair[1]))
            home[group] = send(pair, -1)
    sums = [[x.astype(jnp.float32) for x in terms[1][0]]]
    if home[1] is not None:
        sums.append([x.astype(jnp.float32) for x in home[1][::-1]])
    sums.append([x.astype(jnp.float32) for x in home[0]])
    return [sum(x[k] for x in sums) for k in range(2)]


def kv_phases(half):
    if half < 4:
        return [[(hops, 0) for hops in range(1, half + 1)]]
    phases = [[(1, 0), (3, 0)], [(2, 1), (4, 3)]]
    for hops in range(5, half + 1, 2):
        phases.append([(k, k - 2) for k in (hops, hops + 1) if k <= half])
    return phases


def gather_kv(ring, keys, values, weights, inputs, extras):
    half = ring.half
    gate, up, down = weights
    both = join(
        (in_hbm(keys), in_hbm(values)), (in_vmem(ring.go_mate(keys)), in_vmem(ring.go_mate(values)))
    )
    gate, up, both = lax.optimization_barrier((gate, up, both))
    gate_mate, up_mate = ring.go_mate(gate), ring.go_mate(up)
    held, mates = {0: both}, {}
    for phase in kv_phases(half):
        for block in [b for b in held if 0 < b and b not in mates]:
            mates[block] = ring.go_mate(held[block])
        for hops, source in phase:
            if (hops, source) == (4, 3):
                held[2], held[3], inputs, extras = lax.optimization_barrier(
                    (held[2], held[3], inputs, extras)
                )
            held[hops] = ring.go_split(held[source], hops - source)
        if phase[0][1] == 0:
            held[1], inputs = hold(held[1], inputs)
            inputs = load(*(in_hbm(x) for x in inputs))
    gate_mate, up_mate, down, mates = lax.optimization_barrier((gate_mate, up_mate, down, mates))
    down_mate = ring.go_mate(down)
    for hops in range(1, half):
        if hops not in mates:
            mates[hops] = ring.go_mate(held[hops])
    blocks = tuple(held[hops] for hops in range(half + 1))
    blocks += tuple(mates[hops] for hops in range(1, half))
    return blocks, (gate_mate, up_mate, down_mate), inputs, extras


def block_owners(ring):
    half = ring.half
    owners = [ring.owners([(-hops, hops)]) for hops in range(half + 1)]
    owners += [ring.owners([(hops, -hops)], True) for hops in range(1, half)]
    return np.concatenate(owners, axis=1)


def on_device(
    ring,
    hidden_in,
    queries,
    keys,
    values,
    out_weight,
    norm_gain,
    gate_weight,
    up_weight,
    down_weight,
    pair_ids,
    roles,
    send_rows,
    send_counts,
):
    my_index = lax.axis_index("ctx")
    tok_rows = hidden_in.shape[0]
    own = (gate_weight.T, up_weight.T, down_weight)
    owners = jnp.asarray(block_owners(ring))[my_index]
    pairs = pair_ids.reshape(-1, tok_rows)
    parts = roles.reshape(-1, tok_rows)
    my_roles = lax.dynamic_slice_in_dim(roles, my_index * tok_rows, tok_rows)
    live = (my_roles != 0).astype(jnp.float32)
    inputs = (queries, pairs, parts, hidden_in, norm_gain.reshape(1, -1), out_weight)
    blocks, mates, inputs, extras = gather_kv(ring, keys, values, own, inputs, (owners, live))
    owners, live = extras
    residual, chunks = attend(owners, pairs, parts, inputs, blocks)
    summed = feed_forward(ring, chunks, own, mates)
    ffn_back = jnp.concatenate(summed, axis=0).astype(jnp.bfloat16).astype(jnp.float32)
    return (residual.astype(jnp.float32) + ffn_back * live[:, None]).astype(jnp.bfloat16)


def solution(mesh):
    ring = Ring(mesh.shape["groups"], mesh.shape["ctx"])

    def run(*arrays):
        return on_device(ring, *arrays)

    return jax.shard_map(
        run,
        mesh=mesh,
        in_specs=(
            P(("groups", "ctx"), None),
            P(("groups", "ctx"), None),
            P(("groups", "ctx"), None),
            P(("groups", "ctx"), None),
            P(),
            P(),
            P(None, "ctx"),
            P(None, "ctx"),
            P("ctx", None),
            P("groups"),
            P("groups"),
            P(("groups", "ctx"), None),
            P("groups", None),
        ),
        out_specs=P(("groups", "ctx"), None),
        check_vma=False,
    )
```
